128 devices in a mesh: ctx: 16 (over z_hi, y, core), tp: 8 (over x, z_lo).
Axes of the slice: x: 4, y: 4, z: 4 (z_hi: 2, z_lo: 2; z = z_hi * 2 + z_lo), core: 2. Of those that a mesh axis runs over, the one named last changes fastest.
Arguments:
- query: bfloat16 [4096, 8192], P('ctx', 'tp'), may hold values from -6 to 6
- key_part: bfloat16 [4096, 8192], P('ctx', 'tp'), may hold values from -6 to 6
- value_part: bfloat16 [4096, 8192], P('ctx', 'tp'), may hold values from -6 to 6
- out_cotangent: bfloat16 [4096, 4096], P('ctx', 'tp'), may hold values from -3 to 3
- w_out: bfloat16 [8192, 4096], P('tp'), may hold values from -0.0625 to 0.0625
- residue: float32 [8192, 16], P(('tp', 'ctx')), may hold values from -1.5 to 1.5
- rate: float32 [8192, 16], P(('tp', 'ctx')), may hold values from 0.5 to 200
- skip: float32 [8192], P(('tp', 'ctx')), may hold values from 0.5 to 1.5
Outputs:
- output: bfloat16 [4096, 4096], P('ctx', 'tp')
- d_query: bfloat16 [4096, 8192], P('ctx', 'tp')
- d_key: bfloat16 [4096, 8192], P('ctx', 'tp')
- d_value: bfloat16 [4096, 8192], P('ctx', 'tp')
- d_weight: float32 [8192, 4096], P('tp', 'ctx')
- d_residue: float32 [8192, 16], P(('tp', 'ctx'))
- d_rate: float32 [8192, 16], P(('tp', 'ctx'))
- d_skip: float32 [8192], P(('tp', 'ctx'))
The draws below stay inside these ranges and needn't reach their ends.
All inputs are finite; a program needn't handle non-finite values.
Results may differ from the reference program's by a relative error of at most 0.02.
Values may be sent and summed in bfloat16 or wider, within the bound.
No kernel may reach another device: no remote copies, remote signals or barrier semaphores. Data moves between devices by JAX's collectives and lax.ppermute only.
A program may use at most 128 MiB of HBM per device.

```python
import math
import jax
import jax.numpy as jnp
from jax import lax

D = 8192
DOUT = 4096
MODES = 16
SEQ = 4096


def block_scale(own_key, extent, cuts, low, high):
    def one(dim, shards_of):
        draws = jax.random.uniform(jax.random.fold_in(jax.random.fold_in(own_key, 6), dim), (shards_of,), jnp.float32, low / len(cuts), high / len(cuts))
        return jnp.repeat(jnp.exp(draws), extent[dim] // shards_of).reshape((-1,) + (1,) * (len(extent) - dim - 1))

    factor_of = one(*cuts[0])
    for cut in cuts[1:]:
        factor_of = factor_of * one(*cut)
    return factor_of


def scatter_about(rng, extent, spread, limit, split=(), held_as=jnp.bfloat16):
    array = spread * jax.random.normal(rng, extent, jnp.float32)
    if split:
        array = array * block_scale(rng, extent, split, -0.22, 0.18)
    return jnp.clip(array, -limit, limit).astype(held_as)


def setup_inputs(seed: int = 0) -> dict:
    seeds = jax.random.split(jax.random.key(seed), 9)
    query = scatter_about(seeds[0], (SEQ, D), 1.0, 6.0, ((0, 16), (1, 8)))
    key_part = scatter_about(seeds[1], (SEQ, D), 1.0, 6.0, ((0, 16), (1, 8)))
    value_part = scatter_about(seeds[2], (SEQ, D), 1.0, 6.0, ((0, 16), (1, 8)))
    out_cotangent = scatter_about(seeds[3], (SEQ, DOUT), 0.5, 3.0, ((0, 16), (1, 8)))
    w_out = scatter_about(seeds[4], (D, DOUT), D ** -0.5, 0.0625, ((0, 8),))
    residue = scatter_about(seeds[5], (D, MODES), 0.25, 1.5, ((0, 128),), jnp.float32)
    rate = jnp.clip(jnp.exp(math.log(200.0) - 5.9914645 * jax.random.uniform(seeds[6], (D, MODES), jnp.float32) ** block_scale(seeds[6], (D, MODES), ((0, 128),), -0.2, 0.2)), 0.5, 200.0)
    skip = jnp.clip(0.5 + 1.0 * jax.random.uniform(seeds[7], (D,), jnp.float32) ** block_scale(seeds[7], (D,), ((0, 128),), -0.2, 0.2), 0.5, 1.5)
    return {"query": query, "key_part": key_part, "value_part": value_part, "out_cotangent": out_cotangent, "w_out": w_out, "residue": residue, "rate": rate, "skip": skip}


def filter_basis(rate_block, seq_len):
    steps = jnp.arange(seq_len).astype(rate_block.dtype)
    decay = rate_block / seq_len
    basis = jnp.sqrt(2.0 * decay)[:, :, None] * jnp.exp(-decay[:, :, None] * steps[None, None, :])
    return (basis, steps)

def reference(query, key_part, value_part, out_cotangent, w_out, residue, rate, skip):
    width = 64
    groups = D // width
    mixed = (key_part.astype(jnp.float32) * value_part.astype(jnp.float32)).astype(jnp.bfloat16)
    signal_blocks = mixed.T.reshape(groups, width, SEQ)
    res_blocks = residue.reshape(groups, width, MODES)
    rate_blocks = rate.reshape(groups, width, MODES)
    skip_blocks = skip.reshape(groups, width)
    length = 2 * SEQ

    def forward_block(pack):
        signal, res_one, rate_one, skip_one = pack
        basis, steps = filter_basis(rate_one, SEQ)
        filt = jnp.einsum('cm,cmt->ct', res_one, basis, precision=lax.Precision.HIGHEST)
        source = signal.astype(jnp.float32)
        spectrum = jnp.fft.rfft(source, n=length) * jnp.fft.rfft(filt, n=length)
        conv = jnp.fft.irfft(spectrum, n=length)[:, :SEQ]
        return (conv + skip_one[:, None] * source).astype(jnp.bfloat16)
    conv_out = lax.map(forward_block, (signal_blocks, res_blocks, rate_blocks, skip_blocks)).reshape(D, SEQ).T
    gated = (query.astype(jnp.float32) * conv_out.astype(jnp.float32)).astype(jnp.bfloat16)
    output = jnp.dot(gated, w_out, preferred_element_type=jnp.float32).astype(jnp.bfloat16)
    grad_gated = lax.dot_general(out_cotangent, w_out, (((1,), (1,)), ((), ())), preferred_element_type=jnp.float32)
    d_query = (grad_gated * conv_out.astype(jnp.float32)).astype(jnp.bfloat16)
    d_conv = (grad_gated * query.astype(jnp.float32)).astype(jnp.bfloat16)
    d_weight = lax.dot_general(gated, out_cotangent, (((0,), (0,)), ((), ())), preferred_element_type=jnp.float32)
    cot_blocks = d_conv.T.reshape(groups, width, SEQ)

    def backward_block(pack):
        signal, cot_block, res_one, rate_one, skip_one = pack
        basis, steps = filter_basis(rate_one, SEQ)
        filt = jnp.einsum('cm,cmt->ct', res_one, basis, precision=lax.Precision.HIGHEST)
        source = signal.astype(jnp.float32)
        cotan = cot_block.astype(jnp.float32)
        spec_src = jnp.fft.rfft(source, n=length)
        spec_filt = jnp.fft.rfft(filt, n=length)
        spec_cot = jnp.fft.rfft(cotan, n=length)
        corr = jnp.fft.irfft(spec_cot * jnp.conj(spec_filt), n=length)[:, :SEQ]
        grad_in = (corr + skip_one[:, None] * cotan).astype(jnp.bfloat16)
        filt_grad = jnp.fft.irfft(spec_cot * jnp.conj(spec_src), n=length)[:, :SEQ]
        skip_grad = lax.optimization_barrier(jnp.sum(cotan * source, axis=1))
        proj = jnp.einsum('ct,cmt->cm', filt_grad, basis, precision=lax.Precision.HIGHEST)
        slope = jnp.einsum('ct,cmt->cm', filt_grad * steps[None, :], basis, precision=lax.Precision.HIGHEST)
        rate_grad = res_one * (0.5 * proj / rate_one - slope / SEQ)
        return (grad_in, proj, rate_grad, skip_grad)
    grad_in, d_residue, d_rate, d_skip = lax.map(backward_block, (signal_blocks, cot_blocks, res_blocks, rate_blocks, skip_blocks))
    grad_in = grad_in.reshape(D, SEQ).T.astype(jnp.float32)
    d_key = (grad_in * value_part.astype(jnp.float32)).astype(jnp.bfloat16)
    d_value = (grad_in * key_part.astype(jnp.float32)).astype(jnp.bfloat16)
    return (output, d_query, d_key, d_value, d_weight, d_residue.reshape(D, MODES), d_rate.reshape(D, MODES), d_skip.reshape(D))
```

```python
import functools

import jax
import jax.numpy as jnp
from jax import lax
from jax.experimental import pallas as pl
from jax.experimental.pallas import tpu as pltpu
from jax.sharding import PartitionSpec as P

F32 = jnp.float32
BF16 = jnp.bfloat16
SEQ = 4096
MODES = 16
ROWS = 256
SUB = 8
BLOCKS = 16
UNROLL = 8
VMEM = 48 * 1024 * 1024


def params_of(flops, nbytes):
    return dict(
        compiler_params=pltpu.CompilerParams(vmem_limit_bytes=VMEM),
        cost_estimate=pl.CostEstimate(flops=flops, bytes_accessed=nbytes, transcendentals=0),
    )


def whole():
    return pl.BlockSpec(memory_space=pltpu.VMEM)


def lanes(group):
    return slice(128 * group, 128 * (group + 1))


def group_rows(group):
    return pl.ds(group, ROWS, stride=SUB)


def step_decay(table, mode):
    return jnp.exp(table[mode] * (-1.0 / SEQ))


def block_decay(table, mode):
    return jnp.exp(table[mode] * (-float(ROWS) / SEQ))


def mode_weight(table, mode):
    return table[MODES + mode] * jnp.sqrt(table[mode] * (2.0 / SEQ))


def at(ref, step):
    return ref[pl.ds(pl.multiple_of(step * SUB, SUB), SUB), :]


def zeros(count):
    return tuple(jnp.zeros((SUB, 128), F32) for _ in range(count))


def tree_sum(parts):
    parts = list(parts)
    while len(parts) > 1:
        parts = [sum(parts[i : i + 2]) for i in range(0, len(parts), 2)]
    return parts[0]


def states_kernel(key_ref, value_ref, table, mixed_ref, state_ref):
    for group in range(SUB):
        product = key_ref[:, lanes(group)].astype(F32) * value_ref[:, lanes(group)].astype(F32)
        mixed_ref[group_rows(group), :] = product.astype(BF16).astype(F32)
    decay = [step_decay(table, m) for m in range(MODES)]

    def body(i, held):
        for u in range(UNROLL):
            value = at(mixed_ref, i * UNROLL + u)
            held = tuple(decay[m] * held[m] + value for m in range(MODES))
        return held

    held = lax.fori_loop(0, ROWS // UNROLL, body, zeros(MODES))
    for m in range(MODES):
        state_ref[m] = held[m].astype(state_ref.dtype)


def forward_kernel(own_ref, sent_ref, mixed_ref, query_ref, table, conv_ref, gated_ref, carry_ref, buffer):
    own = own_ref[0]
    for m in range(MODES):
        far = block_decay(table, m)
        carry = jnp.zeros((SUB, 128), F32)
        for j in range(BLOCKS - 1):
            carry = jnp.where(j < own, far * carry + sent_ref[j, m].astype(F32), carry)
        carry_ref[m] = carry
    decay = [step_decay(table, m) for m in range(MODES)]
    weight = [mode_weight(table, m) for m in range(MODES)]
    skip = table[2 * MODES]

    def body(i, held):
        for u in range(UNROLL):
            step = i * UNROLL + u
            value = at(mixed_ref, step)
            held = tuple(decay[m] * held[m] + value for m in range(MODES))
            total = tree_sum([weight[m] * held[m] for m in range(MODES)])
            buffer[pl.ds(pl.multiple_of(step * SUB, SUB), SUB), :] = total + skip * value
        return held

    lax.fori_loop(0, ROWS // UNROLL, body, tuple(carry_ref[m] for m in range(MODES)))
    for group in range(SUB):
        conv = buffer[group_rows(group), :].astype(BF16)
        conv_ref[:, lanes(group)] = conv
        gated_ref[:, lanes(group)] = (query_ref[:, lanes(group)].astype(F32) * conv.astype(F32)).astype(BF16)


def output_kernel(gated_ref, weight_ref, out_ref):
    out_ref[0] = jnp.dot(gated_ref[...], weight_ref[...], preferred_element_type=F32).astype(BF16)


def weight_kernel(core_ref, gated_ref, other_ref, cot_ref, other_cot_ref, out_ref, turned):
    @pl.when(pl.program_id(0) == 0)
    def _():
        turned[:, :ROWS] = gated_ref[...].T
        turned[:, ROWS:] = other_ref[...].T

    total = jnp.dot(turned[:, :ROWS], cot_ref[0], preferred_element_type=F32)
    total += jnp.dot(turned[:, ROWS:], other_cot_ref[0], preferred_element_type=F32)
    out_ref[0] = total.astype(BF16)


def cotangent_kernel(cot_ref, weight_ref, query_ref, conv_ref, table, dquery_ref, dconv_ref, state_ref, sent_ref, total):
    part = pl.program_id(0)
    product = lax.dot_general(cot_ref[0], weight_ref[...], (((1,), (1,)), ((), ())), preferred_element_type=F32)

    @pl.when(part == 0)
    def _():
        total[...] = product

    @pl.when(part > 0)
    def _():
        total[...] += product

    @pl.when(part == pl.num_programs(0) - 1)
    def _():
        for group in range(SUB):
            cot = total[:, lanes(group)]
            dquery_ref[:, lanes(group)] = (cot * conv_ref[:, lanes(group)].astype(F32)).astype(BF16)
            dconv_ref[group_rows(group), :] = (cot * query_ref[:, lanes(group)].astype(F32)).astype(BF16).astype(F32)
        decay = [step_decay(table, m) for m in range(MODES)]

        def body(i, held):
            for u in range(UNROLL):
                value = at(dconv_ref, ROWS - 1 - (i * UNROLL + u))
                held = tuple(decay[m] * held[m] + value for m in range(MODES))
            return held

        held = lax.fori_loop(0, ROWS // UNROLL, body, zeros(MODES))
        for m in range(MODES):
            state_ref[m] = held[m]
            sent_ref[m] = held[m].astype(sent_ref.dtype)


def filter_kernel(mixed_ref, dconv_ref, carry_ref, back_ref, table, out_ref):
    half = MODES // 2
    for first in (0, half):
        modes = range(first, first + half)
        decay = [step_decay(table, m) for m in modes]

        def body(i, packed):
            held, moment, first_sum, second_sum, skip_sum = packed
            for u in range(UNROLL):
                value = at(mixed_ref, i * UNROLL + u)
                cot = at(dconv_ref, i * UNROLL + u)
                past = [decay[m] * held[m] for m in range(half)]
                moment = tuple(decay[m] * moment[m] + past[m] for m in range(half))
                held = tuple(past[m] + value for m in range(half))
                first_sum = tuple(first_sum[m] + cot * held[m] for m in range(half))
                second_sum = tuple(second_sum[m] + cot * moment[m] for m in range(half))
                skip_sum = skip_sum + cot * value
            return (held, moment, first_sum, second_sum, skip_sum)

        start = (tuple(carry_ref[m] for m in modes), zeros(half), zeros(half), zeros(half), zeros(1)[0])
        held, moment, first_sum, second_sum, skip_sum = lax.fori_loop(0, ROWS // UNROLL, body, start)
        for m in range(half):
            out_ref[first + m] = first_sum[m]
            out_ref[MODES + first + m] = second_sum[m]
            out_ref[2 * MODES + first + m] = moment[m]
            out_ref[3 * MODES + first + m] = back_ref[first + m]
        out_ref[4 * MODES] = skip_sum


def backward_kernel(own_ref, sent_ref, dconv_ref, key_ref, value_ref, table, dkey_ref, dvalue_ref, carry_ref, buffer):
    own = own_ref[0]
    for m in range(MODES):
        far = block_decay(table, m)
        carry = jnp.zeros((SUB, 128), F32)
        for j in range(BLOCKS - 1, 0, -1):
            carry = jnp.where(j > own, far * carry + sent_ref[j, m].astype(F32), carry)
        carry_ref[m] = carry
    decay = [step_decay(table, m) for m in range(MODES)]
    weight = [mode_weight(table, m) for m in range(MODES)]
    skip = table[2 * MODES]

    def body(i, held):
        for u in range(UNROLL):
            step = ROWS - 1 - (i * UNROLL + u)
            value = at(dconv_ref, step)
            held = tuple(decay[m] * held[m] + value for m in range(MODES))
            total = tree_sum([weight[m] * held[m] for m in range(MODES)])
            buffer[pl.ds(pl.multiple_of(step * SUB, SUB), SUB), :] = total + skip * value
        return held

    lax.fori_loop(0, ROWS // UNROLL, body, tuple(carry_ref[m] for m in range(MODES)))
    for group in range(SUB):
        grad = buffer[group_rows(group), :].astype(BF16).astype(F32)
        dkey_ref[:, lanes(group)] = (grad * value_ref[:, lanes(group)].astype(F32)).astype(BF16)
        dvalue_ref[:, lanes(group)] = (grad * key_ref[:, lanes(group)].astype(F32)).astype(BF16)


def owner_kernel(parts_ref, rate_ref, residue_ref, dresidue_ref, drate_ref, dskip_ref):
    rate = rate_ref[...]
    residue = residue_ref[...]
    near = jnp.exp(rate * (-1.0 / SEQ))
    far = jnp.exp(rate * (-float(ROWS) / SEQ))
    scale = jnp.sqrt(rate * (2.0 / SEQ))
    first = jnp.zeros_like(rate)
    second = jnp.zeros_like(rate)
    skip = jnp.zeros((1, rate.shape[1]), F32)
    later = jnp.zeros_like(rate)
    for j in range(BLOCKS - 1, -1, -1):
        first += parts_ref[j, 0:MODES]
        second += parts_ref[j, MODES : 2 * MODES] + near * later * parts_ref[j, 2 * MODES : 3 * MODES]
        later = far * later + parts_ref[j, 3 * MODES : 4 * MODES]
        skip += parts_ref[j, 4 * MODES : 4 * MODES + 1]
    proj = scale * first
    dresidue_ref[...] = proj
    drate_ref[...] = residue * (0.5 * proj / rate - scale * second * (1.0 / SEQ))
    dskip_ref[...] = skip


def f32(*shape):
    return jax.ShapeDtypeStruct(shape, F32)


def bf16(*shape):
    return jax.ShapeDtypeStruct(shape, BF16)


def exchange(array, axis, groups=None):
    return lax.all_to_all(array, axis, split_axis=0, concat_axis=0, tiled=True, axis_index_groups=groups)


def to_all(array, axis, count):
    return exchange(jnp.broadcast_to(array[None], (count,) + array.shape), axis)


def local(query, key_part, value_part, out_cotangent, w_out, residue, rate, skip):
    own = lax.axis_index("ctx")
    own_array = own.reshape(1).astype(jnp.int32)
    core = own % 2
    smem = pl.BlockSpec(memory_space=pltpu.SMEM)
    same_core = [[2 * chip + c for chip in range(8)] for c in range(2)]
    swap = [(i, i ^ 1) for i in range(BLOCKS)]

    rate_t, residue_t = rate.T, residue.T
    mine = jnp.concatenate([rate_t, residue_t, skip[None], jnp.zeros((7, skip.shape[0]), F32)], axis=0)
    table = to_all(mine, "ctx", BLOCKS).reshape(SUB, 2, 40, 64).transpose(2, 0, 1, 3).reshape(40, SUB, 128)
    cots = to_all(out_cotangent, "tp", 8)

    mixed, state = pl.pallas_call(
        states_kernel,
        out_shape=(f32(ROWS * SUB, 128), bf16(MODES, SUB, 128)),
        in_specs=[whole()] * 3,
        out_specs=(whole(), whole()),
        name="forward_states",
        **params_of(3_000_000_000, 4_000_000),
    )(key_part, value_part, table)
    sent = to_all(state, "ctx", BLOCKS)

    conv_out, gated, carry = pl.pallas_call(
        forward_kernel,
        out_shape=(bf16(ROWS, 1024), bf16(ROWS, 1024), f32(MODES, SUB, 128)),
        in_specs=[smem] + [whole()] * 4,
        out_specs=(whole(),) * 3,
        scratch_shapes=[pltpu.VMEM((ROWS * SUB, 128), F32)],
        name="forward_conv",
        **params_of(5_000_000_000, 4_000_000),
    )(own_array, sent, mixed, query, table)

    other_gated = lax.ppermute(gated, "ctx", swap)
    other_cots = lax.ppermute(lax.dynamic_slice_in_dim(cots, 256 * (1 - core), 256, axis=2), "ctx", swap)

    partial_out = pl.pallas_call(
        output_kernel,
        grid=(8,),
        out_shape=bf16(8, ROWS, 512),
        in_specs=[
            pl.BlockSpec((ROWS, 1024), lambda p: (0, 0)),
            pl.BlockSpec((1024, 512), lambda p: (0, p)),
        ],
        out_specs=pl.BlockSpec((1, ROWS, 512), lambda p: (p, 0, 0)),
        name="output_projection",
        **params_of(2_147_483_648, 11_000_000),
    )(gated, w_out)
    output = exchange(partial_out, "tp").astype(F32).sum(axis=0).astype(BF16)

    partial_weight = pl.pallas_call(
        weight_kernel,
        grid_spec=pltpu.PrefetchScalarGridSpec(
            num_scalar_prefetch=1,
            grid=(8,),
            in_specs=[
                pl.BlockSpec((ROWS, 1024), lambda p, c: (0, 0)),
                pl.BlockSpec((ROWS, 1024), lambda p, c: (0, 0)),
                pl.BlockSpec((1, ROWS, 256), lambda p, c: (p, 0, c[0])),
                pl.BlockSpec((1, ROWS, 256), lambda p, c: (p, 0, 0)),
            ],
            out_specs=pl.BlockSpec((1, 1024, 256), lambda p, c: (p, 0, 0)),
            scratch_shapes=[pltpu.VMEM((1024, 2 * ROWS), BF16)],
        ),
        out_shape=bf16(8, 1024, 256),
        name="projection_gradient",
        **params_of(2_147_483_648, 8_000_000),
    )(core.reshape(1).astype(jnp.int32), gated, other_gated, cots, other_cots)
    d_weight = exchange(partial_weight, "ctx", same_core).astype(F32).sum(axis=0)

    d_query, d_conv, back, back_sent = pl.pallas_call(
        cotangent_kernel,
        grid=(8,),
        out_shape=(bf16(ROWS, 1024), f32(ROWS * SUB, 128), f32(MODES, SUB, 128), bf16(MODES, SUB, 128)),
        in_specs=[
            pl.BlockSpec((1, ROWS, 512), lambda p: (p, 0, 0)),
            pl.BlockSpec((1024, 512), lambda p: (0, p)),
            pl.BlockSpec((ROWS, 1024), lambda p: (0, 0)),
            pl.BlockSpec((ROWS, 1024), lambda p: (0, 0)),
            pl.BlockSpec((40, SUB, 128), lambda p: (0, 0, 0)),
        ],
        out_specs=(
            pl.BlockSpec((ROWS, 1024), lambda p: (0, 0)),
            pl.BlockSpec((ROWS * SUB, 128), lambda p: (0, 0)),
            pl.BlockSpec((MODES, SUB, 128), lambda p: (0, 0, 0)),
            pl.BlockSpec((MODES, SUB, 128), lambda p: (0, 0, 0)),
        ),
        scratch_shapes=[pltpu.VMEM((ROWS, 1024), F32)],
        name="cotangent_states",
        **params_of(5_000_000_000, 13_000_000),
    )(cots, w_out, query, conv_out, table)
    back_all = to_all(back_sent, "ctx", BLOCKS)

    parts = pl.pallas_call(
        filter_kernel,
        out_shape=f32(72, SUB, 128),
        in_specs=[whole()] * 5,
        out_specs=whole(),
        name="filter_gradients",
        **params_of(9_000_000_000, 4_000_000),
    )(mixed, d_conv, carry, back, table)
    parts = exchange(
        parts.reshape(72, SUB, 2, 64).transpose(1, 2, 0, 3).reshape(BLOCKS, 72, 64), "ctx"
    )

    d_key, d_value, _ = pl.pallas_call(
        backward_kernel,
        out_shape=(bf16(ROWS, 1024), bf16(ROWS, 1024), f32(MODES, SUB, 128)),
        in_specs=[smem] + [whole()] * 5,
        out_specs=(whole(),) * 3,
        scratch_shapes=[pltpu.VMEM((ROWS * SUB, 128), F32)],
        name="backward_conv",
        **params_of(5_000_000_000, 4_000_000),
    )(own_array, back_all, d_conv, key_part, value_part, table)

    d_residue, d_rate, d_skip = pl.pallas_call(
        owner_kernel,
        out_shape=(f32(MODES, 64), f32(MODES, 64), f32(1, 64)),
        in_specs=[whole()] * 3,
        out_specs=(whole(),) * 3,
        name="owner_sums",
        **params_of(1_000_000, 400_000),
    )(parts, rate_t, residue_t)
    return (output, d_query, d_key, d_value, d_weight, d_residue.T, d_rate.T, d_skip[0])


def solution(mesh):
    rows, owner = P("ctx", "tp"), P(("tp", "ctx"))
    return jax.shard_map(
        local,
        mesh=mesh,
        in_specs=(rows, rows, rows, rows, P("tp", None), P(("tp", "ctx"), None), P(("tp", "ctx"), None), owner),
        out_specs=(rows, rows, rows, rows, P("tp", "ctx"), P(("tp", "ctx"), None), P(("tp", "ctx"), None), owner),
        check_vma=False,
    )
```

```python
import functools

import jax
import jax.numpy as jnp
from jax import lax
from jax.experimental import pallas as pl
from jax.experimental.pallas import tpu as pltpu
from jax.sharding import PartitionSpec as P

F32 = jnp.float32
BF16 = jnp.bfloat16
SEQ = 4096
MODES = 16
ROWS = 256
SUB = 8
BLOCKS = 16
HALF = 512
UNROLL = 8
VMEM = 48 * 1024 * 1024


def params_of(flops, nbytes):
    return dict(
        compiler_params=pltpu.CompilerParams(vmem_limit_bytes=VMEM),
        cost_estimate=pl.CostEstimate(flops=flops, bytes_accessed=nbytes, transcendentals=0),
    )


def whole():
    return pl.BlockSpec(memory_space=pltpu.VMEM)


def full(*shape):
    return pl.BlockSpec(shape, lambda *_: (0,) * len(shape))


def lanes(group):
    return slice(128 * group, 128 * (group + 1))


def group_rows(group):
    return pl.ds(group, ROWS, stride=SUB)


def step_decay(table, mode):
    return jnp.exp(table[mode] * (-1.0 / SEQ))


def block_decay(table, mode):
    return jnp.exp(table[mode] * (-float(ROWS) / SEQ))


def mode_weight(table, mode):
    return table[MODES + mode] * jnp.sqrt(table[mode] * (2.0 / SEQ))


def at(ref, step):
    return ref[pl.ds(pl.multiple_of(step * SUB, SUB), SUB), :]


def zeros(count):
    return tuple(jnp.zeros((SUB, 128), F32) for _ in range(count))


def tree_sum(parts):
    parts = list(parts)
    while len(parts) > 1:
        parts = [sum(parts[i : i + 2]) for i in range(0, len(parts), 2)]
    return parts[0]


def states_kernel(key_ref, value_ref, table, mixed_ref, state_ref):
    for group in range(SUB):
        product = key_ref[:, lanes(group)].astype(F32) * value_ref[:, lanes(group)].astype(F32)
        mixed_ref[group_rows(group), :] = product.astype(BF16).astype(F32)
    decay = [step_decay(table, m) for m in range(MODES)]

    def body(i, held):
        for u in range(UNROLL):
            value = at(mixed_ref, i * UNROLL + u)
            held = tuple(decay[m] * held[m] + value for m in range(MODES))
        return held

    held = lax.fori_loop(0, ROWS // UNROLL, body, zeros(MODES))
    for m in range(MODES):
        state_ref[m] = held[m].astype(state_ref.dtype)


def forward_kernel(own_ref, sent_ref, mixed_ref, query_ref, table, conv_ref, gated_ref, carry_ref, buffer):
    own = own_ref[0]
    for m in range(MODES):
        far = block_decay(table, m)
        carry = jnp.zeros((SUB, 128), F32)
        for j in range(BLOCKS - 1):
            carry = jnp.where(j < own, far * carry + sent_ref[j, m].astype(F32), carry)
        carry_ref[m] = carry
    decay = [step_decay(table, m) for m in range(MODES)]
    weight = [mode_weight(table, m) for m in range(MODES)]
    skip = table[2 * MODES]

    def body(i, held):
        for u in range(UNROLL):
            step = i * UNROLL + u
            value = at(mixed_ref, step)
            held = tuple(decay[m] * held[m] + value for m in range(MODES))
            total = tree_sum([weight[m] * held[m] for m in range(MODES)])
            buffer[pl.ds(pl.multiple_of(step * SUB, SUB), SUB), :] = total + skip * value
        return held

    lax.fori_loop(0, ROWS // UNROLL, body, tuple(carry_ref[m] for m in range(MODES)))
    for group in range(SUB):
        conv = buffer[group_rows(group), :].astype(BF16)
        conv_ref[:, lanes(group)] = conv
        gated_ref[:, lanes(group)] = (query_ref[:, lanes(group)].astype(F32) * conv.astype(F32)).astype(BF16)


def output_kernel(order_ref, gated_ref, weight_ref, out_ref):
    out_ref[0] = jnp.dot(gated_ref[...], weight_ref[...], preferred_element_type=F32).astype(BF16)


def weight_kernel(place_ref, gated_ref, other_ref, cot_ref, other_cot_ref, first_ref, second_ref, turned):
    @pl.when(pl.program_id(0) == 0)
    def _():
        turned[:, :ROWS] = gated_ref[...].T
        turned[:, ROWS:] = other_ref[...].T

    total = jnp.dot(turned[:, :ROWS], cot_ref[0], preferred_element_type=F32)
    total += jnp.dot(turned[:, ROWS:], other_cot_ref[0], preferred_element_type=F32)
    first_ref[0] = total[:HALF].astype(BF16)
    second_ref[0] = total[HALF:].astype(BF16)


def cotangent_kernel(order_ref, cot_ref, weight_ref, query_ref, conv_ref, table, dquery_ref, dconv_ref, state_ref, sent_ref, total):
    part = pl.program_id(0)
    product = lax.dot_general(cot_ref[0], weight_ref[...], (((1,), (1,)), ((), ())), preferred_element_type=F32)

    @pl.when(part == 0)
    def _():
        total[...] = product

    @pl.when(part > 0)
    def _():
        total[...] += product

    @pl.when(part == pl.num_programs(0) - 1)
    def _():
        for group in range(SUB):
            cot = total[:, lanes(group)]
            dquery_ref[:, lanes(group)] = (cot * conv_ref[:, lanes(group)].astype(F32)).astype(BF16)
            dconv_ref[group_rows(group), :] = (cot * query_ref[:, lanes(group)].astype(F32)).astype(BF16).astype(F32)
        decay = [step_decay(table, m) for m in range(MODES)]

        def body(i, held):
            for u in range(UNROLL):
                value = at(dconv_ref, ROWS - 1 - (i * UNROLL + u))
                held = tuple(decay[m] * held[m] + value for m in range(MODES))
            return held

        held = lax.fori_loop(0, ROWS // UNROLL, body, zeros(MODES))
        for m in range(MODES):
            state_ref[m] = held[m]
            sent_ref[m] = held[m].astype(sent_ref.dtype)


def filter_kernel(mixed_ref, dconv_ref, carry_ref, back_ref, table, out_ref):
    half = MODES // 2
    for first in (0, half):
        modes = range(first, first + half)
        decay = [step_decay(table, m) for m in modes]

        def body(i, packed):
            held, moment, first_sum, second_sum, skip_sum = packed
            for u in range(UNROLL):
                value = at(mixed_ref, i * UNROLL + u)
                cot = at(dconv_ref, i * UNROLL + u)
                past = [decay[m] * held[m] for m in range(half)]
                moment = tuple(decay[m] * moment[m] + past[m] for m in range(half))
                held = tuple(past[m] + value for m in range(half))
                first_sum = tuple(first_sum[m] + cot * held[m] for m in range(half))
                second_sum = tuple(second_sum[m] + cot * moment[m] for m in range(half))
                skip_sum = skip_sum + cot * value
            return (held, moment, first_sum, second_sum, skip_sum)

        start = (tuple(carry_ref[m] for m in modes), zeros(half), zeros(half), zeros(half), zeros(1)[0])
        held, moment, first_sum, second_sum, skip_sum = lax.fori_loop(0, ROWS // UNROLL, body, start)
        for m in range(half):
            out_ref[first + m] = first_sum[m]
            out_ref[MODES + first + m] = second_sum[m]
            out_ref[2 * MODES + first + m] = moment[m]
            out_ref[3 * MODES + first + m] = back_ref[first + m]
        out_ref[4 * MODES] = skip_sum


def backward_kernel(own_ref, sent_ref, dconv_ref, key_ref, value_ref, table, dkey_ref, dvalue_ref, carry_ref, buffer):
    own = own_ref[0]
    for m in range(MODES):
        far = block_decay(table, m)
        carry = jnp.zeros((SUB, 128), F32)
        for j in range(BLOCKS - 1, 0, -1):
            carry = jnp.where(j > own, far * carry + sent_ref[j, m].astype(F32), carry)
        carry_ref[m] = carry
    decay = [step_decay(table, m) for m in range(MODES)]
    weight = [mode_weight(table, m) for m in range(MODES)]
    skip = table[2 * MODES]

    def body(i, held):
        for u in range(UNROLL):
            step = ROWS - 1 - (i * UNROLL + u)
            value = at(dconv_ref, step)
            held = tuple(decay[m] * held[m] + value for m in range(MODES))
            total = tree_sum([weight[m] * held[m] for m in range(MODES)])
            buffer[pl.ds(pl.multiple_of(step * SUB, SUB), SUB), :] = total + skip * value
        return held

    lax.fori_loop(0, ROWS // UNROLL, body, tuple(carry_ref[m] for m in range(MODES)))
    for group in range(SUB):
        grad = buffer[group_rows(group), :].astype(BF16).astype(F32)
        dkey_ref[:, lanes(group)] = (grad * value_ref[:, lanes(group)].astype(F32)).astype(BF16)
        dvalue_ref[:, lanes(group)] = (grad * key_ref[:, lanes(group)].astype(F32)).astype(BF16)


def owner_kernel(parts_ref, rate_ref, residue_ref, dresidue_ref, drate_ref, dskip_ref):
    rate = rate_ref[...]
    residue = residue_ref[...]
    near = jnp.exp(rate * (-1.0 / SEQ))
    far = jnp.exp(rate * (-float(ROWS) / SEQ))
    scale = jnp.sqrt(rate * (2.0 / SEQ))
    first = jnp.zeros_like(rate)
    second = jnp.zeros_like(rate)
    skip = jnp.zeros((1, rate.shape[1]), F32)
    later = jnp.zeros_like(rate)
    for j in range(BLOCKS - 1, -1, -1):
        first += parts_ref[j, 0:MODES]
        second += parts_ref[j, MODES : 2 * MODES] + near * later * parts_ref[j, 2 * MODES : 3 * MODES]
        later = far * later + parts_ref[j, 3 * MODES : 4 * MODES]
        skip += parts_ref[j, 4 * MODES : 4 * MODES + 1]
    proj = scale * first
    dresidue_ref[...] = proj
    drate_ref[...] = residue * (0.5 * proj / rate - scale * second * (1.0 / SEQ))
    dskip_ref[...] = skip


def f32(*shape):
    return jax.ShapeDtypeStruct(shape, F32)


def bf16(*shape):
    return jax.ShapeDtypeStruct(shape, BF16)


def exchange(array, axis, groups=None):
    return lax.all_to_all(array, axis, split_axis=0, concat_axis=0, tiled=True, axis_index_groups=groups)


def to_all(array, axis, count):
    return exchange(jnp.broadcast_to(array[None], (count,) + array.shape), axis)


def ring_shift(k):
    return [(2 * x + z, 2 * ((x + k) % 4) + z) for x in range(4) for z in range(2)]


def local(query, key_part, value_part, out_cotangent, w_out, residue, rate, skip):
    own = lax.axis_index("ctx")
    own_array = own.reshape(1).astype(jnp.int32)
    core, side = own % 2, own // 8
    place = lax.axis_index("tp")
    place_x, place_z = place // 2, place % 2
    smem = pl.BlockSpec(memory_space=pltpu.SMEM)
    core_swap = [(i, i ^ 1) for i in range(BLOCKS)]
    far_swap = [(i, i ^ 8) for i in range(BLOCKS)]
    near_swap = [(i, i ^ 1) for i in range(8)]
    columns = [[8 * z + 2 * y + c for y in range(4)] for z in range(2) for c in range(2)]

    steps = jnp.arange(8, dtype=jnp.int32)
    came = ((place_x - steps // 2) % 4) * 2 + (place_z + steps) % 2
    goes = ((place_x + steps // 2) % 4) * 2 + (place_z + steps) % 2

    cot_pair = jnp.stack([out_cotangent, lax.ppermute(out_cotangent, "tp", near_swap)])

    rate_t, residue_t = rate.T, residue.T
    mine = jnp.concatenate([rate_t, residue_t, skip[None], jnp.zeros((7, skip.shape[0]), F32)], axis=0)
    table = to_all(mine, "ctx", BLOCKS).reshape(SUB, 2, 40, 64).transpose(2, 0, 1, 3).reshape(40, SUB, 128)
    cots = jnp.concatenate([cot_pair] + [lax.ppermute(cot_pair, "tp", ring_shift(k)) for k in (1, 2, 3)])

    mixed, state = pl.pallas_call(
        states_kernel,
        grid=(1,),
        out_shape=(f32(ROWS * SUB, 128), bf16(MODES, SUB, 128)),
        in_specs=[full(ROWS, 1024), full(ROWS, 1024), full(40, SUB, 128)],
        out_specs=(full(ROWS * SUB, 128), full(MODES, SUB, 128)),
        name="forward_states",
        **params_of(3_000_000_000, 4_000_000),
    )(key_part, value_part, table)
    sent = to_all(state, "ctx", BLOCKS)

    conv_out, gated, carry = pl.pallas_call(
        forward_kernel,
        grid=(1,),
        out_shape=(bf16(ROWS, 1024), bf16(ROWS, 1024), f32(MODES, SUB, 128)),
        in_specs=[smem, full(BLOCKS, MODES, SUB, 128), full(ROWS * SUB, 128), full(ROWS, 1024), full(40, SUB, 128)],
        out_specs=(full(ROWS, 1024), full(ROWS, 1024), full(MODES, SUB, 128)),
        scratch_shapes=[pltpu.VMEM((ROWS * SUB, 128), F32)],
        name="forward_conv",
        **params_of(5_000_000_000, 4_000_000),
    )(own_array, sent, mixed, query, table)

    other_gated = lax.ppermute(gated, "ctx", core_swap)
    other_cots = lax.ppermute(lax.dynamic_slice_in_dim(cots, 256 * (1 - core), 256, axis=2), "ctx", core_swap)

    partial_out = pl.pallas_call(
        output_kernel,
        grid_spec=pltpu.PrefetchScalarGridSpec(
            num_scalar_prefetch=1,
            grid=(8,),
            in_specs=[
                pl.BlockSpec((ROWS, 1024), lambda p, order: (0, 0)),
                pl.BlockSpec((1024, 512), lambda p, order: (0, order[p])),
            ],
            out_specs=pl.BlockSpec((1, ROWS, 512), lambda p, order: (p, 0, 0)),
        ),
        out_shape=bf16(8, ROWS, 512),
        name="output_projection",
        **params_of(2_147_483_648, 11_000_000),
    )(goes, gated, w_out)
    arrived = [lax.ppermute(partial_out[2 * k : 2 * k + 2], "tp", ring_shift(k)) for k in (1, 2, 3)]
    along_x = partial_out[:2].astype(F32) + sum(part.astype(F32) for part in arrived)
    output = (along_x[0] + lax.ppermute(along_x[1].astype(BF16), "tp", near_swap).astype(F32)).astype(BF16)

    first, second = pl.pallas_call(
        weight_kernel,
        grid_spec=pltpu.PrefetchScalarGridSpec(
            num_scalar_prefetch=1,
            grid=(8,),
            in_specs=[
                pl.BlockSpec((ROWS, 1024), lambda p, c: (0, 0)),
                pl.BlockSpec((ROWS, 1024), lambda p, c: (0, 0)),
                pl.BlockSpec((1, ROWS, 256), lambda p, c: (p, 0, c[8])),
                pl.BlockSpec((1, ROWS, 256), lambda p, c: (p, 0, 0)),
            ],
            out_specs=(
                pl.BlockSpec((1, HALF, 256), lambda p, c: (2 * (c[p] % 4) + (c[p] // 4 + c[9]) % 2, 0, 0)),
                pl.BlockSpec((1, HALF, 256), lambda p, c: (4 * ((c[p] // 4 + c[9]) % 2) + c[p] % 4, 0, 0)),
            ),
            scratch_shapes=[pltpu.VMEM((1024, 2 * ROWS), BF16)],
        ),
        out_shape=(bf16(8, HALF, 256), bf16(8, HALF, 256)),
        name="projection_gradient",
        **params_of(2_147_483_648, 8_000_000),
    )(jnp.concatenate([came, jnp.stack([core, side]).astype(jnp.int32)]), gated, other_gated, cots, other_cots)
    along_y = lax.psum_scatter(first, "ctx", scatter_dimension=0, tiled=True, axis_index_groups=columns)
    along_z = (second[:4].astype(F32) + lax.ppermute(second[4:], "ctx", far_swap).astype(F32)).astype(BF16)
    first_sum = along_y[0].astype(F32) + lax.ppermute(along_y[1], "ctx", far_swap).astype(F32)
    second_sum = lax.psum_scatter(along_z, "ctx", scatter_dimension=0, tiled=True, axis_index_groups=columns)[0]
    d_weight = jnp.concatenate([first_sum, second_sum.astype(F32)])

    d_query, d_conv, back, back_sent = pl.pallas_call(
        cotangent_kernel,
        grid_spec=pltpu.PrefetchScalarGridSpec(
            num_scalar_prefetch=1,
            grid=(8,),
            in_specs=[
                pl.BlockSpec((1, ROWS, 512), lambda p, order: (p, 0, 0)),
                pl.BlockSpec((1024, 512), lambda p, order: (0, order[p])),
                full(ROWS, 1024),
                full(ROWS, 1024),
                full(40, SUB, 128),
            ],
            out_specs=(
                full(ROWS, 1024),
                full(ROWS * SUB, 128),
                full(MODES, SUB, 128),
                full(MODES, SUB, 128),
            ),
            scratch_shapes=[pltpu.VMEM((ROWS, 1024), F32)],
        ),
        out_shape=(bf16(ROWS, 1024), f32(ROWS * SUB, 128), f32(MODES, SUB, 128), bf16(MODES, SUB, 128)),
        name="cotangent_states",
        **params_of(5_000_000_000, 13_000_000),
    )(came, cots, w_out, query, conv_out, table)
    back_all = to_all(back_sent, "ctx", BLOCKS)

    parts = pl.pallas_call(
        filter_kernel,
        grid=(1,),
        out_shape=f32(72, SUB, 128),
        in_specs=[full(ROWS * SUB, 128), full(ROWS * SUB, 128)] + [full(MODES, SUB, 128)] * 2 + [full(40, SUB, 128)],
        out_specs=full(72, SUB, 128),
        name="filter_gradients",
        **params_of(9_000_000_000, 4_000_000),
    )(mixed, d_conv, carry, back, table)
    parts = exchange(
        parts.reshape(72, SUB, 2, 64).transpose(1, 2, 0, 3).reshape(BLOCKS, 72, 64), "ctx"
    )

    d_key, d_value, _ = pl.pallas_call(
        backward_kernel,
        grid=(1,),
        out_shape=(bf16(ROWS, 1024), bf16(ROWS, 1024), f32(MODES, SUB, 128)),
        in_specs=[
            smem,
            full(BLOCKS, MODES, SUB, 128),
            full(ROWS * SUB, 128),
            full(ROWS, 1024),
            full(ROWS, 1024),
            full(40, SUB, 128),
        ],
        out_specs=(full(ROWS, 1024), full(ROWS, 1024), full(MODES, SUB, 128)),
        scratch_shapes=[pltpu.VMEM((ROWS * SUB, 128), F32)],
        name="backward_conv",
        **params_of(5_000_000_000, 4_000_000),
    )(own_array, back_all, d_conv, key_part, value_part, table)

    d_residue, d_rate, d_skip = pl.pallas_call(
        owner_kernel,
        out_shape=(f32(MODES, 64), f32(MODES, 64), f32(1, 64)),
        in_specs=[whole()] * 3,
        out_specs=(whole(),) * 3,
        name="owner_sums",
        **params_of(1_000_000, 400_000),
    )(parts, rate_t, residue_t)
    return (output, d_query, d_key, d_value, d_weight, d_residue.T, d_rate.T, d_skip[0])


def solution(mesh):
    rows, owner = P("ctx", "tp"), P(("tp", "ctx"))
    return jax.shard_map(
        local,
        mesh=mesh,
        in_specs=(rows, rows, rows, rows, P("tp", None), P(("tp", "ctx"), None), P(("tp", "ctx"), None), owner),
        out_specs=(rows, rows, rows, rows, P("tp", "ctx"), P(("tp", "ctx"), None), P(("tp", "ctx"), None), owner),
        check_vma=False,
    )
```

```python
import functools

import jax
import jax.numpy as jnp
from jax import lax
from jax.experimental import pallas as pl
from jax.experimental.pallas import tpu as pltpu
from jax.sharding import PartitionSpec as P

F32 = jnp.float32
BF16 = jnp.bfloat16
SEQ = 4096
MODES = 16
ROWS = 256
SUB = 8
BLOCKS = 16
HALF = 512
UNROLL = 8
PACK = 24
TABLE = 2 * PACK * SUB
TERMS = 40
VMEM = 40 * 1024 * 1024


def params_of(flops, nbytes):
    return dict(
        compiler_params=pltpu.CompilerParams(vmem_limit_bytes=VMEM),
        cost_estimate=pl.CostEstimate(flops=flops, bytes_accessed=nbytes, transcendentals=0),
    )


def whole():
    return pl.BlockSpec(memory_space=pltpu.VMEM)


def full(*shape):
    return pl.BlockSpec(shape, lambda *_: (0,) * len(shape))


def lanes(group):
    return slice(128 * group, 128 * (group + 1))


def group_rows(group):
    return pl.ds(group, ROWS, stride=SUB)


def rate_of(table, mode):
    return table[SUB * mode : SUB * (mode + 1), :]


def step_decay(table, mode):
    return jnp.exp(rate_of(table, mode) * (-1.0 / SEQ))


def block_decay(table, mode):
    return jnp.exp(rate_of(table, mode) * (-float(ROWS) / SEQ))


def mode_weight(table, mode):
    return rate_of(table, PACK + mode) * jnp.sqrt(rate_of(table, mode) * (2.0 / SEQ))


def skip_of(table):
    return rate_of(table, MODES)


def at(ref, step):
    return ref[pl.ds(pl.multiple_of(step * SUB, SUB), SUB), :]


def zeros(count):
    return tuple(jnp.zeros((SUB, 128), F32) for _ in range(count))


def tree_sum(parts):
    parts = list(parts)
    while len(parts) > 1:
        parts = [sum(parts[i : i + 2]) for i in range(0, len(parts), 2)]
    return parts[0]


def states_kernel(key_ref, value_ref, packed_ref, mixed_ref, sent_ref, table):
    left = lax.broadcasted_iota(jnp.int32, (PACK, 128), 1) < 64
    for group in range(SUB):
        one, two = packed_ref[2 * group], packed_ref[2 * group + 1]
        table[pl.ds(group, PACK, stride=SUB), :] = jnp.where(left, one, pltpu.roll(two, 64, 1))
        table[pl.ds(PACK * SUB + group, PACK, stride=SUB), :] = jnp.where(left, pltpu.roll(one, 64, 1), two)
        product = key_ref[:, lanes(group)].astype(F32) * value_ref[:, lanes(group)].astype(F32)
        mixed_ref[group_rows(group), :] = product.astype(BF16).astype(F32)
    decay = [step_decay(table, m) for m in range(MODES)]

    def body(i, held):
        for u in range(UNROLL):
            value = at(mixed_ref, i * UNROLL + u)
            held = tuple(decay[m] * held[m] + value for m in range(MODES))
        return held

    held = lax.fori_loop(0, ROWS // UNROLL, body, zeros(MODES))
    for m in range(MODES):
        state = held[m].astype(BF16)
        for j in range(BLOCKS):
            sent_ref[j, m] = state


def forward_kernel(own_ref, sent_ref, mixed_ref, query_ref, table, conv_ref, gated_ref, carry_ref, buffer):
    own = own_ref[0]
    for m in range(MODES):
        far = block_decay(table, m)
        carry = jnp.zeros((SUB, 128), F32)
        for j in range(BLOCKS - 1):
            carry = jnp.where(j < own, far * carry + sent_ref[j, m].astype(F32), carry)
        carry_ref[m] = carry
    decay = [step_decay(table, m) for m in range(MODES)]
    weight = [mode_weight(table, m) for m in range(MODES)]
    skip = skip_of(table)

    def body(i, held):
        for u in range(UNROLL):
            step = i * UNROLL + u
            value = at(mixed_ref, step)
            held = tuple(decay[m] * held[m] + value for m in range(MODES))
            total = tree_sum([weight[m] * held[m] for m in range(MODES)])
            buffer[pl.ds(pl.multiple_of(step * SUB, SUB), SUB), :] = total + skip * value
        return held

    lax.fori_loop(0, ROWS // UNROLL, body, tuple(carry_ref[m] for m in range(MODES)))
    for group in range(SUB):
        conv = buffer[group_rows(group), :].astype(BF16)
        conv_ref[:, lanes(group)] = conv
        gated_ref[:, lanes(group)] = (query_ref[:, lanes(group)].astype(F32) * conv.astype(F32)).astype(BF16)


def output_kernel(order_ref, gated_ref, weight_ref, *out_refs):
    for i in range(8):
        columns = pl.ds(pl.multiple_of(order_ref[i] * 512, 512), 512)
        out_refs[i // 2][i % 2] = jnp.dot(gated_ref[...], weight_ref[:, columns], preferred_element_type=F32).astype(BF16)


def weight_kernel(index_ref, gated_ref, other_ref, cot_ref, other_cot_ref, *refs):
    along_y, along_z, turned = refs[:4], refs[4:6], refs[6]
    turned[:, :ROWS] = gated_ref[...].T
    turned[:, ROWS:] = other_ref[...].T
    for z in (1, 0):
        for k in range(4):
            block = index_ref[4 * z + k]
            total = jnp.dot(turned[:, :ROWS], cot_ref[block], preferred_element_type=F32)
            total += jnp.dot(turned[:, ROWS:], other_cot_ref[block], preferred_element_type=F32)
            along_y[k][z] = total[:HALF].astype(BF16)
            along_z[z][k] = total[HALF:].astype(BF16)


def cotangent_kernel(order_ref, cot_ref, weight_ref, query_ref, conv_ref, table, dquery_ref, dconv_ref, state_ref, sent_ref, total):
    for i in range(8):
        columns = pl.ds(pl.multiple_of(order_ref[i] * 512, 512), 512)
        product = lax.dot_general(cot_ref[i], weight_ref[:, columns], (((1,), (1,)), ((), ())), preferred_element_type=F32)
        if i == 0:
            total[...] = product
        else:
            total[...] += product
    for group in range(SUB):
        cot = total[:, lanes(group)]
        dquery_ref[:, lanes(group)] = (cot * conv_ref[:, lanes(group)].astype(F32)).astype(BF16)
        dconv_ref[group_rows(group), :] = (cot * query_ref[:, lanes(group)].astype(F32)).astype(BF16).astype(F32)
    decay = [step_decay(table, m) for m in range(MODES)]

    def body(i, held):
        for u in range(UNROLL):
            value = at(dconv_ref, ROWS - 1 - (i * UNROLL + u))
            held = tuple(decay[m] * held[m] + value for m in range(MODES))
        return held

    held = lax.fori_loop(0, ROWS // UNROLL, body, zeros(MODES))
    for m in range(MODES):
        state_ref[m] = held[m]
        state = held[m].astype(BF16)
        for j in range(BLOCKS):
            sent_ref[j, m] = state


def filter_kernel(mixed_ref, dconv_ref, carry_ref, back_ref, table, out_ref):
    left = lax.broadcasted_iota(jnp.int32, (SUB, 128), 1) < 64

    def put(row, one, two):
        out_ref[pl.ds(row, SUB, stride=2 * TERMS), :] = jnp.where(left, one, pltpu.roll(two, 64, 1))
        out_ref[pl.ds(TERMS + row, SUB, stride=2 * TERMS), :] = jnp.where(left, pltpu.roll(one, 64, 1), two)

    half = MODES // 2
    for first in (0, half):
        modes = range(first, first + half)
        decay = [step_decay(table, m) for m in modes]

        def body(i, packed):
            held, moment, first_sum, second_sum, skip_sum = packed
            for u in range(UNROLL):
                value = at(mixed_ref, i * UNROLL + u)
                cot = at(dconv_ref, i * UNROLL + u)
                past = [decay[m] * held[m] for m in range(half)]
                moment = tuple(decay[m] * moment[m] + past[m] for m in range(half))
                held = tuple(past[m] + value for m in range(half))
                first_sum = tuple(first_sum[m] + cot * held[m] for m in range(half))
                second_sum = tuple(second_sum[m] + cot * moment[m] for m in range(half))
                skip_sum = skip_sum + cot * value
            return (held, moment, first_sum, second_sum, skip_sum)

        start = (tuple(carry_ref[m] for m in modes), zeros(half), zeros(half), zeros(half), zeros(1)[0])
        held, moment, first_sum, second_sum, skip_sum = lax.fori_loop(0, ROWS // UNROLL, body, start)
        for m in range(half):
            put(first + m, first_sum[m], second_sum[m])
            put(MODES + first + m, moment[m], back_ref[first + m])
    for row in range(2 * MODES, TERMS):
        put(row, skip_sum, skip_sum)


def backward_kernel(own_ref, sent_ref, dconv_ref, key_ref, value_ref, table, dkey_ref, dvalue_ref, carry_ref, buffer):
    own = own_ref[0]
    for m in range(MODES):
        far = block_decay(table, m)
        carry = jnp.zeros((SUB, 128), F32)
        for j in range(BLOCKS - 1, 0, -1):
            carry = jnp.where(j > own, far * carry + sent_ref[j, m].astype(F32), carry)
        carry_ref[m] = carry
    decay = [step_decay(table, m) for m in range(MODES)]
    weight = [mode_weight(table, m) for m in range(MODES)]
    skip = skip_of(table)

    def body(i, held):
        for u in range(UNROLL):
            step = ROWS - 1 - (i * UNROLL + u)
            value = at(dconv_ref, step)
            held = tuple(decay[m] * held[m] + value for m in range(MODES))
            total = tree_sum([weight[m] * held[m] for m in range(MODES)])
            buffer[pl.ds(pl.multiple_of(step * SUB, SUB), SUB), :] = total + skip * value
        return held

    lax.fori_loop(0, ROWS // UNROLL, body, tuple(carry_ref[m] for m in range(MODES)))
    for group in range(SUB):
        grad = buffer[group_rows(group), :].astype(BF16).astype(F32)
        dkey_ref[:, lanes(group)] = (grad * value_ref[:, lanes(group)].astype(F32)).astype(BF16)
        dvalue_ref[:, lanes(group)] = (grad * key_ref[:, lanes(group)].astype(F32)).astype(BF16)


def owner_kernel(parts_ref, rate_ref, residue_ref, dresidue_ref, drate_ref, dskip_ref):
    rate = rate_ref[...]
    residue = residue_ref[...]
    near = jnp.exp(rate * (-1.0 / SEQ))
    far = jnp.exp(rate * (-float(ROWS) / SEQ))
    scale = jnp.sqrt(rate * (2.0 / SEQ))
    first = jnp.zeros_like(rate)
    second = jnp.zeros_like(rate)
    skip = jnp.zeros((1, rate.shape[1]), F32)
    later = jnp.zeros_like(rate)
    for j in range(BLOCKS - 1, -1, -1):
        sums, ends = parts_ref[j, 0:MODES], parts_ref[j, MODES : 2 * MODES]
        first += sums[:, :64]
        second += sums[:, 64:] + near * later * ends[:, :64]
        later = far * later + ends[:, 64:]
        skip += parts_ref[j, 2 * MODES : 2 * MODES + 1, :64]
    proj = scale * first
    dresidue_ref[...] = proj
    drate_ref[...] = residue * (0.5 * proj / rate - scale * second * (1.0 / SEQ))
    dskip_ref[...] = skip


def f32(*shape):
    return jax.ShapeDtypeStruct(shape, F32)


def bf16(*shape):
    return jax.ShapeDtypeStruct(shape, BF16)


def exchange(array, axis, groups=None):
    return lax.all_to_all(array, axis, split_axis=0, concat_axis=0, tiled=True, axis_index_groups=groups)


def to_all(array, axis, count):
    return exchange(jnp.broadcast_to(array[None], (count,) + array.shape), axis)


def shift_x(k):
    return [(2 * x + z, 2 * ((x + k) % 4) + z) for x in range(4) for z in range(2)]


def shift_y(k):
    return [(8 * z + 2 * y + c, 8 * z + 2 * ((y + k) % 4) + c) for z in range(2) for y in range(4) for c in range(2)]


def local(query, key_part, value_part, out_cotangent, w_out, residue, rate, skip):
    own = lax.axis_index("ctx")
    own_array = own.reshape(1).astype(jnp.int32)
    core, own_y, own_z = own % 2, own // 2 % 4, own // 8
    place = lax.axis_index("tp")
    place_x, place_z = place // 2, place % 2
    smem = pl.BlockSpec(memory_space=pltpu.SMEM)
    core_swap = [(i, i ^ 1) for i in range(BLOCKS)]
    far_swap = [(i, i ^ 8) for i in range(BLOCKS)]
    near_swap = [(i, i ^ 1) for i in range(8)]

    steps = jnp.arange(8, dtype=jnp.int32)
    came = ((place_x - steps // 2) % 4) * 2 + (place_z + steps) % 2
    goes = ((place_x + steps // 2) % 4) * 2 + (place_z + steps) % 2
    chip = ((own_z + steps // 4) % 2) * 4 + (own_y + steps) % 4
    index = 2 * ((place_x - chip // 2) % 4) + (chip - place_z) % 2

    packed = jnp.concatenate(
        [
            jnp.concatenate([rate.T, residue.T], axis=1),
            jnp.broadcast_to(jnp.concatenate([skip, skip])[None], (PACK - MODES, 128)),
        ]
    )
    packed = to_all(packed, "ctx", BLOCKS)

    cot_pair = jnp.stack([out_cotangent, lax.ppermute(out_cotangent, "tp", near_swap)])
    cots = jnp.concatenate([cot_pair] + [lax.ppermute(cot_pair, "tp", shift_x(k)) for k in (1, 2, 3)])

    mixed, sent, table = pl.pallas_call(
        states_kernel,
        grid=(1,),
        out_shape=(f32(ROWS * SUB, 128), bf16(BLOCKS, MODES, SUB, 128), f32(TABLE, 128)),
        in_specs=[full(ROWS, 1024), full(ROWS, 1024), full(BLOCKS, PACK, 128)],
        out_specs=(full(ROWS * SUB, 128), full(BLOCKS, MODES, SUB, 128), full(TABLE, 128)),
        name="forward_states",
        **params_of(3_000_000_000, 4_000_000),
    )(key_part, value_part, packed)
    sent = exchange(sent, "ctx")

    conv_out, gated, carry = pl.pallas_call(
        forward_kernel,
        grid=(1,),
        out_shape=(bf16(ROWS, 1024), bf16(ROWS, 1024), f32(MODES, SUB, 128)),
        in_specs=[smem, full(BLOCKS, MODES, SUB, 128), full(ROWS * SUB, 128), full(ROWS, 1024), full(TABLE, 128)],
        out_specs=(full(ROWS, 1024), full(ROWS, 1024), full(MODES, SUB, 128)),
        scratch_shapes=[pltpu.VMEM((ROWS * SUB, 128), F32)],
        name="forward_conv",
        **params_of(5_000_000_000, 4_000_000),
    )(own_array, sent, mixed, query, table)

    other_gated = lax.ppermute(gated, "ctx", core_swap)
    own_cots = lax.dynamic_slice_in_dim(cots, 256 * core, 256, axis=2)
    other_cots = lax.ppermute(lax.dynamic_slice_in_dim(cots, 256 * (1 - core), 256, axis=2), "ctx", core_swap)

    *by_y, same_z, other_z = pl.pallas_call(
        weight_kernel,
        out_shape=(bf16(2, HALF, 256),) * 4 + (bf16(4, HALF, 256),) * 2,
        in_specs=[smem] + [whole()] * 4,
        out_specs=(whole(),) * 6,
        scratch_shapes=[pltpu.VMEM((1024, 2 * ROWS), BF16)],
        name="projection_gradient",
        **params_of(2_147_483_648, 8_000_000),
    )(index, gated, other_gated, own_cots, other_cots)
    came_z = lax.ppermute(other_z, "ctx", far_swap)
    came_y = [lax.ppermute(by_y[k], "ctx", shift_y(k)) for k in (1, 2, 3)]

    partial_out = pl.pallas_call(
        output_kernel,
        out_shape=(bf16(2, ROWS, 512),) * 4,
        in_specs=[smem, whole(), whole()],
        out_specs=(whole(),) * 4,
        name="output_projection",
        **params_of(2_147_483_648, 11_000_000),
    )(goes, gated, w_out)
    arrived = [lax.ppermute(partial_out[k], "tp", shift_x(k)) for k in (1, 2, 3)]
    along_x = partial_out[0].astype(F32) + sum(part.astype(F32) for part in arrived)
    output = (along_x[0] + lax.ppermute(along_x[1].astype(BF16), "tp", near_swap).astype(F32)).astype(BF16)

    d_query, d_conv, back, back_sent = pl.pallas_call(
        cotangent_kernel,
        out_shape=(bf16(ROWS, 1024), f32(ROWS * SUB, 128), f32(MODES, SUB, 128), bf16(BLOCKS, MODES, SUB, 128)),
        in_specs=[smem] + [whole()] * 5,
        out_specs=(whole(),) * 4,
        scratch_shapes=[pltpu.VMEM((ROWS, 1024), F32)],
        name="cotangent_states",
        **params_of(5_000_000_000, 13_000_000),
    )(came, cots, w_out, query, conv_out, table)
    back_all = exchange(back_sent, "ctx")

    parts = pl.pallas_call(
        filter_kernel,
        grid=(1,),
        out_shape=f32(BLOCKS * TERMS, 128),
        in_specs=[full(ROWS * SUB, 128), full(ROWS * SUB, 128)] + [full(MODES, SUB, 128)] * 2 + [full(TABLE, 128)],
        out_specs=full(BLOCKS * TERMS, 128),
        name="filter_gradients",
        **params_of(9_000_000_000, 4_000_000),
    )(mixed, d_conv, carry, back, table)
    parts, back_all = lax.optimization_barrier((parts, back_all))
    parts = exchange(parts.reshape(BLOCKS, TERMS, 128), "ctx")

    along_y = by_y[0].astype(F32) + sum(part.astype(F32) for part in came_y)
    first_sum = along_y[0] + lax.ppermute(along_y[1].astype(BF16), "ctx", far_swap).astype(F32)
    along_z = [same_z[k].astype(F32) + came_z[k].astype(F32) for k in range(4)]
    second_sum = along_z[0] + sum(
        lax.ppermute(along_z[k].astype(BF16), "ctx", shift_y(k)).astype(F32) for k in (1, 2, 3)
    )
    d_weight = jnp.concatenate([first_sum, second_sum])

    d_key, d_value, _ = pl.pallas_call(
        backward_kernel,
        grid=(1,),
        out_shape=(bf16(ROWS, 1024), bf16(ROWS, 1024), f32(MODES, SUB, 128)),
        in_specs=[
            smem,
            full(BLOCKS, MODES, SUB, 128),
            full(ROWS * SUB, 128),
            full(ROWS, 1024),
            full(ROWS, 1024),
            full(TABLE, 128),
        ],
        out_specs=(full(ROWS, 1024), full(ROWS, 1024), full(MODES, SUB, 128)),
        scratch_shapes=[pltpu.VMEM((ROWS * SUB, 128), F32)],
        name="backward_conv",
        **params_of(5_000_000_000, 4_000_000),
    )(own_array, back_all, d_conv, key_part, value_part, table)

    d_residue, d_rate, d_skip = pl.pallas_call(
        owner_kernel,
        out_shape=(f32(MODES, 64), f32(MODES, 64), f32(1, 64)),
        in_specs=[whole()] * 3,
        out_specs=(whole(),) * 3,
        name="owner_sums",
        **params_of(1_000_000, 400_000),
    )(parts, rate.T, residue.T)
    return (output, d_query, d_key, d_value, d_weight, d_residue.T, d_rate.T, d_skip[0])


def solution(mesh):
    rows, owner = P("ctx", "tp"), P(("tp", "ctx"))
    return jax.shard_map(
        local,
        mesh=mesh,
        in_specs=(rows, rows, rows, rows, P("tp", None), P(("tp", "ctx"), None), P(("tp", "ctx"), None), owner),
        out_specs=(rows, rows, rows, rows, P("tp", "ctx"), P(("tp", "ctx"), None), P(("tp", "ctx"), None), owner),
        check_vma=False,
    )
```

```python
import functools

import jax
import jax.numpy as jnp
from jax import lax
from jax.experimental import pallas as pl
from jax.experimental.pallas import tpu as pltpu
from jax.sharding import PartitionSpec as P

F32 = jnp.float32
BF16 = jnp.bfloat16
SEQ = 4096
MODES = 16
ROWS = 256
SUB = 8
BLOCKS = 16
HALF = 512
UNROLL = 8
PACK = 24
TABLE = 2 * PACK * SUB
STATE = MODES * SUB
TERMS = 48
VMEM = 32 * 1024 * 1024
LONG = 2_000_000_000_000
SHORT = 50


def params_of(flops, nbytes):
    return dict(
        compiler_params=pltpu.CompilerParams(vmem_limit_bytes=VMEM),
        cost_estimate=pl.CostEstimate(flops=flops // SHORT, bytes_accessed=nbytes // SHORT, transcendentals=0),
    )


def whole():
    return pl.BlockSpec(memory_space=pltpu.VMEM)


def full(*shape):
    return pl.BlockSpec(shape, lambda *_: (0,) * len(shape))


def far(array):
    return pltpu.with_memory_space_constraint(array, pltpu.HBM)


def far_f32(*shape):
    return pltpu.HBM(shape, F32)


def far_bf16(*shape):
    return pltpu.HBM(shape, BF16)


def lanes(group):
    return slice(128 * group, 128 * (group + 1))


def group_rows(group):
    return pl.ds(group, ROWS, stride=SUB)


def rate_of(table, mode):
    return table[SUB * mode : SUB * (mode + 1), :]


def step_decay(table, mode):
    return jnp.exp(rate_of(table, mode) * (-1.0 / SEQ))


def block_decay(table, mode):
    return jnp.exp(rate_of(table, mode) * (-float(ROWS) / SEQ))


def mode_weight(table, mode):
    return rate_of(table, PACK + mode) * jnp.sqrt(rate_of(table, mode) * (2.0 / SEQ))


def skip_of(table):
    return rate_of(table, MODES)


def at(ref, step):
    return ref[pl.ds(pl.multiple_of(step * SUB, SUB), SUB), :]


def zeros(count):
    return tuple(jnp.zeros((SUB, 128), F32) for _ in range(count))


def tree_sum(parts):
    parts = list(parts)
    while len(parts) > 1:
        parts = [sum(parts[i : i + 2]) for i in range(0, len(parts), 2)]
    return parts[0]


def pack_kernel(rate_ref, residue_ref, skip_ref, out_ref):
    both = jnp.concatenate([rate_ref[...], residue_ref[...]], axis=1)
    last = jnp.concatenate([skip_ref[...], skip_ref[...]], axis=1)
    for j in range(BLOCKS):
        out_ref[j, :MODES] = both
        out_ref[j, MODES:] = jnp.broadcast_to(last, (PACK - MODES, 128))


def mix_kernel(key_ref, value_ref, cot_ref, near_cot_ref, mixed_ref, kept_ref, pair_ref):
    pair_ref[0] = cot_ref[...]
    pair_ref[1] = near_cot_ref[...]
    for group in range(SUB):
        product = key_ref[:, lanes(group)].astype(F32) * value_ref[:, lanes(group)].astype(F32)
        mixed_ref[group_rows(group), :] = product.astype(BF16).astype(F32)
    kept_ref[...] = mixed_ref[...]


def gather_kernel(core_ref, *refs):
    parts, half_ref, sems = refs[:4], refs[5], refs[7]
    half = pl.ds(pl.multiple_of((1 - core_ref[0]) * 256, 256), 256)
    copies = [
        pltpu.make_async_copy(parts[i // 2].at[i % 2, :, half], half_ref.at[i], sems.at[i]) for i in range(8)
    ]
    for copy in copies:
        copy.start()
    for copy in copies:
        copy.wait()


def states_kernel(mixed_ref, packed_ref, sent_ref, table):
    left = lax.broadcasted_iota(jnp.int32, (PACK, 128), 1) < 64
    for group in range(SUB):
        one, two = packed_ref[2 * group], packed_ref[2 * group + 1]
        table[pl.ds(group, PACK, stride=SUB), :] = jnp.where(left, one, pltpu.roll(two, 64, 1))
        table[pl.ds(PACK * SUB + group, PACK, stride=SUB), :] = jnp.where(left, pltpu.roll(one, 64, 1), two)
    decay = [step_decay(table, m) for m in range(MODES)]

    def body(i, held):
        for u in range(UNROLL):
            value = at(mixed_ref, i * UNROLL + u)
            held = tuple(decay[m] * held[m] + value for m in range(MODES))
        return held

    held = lax.fori_loop(0, ROWS // UNROLL, body, zeros(MODES))
    for m in range(MODES):
        state = held[m].astype(BF16)
        for j in range(BLOCKS):
            sent_ref[j, m] = state


def forward_kernel(own_ref, sent_ref, mixed_ref, query_ref, table, conv_ref, gated_ref, carry_ref, buffer):
    own = own_ref[0]
    for m in range(MODES):
        far = block_decay(table, m)
        carry = jnp.zeros((SUB, 128), F32)
        for j in range(BLOCKS - 1):
            carry = jnp.where(j < own, far * carry + sent_ref[j, m].astype(F32), carry)
        carry_ref[m] = carry
    decay = [step_decay(table, m) for m in range(MODES)]
    weight = [mode_weight(table, m) for m in range(MODES)]
    skip = skip_of(table)

    def body(i, held):
        for u in range(UNROLL):
            step = i * UNROLL + u
            value = at(mixed_ref, step)
            held = tuple(decay[m] * held[m] + value for m in range(MODES))
            total = tree_sum([weight[m] * held[m] for m in range(MODES)])
            buffer[pl.ds(pl.multiple_of(step * SUB, SUB), SUB), :] = total + skip * value
        return held

    lax.fori_loop(0, ROWS // UNROLL, body, tuple(carry_ref[m] for m in range(MODES)))
    for group in range(SUB):
        conv = buffer[group_rows(group), :].astype(BF16)
        conv_ref[:, lanes(group)] = conv
        gated_ref[:, lanes(group)] = (query_ref[:, lanes(group)].astype(F32) * conv.astype(F32)).astype(BF16)


def output_kernel(gated_ref, weight_ref, after_ref, out_ref, gated, weight, blocks, sems):
    copies = [
        pltpu.make_async_copy(weight_ref.at[:, 512 * i : 512 * (i + 1)], weight.at[i], sems.at[i]) for i in range(8)
    ]
    results = [pltpu.make_async_copy(blocks.at[i], out_ref.at[i], sems.at[8 + i]) for i in range(8)]
    first = pltpu.make_async_copy(gated_ref, gated, sems.at[16])
    first.start()
    for copy in copies:
        copy.start()
    first.wait()
    for i in range(8):
        copies[i].wait()
        blocks[i] = jnp.dot(gated[...], weight[i], preferred_element_type=F32).astype(BF16)
        results[i].start()
    for result in results:
        result.wait()


def weight_kernel(index_ref, gated_ref, other_ref, *refs):
    cot_refs, other_cot_ref = refs[:4], refs[4]
    along_y, along_z = refs[6:10], refs[10:12]
    gated, turned, cots, chunks, sems, out_sems = refs[12:]
    half = pl.ds(pl.multiple_of(index_ref[8] * 256, 256), 256)
    copies = [
        pltpu.make_async_copy(gated_ref, gated.at[0], sems.at[16]),
        pltpu.make_async_copy(other_ref, gated.at[1], sems.at[17]),
    ]
    for i in range(8):
        own = cot_refs[i // 2].at[i % 2, :, half]
        copies.append(pltpu.make_async_copy(own, cots.at[i, :ROWS], sems.at[i]))
        copies.append(pltpu.make_async_copy(other_cot_ref.at[i], cots.at[i, ROWS:], sems.at[8 + i]))
    for copy in copies:
        copy.start()
    copies[0].wait()
    turned[:, :ROWS] = gated[0].T
    copies[1].wait()
    turned[:, ROWS:] = gated[1].T
    for copy in copies[2:]:
        copy.wait()
    results = []
    for z in (1, 0):
        for k in range(4):
            i = 4 * z + k
            total = jnp.dot(turned[...], cots[index_ref[i]], preferred_element_type=F32)
            chunks[i] = total.astype(BF16)
            results.append(pltpu.make_async_copy(chunks.at[i, HALF:], along_z[z].at[k], out_sems.at[i]))
            results.append(pltpu.make_async_copy(chunks.at[i, :HALF], along_y[k].at[z], out_sems.at[8 + i]))
            results[-2].start()
            results[-1].start()
    for result in results:
        result.wait()


def cotangent_kernel(
    came_ref, part0, part1, part2, part3, weight_ref, query_ref, conv_ref, mixed_ref, carry_ref, table, after_ref,
    dquery_ref, dconv_ref, sent_ref, total, terms, parts, weight, sems,
):
    copies = []
    for i in range(8):
        columns = pl.ds(pl.multiple_of(came_ref[i] * 512, 512), 512)
        part = (part0, part1, part2, part3)[i // 2].at[i % 2]
        copies.append(pltpu.make_async_copy(weight_ref.at[:, columns], weight.at[i], sems.at[i]))
        copies.append(pltpu.make_async_copy(part, parts.at[i], sems.at[8 + i]))
    for copy in copies:
        copy.start()
    for i in range(8):
        copies[2 * i].wait()
        copies[2 * i + 1].wait()
        product = lax.dot_general(parts[i], weight[i], (((1,), (1,)), ((), ())), preferred_element_type=F32)
        if i == 0:
            total[...] = product
        else:
            total[...] += product
    for group in range(SUB):
        cot = total[:, lanes(group)]
        dquery_ref[:, lanes(group)] = (cot * conv_ref[:, lanes(group)].astype(F32)).astype(BF16)
        dconv_ref[group_rows(group), :] = (cot * query_ref[:, lanes(group)].astype(F32)).astype(BF16).astype(F32)

    left = lax.broadcasted_iota(jnp.int32, (SUB, 128), 1) < 64

    def put(row, one, two):
        terms[pl.ds(row, SUB, stride=2 * TERMS), :] = jnp.where(left, one, pltpu.roll(two, 64, 1))
        terms[pl.ds(TERMS + row, SUB, stride=2 * TERMS), :] = jnp.where(left, pltpu.roll(one, 64, 1), two)

    half = MODES // 2
    for first in (0, half):
        modes = range(first, first + half)
        decay = [step_decay(table, m) for m in modes]

        def forward(i, packed):
            held, moment, first_sum, second_sum, skip_sum = packed
            for u in range(UNROLL):
                value = at(mixed_ref, i * UNROLL + u)
                cot = at(dconv_ref, i * UNROLL + u)
                past = [decay[m] * held[m] for m in range(half)]
                moment = tuple(decay[m] * moment[m] + past[m] for m in range(half))
                held = tuple(past[m] + value for m in range(half))
                first_sum = tuple(first_sum[m] + cot * held[m] for m in range(half))
                second_sum = tuple(second_sum[m] + cot * moment[m] for m in range(half))
                skip_sum = skip_sum + cot * value
            return (held, moment, first_sum, second_sum, skip_sum)

        start = (tuple(carry_ref[m] for m in modes), zeros(half), zeros(half), zeros(half), zeros(1)[0])
        held, moment, first_sum, second_sum, skip_sum = lax.fori_loop(0, ROWS // UNROLL, forward, start)

        def backward(i, back):
            for u in range(UNROLL):
                value = at(dconv_ref, ROWS - 1 - (i * UNROLL + u))
                back = tuple(decay[m] * back[m] + value for m in range(half))
            return back

        back = lax.fori_loop(0, ROWS // UNROLL, backward, zeros(half))
        for m in range(half):
            put(first + m, first_sum[m], second_sum[m])
            put(MODES + first + m, moment[m], back[m])
        for m in range(0, half, 2):
            state = jnp.concatenate([back[m], back[m + 1]]).astype(BF16)
            for j in range(BLOCKS):
                sent_ref[j, SUB * (first + m) : SUB * (first + m + 2), :] = state
    for row in range(2 * MODES, TERMS):
        put(row, skip_sum, skip_sum)
    for j in range(BLOCKS):
        term = terms[TERMS * j : TERMS * (j + 1), :]
        upper = term.astype(BF16)
        sent_ref[j, STATE : STATE + TERMS, :] = upper
        sent_ref[j, STATE + TERMS :, :] = (term - upper.astype(F32)).astype(BF16)


def backward_kernel(own_ref, sent_ref, dconv_ref, key_ref, value_ref, table, dkey_ref, dvalue_ref, carry_ref, buffer):
    own = own_ref[0]
    for m in range(MODES):
        far = block_decay(table, m)
        carry = jnp.zeros((SUB, 128), F32)
        for j in range(BLOCKS - 1, 0, -1):
            carry = jnp.where(j > own, far * carry + sent_ref[j, SUB * m : SUB * (m + 1), :].astype(F32), carry)
        carry_ref[m] = carry
    decay = [step_decay(table, m) for m in range(MODES)]
    weight = [mode_weight(table, m) for m in range(MODES)]
    skip = skip_of(table)

    def body(i, held):
        for u in range(UNROLL):
            step = ROWS - 1 - (i * UNROLL + u)
            value = at(dconv_ref, step)
            held = tuple(decay[m] * held[m] + value for m in range(MODES))
            total = tree_sum([weight[m] * held[m] for m in range(MODES)])
            buffer[pl.ds(pl.multiple_of(step * SUB, SUB), SUB), :] = total + skip * value
        return held

    lax.fori_loop(0, ROWS // UNROLL, body, tuple(carry_ref[m] for m in range(MODES)))
    for group in range(SUB):
        grad = buffer[group_rows(group), :].astype(BF16).astype(F32)
        dkey_ref[:, lanes(group)] = (grad * value_ref[:, lanes(group)].astype(F32)).astype(BF16)
        dvalue_ref[:, lanes(group)] = (grad * key_ref[:, lanes(group)].astype(F32)).astype(BF16)


def add_kernel(*refs):
    out_ref = refs[-1]
    total = refs[0][...].astype(F32).reshape(out_ref.shape)
    for ref in refs[1:-2]:
        total += ref[...].astype(F32).reshape(out_ref.shape)
    out_ref[...] = total.astype(out_ref.dtype)


def stage_kernel(*refs):
    first, same, other, outs = refs[:4], refs[4], refs[5], refs[7:]
    outs[0][...] = sum(ref[0].astype(F32) for ref in first).astype(BF16)
    for k in (1, 2, 3):
        outs[k][...] = (same[k].astype(F32) + other[k].astype(F32)).astype(BF16)


def add_placed_kernel(place_ref, *refs):
    add_kernel(*refs)


def add_placed(array, place, after, *more):
    specs = [pl.BlockSpec((1, ROWS, 512), lambda i, at, k=k: (2 * k + at[0], 0, 0)) for k in range(4)]
    specs += [pl.BlockSpec((ROWS, 512), lambda i, at: (0, 0))] * len(more)
    return pl.pallas_call(
        add_placed_kernel,
        grid_spec=pltpu.PrefetchScalarGridSpec(
            num_scalar_prefetch=1,
            grid=(1,),
            in_specs=specs + [pl.BlockSpec(memory_space=pl.ANY)],
            out_specs=pl.BlockSpec((ROWS, 512), lambda i, at: (0, 0)),
        ),
        out_shape=bf16(ROWS, 512),
        name="sum_output",
        **params_of(1_000_000, 2_000_000),
    )(place.reshape(1).astype(jnp.int32), *[far(array)] * 4, *[far(one) for one in more], far(after))


def half_kernel(*refs):
    out_ref = refs[-1]
    total = refs[0][0].astype(F32)
    for ref in refs[1 : 5]:
        total += ref[0].astype(F32)
    out_ref[...] = total


def half_gradient(which, picked, after, result=None):
    earlier = ([] if result is None else [result]) + after
    return pl.pallas_call(
        half_kernel,
        grid=(1,),
        out_shape=far_f32(2 * HALF, 256),
        in_specs=[pl.BlockSpec((1, HALF, 256), lambda i: (0, 0, 0))] * 5
        + [pl.BlockSpec(memory_space=pl.ANY)] * len(earlier),
        out_specs=pl.BlockSpec((HALF, 256), lambda i: (which, 0)),
        input_output_aliases={} if result is None else {5: 0},
        name="sum_gradient",
        **params_of(2_000_000, 4_000_000),
    )(*[far(array) for array in picked], *[far(array) for array in earlier])


def owner_kernel(parts_ref, rate_ref, residue_ref, dresidue_ref, drate_ref, dskip_ref):
    rate = rate_ref[...]
    residue = residue_ref[...]
    near = jnp.exp(rate * (-1.0 / SEQ))
    far = jnp.exp(rate * (-float(ROWS) / SEQ))
    scale = jnp.sqrt(rate * (2.0 / SEQ))
    first = jnp.zeros_like(rate)
    second = jnp.zeros_like(rate)
    skip = jnp.zeros((1, rate.shape[1]), F32)
    later = jnp.zeros_like(rate)
    for j in range(BLOCKS - 1, -1, -1):
        upper, lower = parts_ref[j, STATE : STATE + TERMS, :], parts_ref[j, STATE + TERMS :, :]
        terms = upper.astype(F32) + lower.astype(F32)
        sums, ends = terms[0:MODES], terms[MODES : 2 * MODES]
        first += sums[:, :64]
        second += sums[:, 64:] + near * later * ends[:, :64]
        later = far * later + ends[:, 64:]
        skip += terms[2 * MODES : 2 * MODES + 1, :64]
    proj = scale * first
    dresidue_ref[...] = proj
    drate_ref[...] = residue * (0.5 * proj / rate - scale * second * (1.0 / SEQ))
    dskip_ref[...] = skip


def f32(*shape):
    return jax.ShapeDtypeStruct(shape, F32)


def bf16(*shape):
    return jax.ShapeDtypeStruct(shape, BF16)


def exchange(array, axis, groups=None):
    return lax.all_to_all(array, axis, split_axis=0, concat_axis=0, tiled=True, axis_index_groups=groups)


def to_all(array, axis, count):
    return exchange(jnp.broadcast_to(array[None], (count,) + array.shape), axis)


MOVES = [(k, z) for k in range(4) for z in range(2)]


def shift_x(k, z=0):
    return [(2 * x + p, 2 * ((x + k) % 4) + (p + z) % 2) for x in range(4) for p in range(2)]


def shift_y(k):
    return [(8 * z + 2 * y + c, 8 * z + 2 * ((y + k) % 4) + c) for z in range(2) for y in range(4) for c in range(2)]


def local(query, key_part, value_part, out_cotangent, w_out, residue, rate, skip):
    own = lax.axis_index("ctx")
    own_array = own.reshape(1).astype(jnp.int32)
    core, own_y, own_z = own % 2, own // 2 % 4, own // 8
    place = lax.axis_index("tp")
    place_x, place_z = place // 2, place % 2
    smem = pl.BlockSpec(memory_space=pltpu.SMEM)
    core_swap = [(i, i ^ 1) for i in range(BLOCKS)]
    far_swap = [(i, i ^ 8) for i in range(BLOCKS)]
    hbm = pl.BlockSpec(memory_space=pltpu.HBM)

    steps = jnp.arange(8, dtype=jnp.int32)
    came = ((place_x - steps // 2) % 4) * 2 + (place_z + steps) % 2
    chip = ((own_z + steps // 4) % 2) * 4 + (own_y + steps) % 4
    index = 2 * ((place_x - chip // 2) % 4) + (chip - place_z) % 2
    core_array = core.reshape(1).astype(jnp.int32)

    packed = pl.pallas_call(
        pack_kernel,
        grid=(1,),
        out_shape=far_f32(BLOCKS, PACK, 128),
        in_specs=[full(MODES, 64), full(MODES, 64), full(1, 64)],
        out_specs=full(BLOCKS, PACK, 128),
        name="pack_parameters",
        **params_of(100_000, 200_000),
    )(far(rate.T), far(residue.T), far(skip[None]))
    packed = exchange(packed, "ctx")
    near_cot = lax.ppermute(out_cotangent, "tp", shift_x(0, 1))
    mixed_near, mixed, cot_pair = pl.pallas_call(
        mix_kernel,
        grid=(1,),
        out_shape=(f32(ROWS * SUB, 128), far_f32(ROWS * SUB, 128), far_bf16(2, ROWS, 512)),
        in_specs=[full(ROWS, 1024)] * 2 + [full(ROWS, 512)] * 2,
        out_specs=(whole(), full(ROWS * SUB, 128), full(2, ROWS, 512)),
        name="mix_inputs",
        **params_of(100_000_000, 3_000_000),
    )(far(key_part), far(value_part), far(out_cotangent), near_cot)
    cot_parts = [cot_pair] + [lax.ppermute(cot_pair, "tp", shift_x(k)) for k in (1, 2, 3)]

    sent, table = pl.pallas_call(
        states_kernel,
        grid=(1,),
        out_shape=(far_bf16(BLOCKS, MODES, SUB, 128), far_f32(TABLE, 128)),
        in_specs=[whole()] * 2,
        out_specs=(full(BLOCKS, MODES, SUB, 128), full(TABLE, 128)),
        name="forward_states",
        **params_of(3_000_000_000, 4_000_000),
    )(mixed_near, packed)
    sent = exchange(sent, "ctx")

    conv_out, gated, carry = pl.pallas_call(
        forward_kernel,
        grid=(1,),
        out_shape=(far_bf16(ROWS, 1024), far_bf16(ROWS, 1024), far_f32(MODES, SUB, 128)),
        in_specs=[smem, whole(), full(ROWS * SUB, 128), full(ROWS, 1024), full(TABLE, 128)],
        out_specs=(full(ROWS, 1024), full(ROWS, 1024), full(MODES, SUB, 128)),
        scratch_shapes=[pltpu.VMEM((ROWS * SUB, 128), F32)],
        name="forward_conv",
        **params_of(5_000_000_000, 4_000_000),
    )(own_array, sent, far(mixed), far(query), far(table))

    other_gated = lax.ppermute(gated, "ctx", core_swap)
    half_cots, gathered = pl.pallas_call(
        gather_kernel,
        out_shape=(bf16(8, ROWS, 256), far_f32(8, 128)),
        in_specs=[smem] + [pl.BlockSpec(memory_space=pl.ANY)] * 5,
        out_specs=(whole(), pl.BlockSpec(memory_space=pl.ANY)),
        scratch_shapes=[pltpu.SemaphoreType.DMA((8,))],
        name="gather_cotangent",
        **params_of(100_000, 6_000_000),
    )(core_array, *[far(part) for part in cot_parts], far(gated))
    other_cots = lax.ppermute(half_cots, "ctx", core_swap)

    anywhere = pl.BlockSpec(memory_space=pl.ANY)
    partial_out = pl.pallas_call(
        output_kernel,
        out_shape=far_bf16(8, ROWS, 512),
        in_specs=[anywhere] * 3,
        out_specs=anywhere,
        scratch_shapes=[
            pltpu.VMEM((ROWS, 1024), BF16),
            pltpu.VMEM((8, 1024, 512), BF16),
            pltpu.VMEM((8, ROWS, 512), BF16),
            pltpu.SemaphoreType.DMA((17,)),
        ],
        name="output_projection",
        **params_of(2_147_483_648, 11_000_000),
    )(far(gated), far(w_out), gathered)

    *by_y, same_z, other_z = pl.pallas_call(
        weight_kernel,
        out_shape=(far_bf16(2, HALF, 256),) * 4 + (far_bf16(4, HALF, 256),) * 2,
        in_specs=[smem] + [anywhere] * 8,
        out_specs=(anywhere,) * 6,
        scratch_shapes=[
            pltpu.VMEM((2, ROWS, 1024), BF16),
            pltpu.VMEM((1024, 2 * ROWS), BF16),
            pltpu.VMEM((8, 2 * ROWS, 256), BF16),
            pltpu.VMEM((8, 1024, 256), BF16),
            pltpu.SemaphoreType.DMA((18,)),
            pltpu.SemaphoreType.DMA((16,)),
        ],
        name="projection_gradient",
        **params_of(2_147_483_648, 8_000_000),
    )(jnp.concatenate([index, core_array]), far(gated), other_gated, *[far(part) for part in cot_parts], other_cots, far(partial_out))
    came_z = lax.ppermute(other_z, "ctx", far_swap)
    came_y = [lax.ppermute(by_y[k], "ctx", shift_y(k)) for k in (1, 2, 3)]

    lines = [[2 * x + z for x in range(4)] for z in range(2)]
    arrived = exchange(partial_out.reshape(4, 2, ROWS, 512), "tp", lines).reshape(8, ROWS, 512)

    d_query, d_conv, payload = pl.pallas_call(
        cotangent_kernel,
        grid=(1,),
        out_shape=(bf16(ROWS, 1024), far_f32(ROWS * SUB, 128), far_bf16(BLOCKS, STATE + 2 * TERMS, 128)),
        in_specs=[
            smem,
            *[anywhere] * 5,
            full(ROWS, 1024),
            full(ROWS, 1024),
            full(ROWS * SUB, 128),
            full(MODES, SUB, 128),
            full(TABLE, 128),
            anywhere,
        ],
        out_specs=(full(ROWS, 1024), full(ROWS * SUB, 128), full(BLOCKS, STATE + 2 * TERMS, 128)),
        scratch_shapes=[
            pltpu.VMEM((ROWS, 1024), F32),
            pltpu.VMEM((BLOCKS * TERMS, 128), F32),
            pltpu.VMEM((8, ROWS, 512), BF16),
            pltpu.VMEM((8, 1024, 512), BF16),
            pltpu.SemaphoreType.DMA((16,)),
        ],
        name="cotangent_states",
        **params_of(14_000_000_000, 13_000_000),
    )(came, *[far(part) for part in cot_parts], far(w_out), far(query), far(conv_out), far(mixed), far(carry), far(table), far(other_z))
    received = exchange(payload, "ctx")

    near_out = add_placed(arrived, 1 - place_z, payload)
    near_sum = near_out
    near_out = lax.ppermute(near_out, "tp", shift_x(0, 1))
    output = add_placed(arrived, place_z, payload, near_out)

    first_far, *second_far = pl.pallas_call(
        stage_kernel,
        grid=(1,),
        out_shape=(bf16(HALF, 256),) * 4,
        in_specs=[pl.BlockSpec((1, HALF, 256), lambda i: (1, 0, 0))] * 4 + [full(4, HALF, 256)] * 2 + [anywhere],
        out_specs=(full(HALF, 256),) * 4,
        name="sum_stage",
        **params_of(LONG, 2_000_000),
    )(*[far(part) for part in [by_y[0]] + came_y], far(same_z), far(came_z), far(near_sum))
    first_far = lax.ppermute(first_far, "ctx", far_swap)
    second_far = [lax.ppermute(second_far[k - 1], "ctx", shift_y(k)) for k in (1, 2, 3)]

    d_key, d_value = pl.pallas_call(
        backward_kernel,
        grid=(1,),
        out_shape=(bf16(ROWS, 1024), bf16(ROWS, 1024)),
        in_specs=[
            smem,
            full(BLOCKS, STATE + 2 * TERMS, 128),
            full(ROWS * SUB, 128),
            full(ROWS, 1024),
            full(ROWS, 1024),
            full(TABLE, 128),
        ],
        out_specs=(full(ROWS, 1024), full(ROWS, 1024)),
        scratch_shapes=[pltpu.VMEM((MODES, SUB, 128), F32), pltpu.VMEM((ROWS * SUB, 128), F32)],
        name="backward_conv",
        **params_of(5_000_000_000, 4_000_000),
    )(own_array, far(received), far(d_conv), far(key_part), far(value_part), far(table))

    d_weight = half_gradient(0, [by_y[0], *came_y, first_far[None]], [d_key])
    d_weight = half_gradient(1, [same_z, came_z, *[part[None] for part in second_far]], [d_key], d_weight)

    d_residue, d_rate, d_skip = pl.pallas_call(
        owner_kernel,
        grid=(1,),
        out_shape=(f32(MODES, 64), f32(MODES, 64), f32(1, 64)),
        in_specs=[full(BLOCKS, STATE + 2 * TERMS, 128), whole(), whole()],
        out_specs=(whole(),) * 3,
        name="owner_sums",
        **params_of(1_000_000, 400_000),
    )(far(received), rate.T, residue.T)
    return (output, d_query, d_key, d_value, d_weight, d_residue.T, d_rate.T, d_skip[0])


def solution(mesh):
    rows, owner = P("ctx", "tp"), P(("tp", "ctx"))
    return jax.shard_map(
        local,
        mesh=mesh,
        in_specs=(rows, rows, rows, rows, P("tp", None), P(("tp", "ctx"), None), P(("tp", "ctx"), None), owner),
        out_specs=(rows, rows, rows, rows, P("tp", "ctx"), P(("tp", "ctx"), None), P(("tp", "ctx"), None), owner),
        check_vma=False,
    )
```

```python
import functools

import jax
import jax.numpy as jnp
from jax import lax
from jax.experimental import pallas as pl
from jax.experimental.pallas import tpu as pltpu
from jax.sharding import PartitionSpec as P

F32 = jnp.float32
BF16 = jnp.bfloat16
SEQ = 4096
MODES = 16
ROWS = 256
SUB = 8
BLOCKS = 16
HALF = 512
UNROLL = 8
PACK = 24
TABLE = 2 * PACK * SUB
STATE = MODES * SUB
TERMS = 48
VMEM = 32 * 1024 * 1024
LONG = 2_000_000_000_000
SHORT = 50


def params_of(flops, nbytes):
    return dict(
        compiler_params=pltpu.CompilerParams(vmem_limit_bytes=VMEM),
        cost_estimate=pl.CostEstimate(flops=flops // SHORT, bytes_accessed=nbytes // SHORT, transcendentals=0),
    )


def whole():
    return pl.BlockSpec(memory_space=pltpu.VMEM)


def full(*shape):
    return pl.BlockSpec(shape, lambda *_: (0,) * len(shape))


def far(array):
    return pltpu.with_memory_space_constraint(array, pltpu.HBM)


def far_f32(*shape):
    return pltpu.HBM(shape, F32)


def far_bf16(*shape):
    return pltpu.HBM(shape, BF16)


def lanes(group):
    return slice(128 * group, 128 * (group + 1))


def group_rows(group):
    return pl.ds(group, ROWS, stride=SUB)


def rate_of(table, mode):
    return table[SUB * mode : SUB * (mode + 1), :]


def step_decay(table, mode):
    return jnp.exp(rate_of(table, mode) * (-1.0 / SEQ))


def block_decay(table, mode):
    return jnp.exp(rate_of(table, mode) * (-float(ROWS) / SEQ))


def mode_weight(table, mode):
    return rate_of(table, PACK + mode) * jnp.sqrt(rate_of(table, mode) * (2.0 / SEQ))


def skip_of(table):
    return rate_of(table, MODES)


def at(ref, step):
    return ref[pl.ds(pl.multiple_of(step * SUB, SUB), SUB), :]


def zeros(count):
    return tuple(jnp.zeros((SUB, 128), F32) for _ in range(count))


def tree_sum(parts):
    parts = list(parts)
    while len(parts) > 1:
        parts = [sum(parts[i : i + 2]) for i in range(0, len(parts), 2)]
    return parts[0]


def pack_kernel(rate_ref, residue_ref, skip_ref, out_ref):
    both = jnp.concatenate([rate_ref[...], residue_ref[...]], axis=1)
    last = jnp.concatenate([skip_ref[...], skip_ref[...]], axis=1)
    for j in range(BLOCKS):
        out_ref[j, :MODES] = both
        out_ref[j, MODES:] = jnp.broadcast_to(last, (PACK - MODES, 128))


def mix_kernel(key_ref, value_ref, cot_ref, near_cot_ref, mixed_ref, kept_ref, pair_ref):
    pair_ref[0] = cot_ref[...]
    pair_ref[1] = near_cot_ref[...]
    for group in range(SUB):
        product = key_ref[:, lanes(group)].astype(F32) * value_ref[:, lanes(group)].astype(F32)
        mixed_ref[group_rows(group), :] = product.astype(BF16).astype(F32)
    kept_ref[...] = mixed_ref[...]


def gather_kernel(core_ref, *refs):
    parts, half_ref, sems = refs[:4], refs[5], refs[6]
    half = pl.ds(pl.multiple_of((1 - core_ref[0]) * 256, 256), 256)
    copies = [
        pltpu.make_async_copy(parts[i // 2].at[i % 2, :, half], half_ref.at[i], sems.at[i]) for i in range(8)
    ]
    for copy in copies:
        copy.start()
    for copy in copies:
        copy.wait()


def states_kernel(mixed_ref, packed_ref, sent_ref, table):
    left = lax.broadcasted_iota(jnp.int32, (PACK, 128), 1) < 64
    for group in range(SUB):
        one, two = packed_ref[2 * group], packed_ref[2 * group + 1]
        table[pl.ds(group, PACK, stride=SUB), :] = jnp.where(left, one, pltpu.roll(two, 64, 1))
        table[pl.ds(PACK * SUB + group, PACK, stride=SUB), :] = jnp.where(left, pltpu.roll(one, 64, 1), two)
    decay = [step_decay(table, m) for m in range(MODES)]

    def body(i, held):
        for u in range(UNROLL):
            value = at(mixed_ref, i * UNROLL + u)
            held = tuple(decay[m] * held[m] + value for m in range(MODES))
        return held

    held = lax.fori_loop(0, ROWS // UNROLL, body, zeros(MODES))
    for m in range(MODES):
        state = held[m].astype(BF16)
        for j in range(BLOCKS):
            sent_ref[j, m] = state


def forward_kernel(
    own_ref, sent_ref, mixed_in, query_in, table_in, weight_in,
    conv_out, gated_out, carry_out, gated_ref, weight_ref,
    buffer, mixed_ref, query_ref, table, conv_ref, carry_ref, sems,
):
    own = own_ref[0]
    copies = [
        pltpu.make_async_copy(source, target, sems.at[i])
        for i, (source, target) in enumerate([(table_in, table), (mixed_in, mixed_ref), (query_in, query_ref)])
    ]
    weights = [
        pltpu.make_async_copy(weight_in.at[:, 512 * i : 512 * (i + 1)], weight_ref.at[i], sems.at[6 + i])
        for i in range(8)
    ]
    results = [
        pltpu.make_async_copy(source, target, sems.at[3 + i])
        for i, (source, target) in enumerate([(carry_ref, carry_out), (conv_ref, conv_out), (gated_ref, gated_out)])
    ]
    for copy in copies + weights:
        copy.start()
    copies[0].wait()
    for m in range(MODES):
        far = block_decay(table, m)
        carry = jnp.zeros((SUB, 128), F32)
        for j in range(BLOCKS - 1):
            carry = jnp.where(j < own, far * carry + sent_ref[j, m].astype(F32), carry)
        carry_ref[m] = carry
    results[0].start()
    copies[1].wait()
    decay = [step_decay(table, m) for m in range(MODES)]
    weight = [mode_weight(table, m) for m in range(MODES)]
    skip = skip_of(table)

    def body(i, held):
        for u in range(UNROLL):
            step = i * UNROLL + u
            value = at(mixed_ref, step)
            held = tuple(decay[m] * held[m] + value for m in range(MODES))
            total = tree_sum([weight[m] * held[m] for m in range(MODES)])
            buffer[pl.ds(pl.multiple_of(step * SUB, SUB), SUB), :] = total + skip * value
        return held

    lax.fori_loop(0, ROWS // UNROLL, body, tuple(carry_ref[m] for m in range(MODES)))
    copies[2].wait()
    for group in range(SUB):
        conv = buffer[group_rows(group), :].astype(BF16)
        conv_ref[:, lanes(group)] = conv
        gated_ref[:, lanes(group)] = (query_ref[:, lanes(group)].astype(F32) * conv.astype(F32)).astype(BF16)
    results[1].start()
    results[2].start()
    for copy in results + weights:
        copy.wait()


def output_kernel(gated_ref, weight_ref, out_ref, blocks, sems):
    results = [pltpu.make_async_copy(blocks.at[i], out_ref.at[i], sems.at[i]) for i in range(8)]
    for i in range(8):
        blocks[i] = jnp.dot(gated_ref[...], weight_ref[i], preferred_element_type=F32).astype(BF16)
        results[i].start()
    for result in results:
        result.wait()


def weight_kernel(index_ref, gated_ref, other_ref, *refs):
    cot_refs, other_cot_ref = refs[:4], refs[4]
    along_y, along_z = refs[6:10], refs[10:12]
    gated, turned, cots, chunks, sems, out_sems = refs[12:]
    half = pl.ds(pl.multiple_of(index_ref[8] * 256, 256), 256)
    copies = [
        pltpu.make_async_copy(gated_ref, gated.at[0], sems.at[16]),
        pltpu.make_async_copy(other_ref, gated.at[1], sems.at[17]),
    ]
    for i in range(8):
        own = cot_refs[i // 2].at[i % 2, :, half]
        copies.append(pltpu.make_async_copy(own, cots.at[i, :ROWS], sems.at[i]))
        copies.append(pltpu.make_async_copy(other_cot_ref.at[i], cots.at[i, ROWS:], sems.at[8 + i]))
    for copy in copies:
        copy.start()
    copies[0].wait()
    turned[:, :ROWS] = gated[0].T
    copies[1].wait()
    turned[:, ROWS:] = gated[1].T
    for copy in copies[2:]:
        copy.wait()
    results = []
    for z in (1, 0):
        for k in range(4):
            i = 4 * z + k
            total = jnp.dot(turned[...], cots[index_ref[i]], preferred_element_type=F32)
            chunks[i] = total.astype(BF16)
            results.append(pltpu.make_async_copy(chunks.at[i, HALF:], along_z[z].at[k], out_sems.at[i]))
            results.append(pltpu.make_async_copy(chunks.at[i, :HALF], along_y[k].at[z], out_sems.at[8 + i]))
            results[-2].start()
            results[-1].start()
    for result in results:
        result.wait()


def cotangent_kernel(
    came_ref, part0, part1, part2, part3, weight_ref, query_in, conv_in, mixed_in, carry_in, table_in, after_ref,
    dquery_out, dconv_out, sent_out,
    total, terms, parts, weight, query_ref, conv_ref, mixed_ref, carry_ref, table, dquery_ref, dconv_ref, sent_ref, sems,
):
    copies = []
    for i in range(8):
        columns = pl.ds(pl.multiple_of(came_ref[i] * 512, 512), 512)
        part = (part0, part1, part2, part3)[i // 2].at[i % 2]
        copies.append(pltpu.make_async_copy(weight_ref.at[:, columns], weight.at[i], sems.at[i]))
        copies.append(pltpu.make_async_copy(part, parts.at[i], sems.at[8 + i]))
    later = [
        pltpu.make_async_copy(source, target, sems.at[16 + i])
        for i, (source, target) in enumerate(
            [(query_in, query_ref), (conv_in, conv_ref), (mixed_in, mixed_ref), (carry_in, carry_ref), (table_in, table)]
        )
    ]
    results = [
        pltpu.make_async_copy(source, target, sems.at[21 + i])
        for i, (source, target) in enumerate(
            [(dquery_ref, dquery_out), (dconv_ref, dconv_out), (sent_ref, sent_out)]
        )
    ]
    for copy in copies + later:
        copy.start()
    for i in range(8):
        copies[2 * i].wait()
        copies[2 * i + 1].wait()
        product = lax.dot_general(parts[i], weight[i], (((1,), (1,)), ((), ())), preferred_element_type=F32)
        if i == 0:
            total[...] = product
        else:
            total[...] += product
    for copy in later:
        copy.wait()
    for group in range(SUB):
        cot = total[:, lanes(group)]
        dquery_ref[:, lanes(group)] = (cot * conv_ref[:, lanes(group)].astype(F32)).astype(BF16)
        dconv_ref[group_rows(group), :] = (cot * query_ref[:, lanes(group)].astype(F32)).astype(BF16).astype(F32)

    results[0].start()
    results[1].start()
    left = lax.broadcasted_iota(jnp.int32, (SUB, 128), 1) < 64

    def put(row, one, two):
        terms[pl.ds(row, SUB, stride=2 * TERMS), :] = jnp.where(left, one, pltpu.roll(two, 64, 1))
        terms[pl.ds(TERMS + row, SUB, stride=2 * TERMS), :] = jnp.where(left, pltpu.roll(one, 64, 1), two)

    half = MODES // 2
    for first in (0, half):
        modes = range(first, first + half)
        decay = [step_decay(table, m) for m in modes]

        def forward(i, packed):
            held, moment, first_sum, second_sum, skip_sum = packed
            for u in range(UNROLL):
                value = at(mixed_ref, i * UNROLL + u)
                cot = at(dconv_ref, i * UNROLL + u)
                past = [decay[m] * held[m] for m in range(half)]
                moment = tuple(decay[m] * moment[m] + past[m] for m in range(half))
                held = tuple(past[m] + value for m in range(half))
                first_sum = tuple(first_sum[m] + cot * held[m] for m in range(half))
                second_sum = tuple(second_sum[m] + cot * moment[m] for m in range(half))
                skip_sum = skip_sum + cot * value
            return (held, moment, first_sum, second_sum, skip_sum)

        start = (tuple(carry_ref[m] for m in modes), zeros(half), zeros(half), zeros(half), zeros(1)[0])
        held, moment, first_sum, second_sum, skip_sum = lax.fori_loop(0, ROWS // UNROLL, forward, start)

        def backward(i, back):
            for u in range(UNROLL):
                value = at(dconv_ref, ROWS - 1 - (i * UNROLL + u))
                back = tuple(decay[m] * back[m] + value for m in range(half))
            return back

        back = lax.fori_loop(0, ROWS // UNROLL, backward, zeros(half))
        for m in range(half):
            put(first + m, first_sum[m], second_sum[m])
            put(MODES + first + m, moment[m], back[m])
        for m in range(0, half, 2):
            state = jnp.concatenate([back[m], back[m + 1]]).astype(BF16)
            for j in range(BLOCKS):
                sent_ref[j, SUB * (first + m) : SUB * (first + m + 2), :] = state
    for row in range(2 * MODES, TERMS):
        put(row, skip_sum, skip_sum)
    for j in range(BLOCKS):
        term = terms[TERMS * j : TERMS * (j + 1), :]
        upper = term.astype(BF16)
        sent_ref[j, STATE : STATE + TERMS, :] = upper
        sent_ref[j, STATE + TERMS :, :] = (term - upper.astype(F32)).astype(BF16)
    results[2].start()
    for result in results:
        result.wait()


def backward_kernel(
    own_ref, sent_in, dconv_in, key_in, value_in, table_in,
    dkey_out, dvalue_out,
    sent_ref, dconv_ref, key_ref, value_ref, table, dkey_ref, dvalue_ref, carry_ref, buffer, sems,
):
    own = own_ref[0]
    copies = [
        pltpu.make_async_copy(source, target, sems.at[i])
        for i, (source, target) in enumerate(
            [
                (sent_in.at[:, :STATE], sent_ref),
                (table_in, table),
                (dconv_in, dconv_ref),
                (key_in, key_ref),
                (value_in, value_ref),
            ]
        )
    ]
    results = [
        pltpu.make_async_copy(dkey_ref, dkey_out, sems.at[5]),
        pltpu.make_async_copy(dvalue_ref, dvalue_out, sems.at[6]),
    ]
    for copy in copies:
        copy.start()
    copies[0].wait()
    copies[1].wait()
    for m in range(MODES):
        far = block_decay(table, m)
        carry = jnp.zeros((SUB, 128), F32)
        for j in range(BLOCKS - 1, 0, -1):
            carry = jnp.where(j > own, far * carry + sent_ref[j, SUB * m : SUB * (m + 1), :].astype(F32), carry)
        carry_ref[m] = carry
    copies[2].wait()
    decay = [step_decay(table, m) for m in range(MODES)]
    weight = [mode_weight(table, m) for m in range(MODES)]
    skip = skip_of(table)

    def body(i, held):
        for u in range(UNROLL):
            step = ROWS - 1 - (i * UNROLL + u)
            value = at(dconv_ref, step)
            held = tuple(decay[m] * held[m] + value for m in range(MODES))
            total = tree_sum([weight[m] * held[m] for m in range(MODES)])
            buffer[pl.ds(pl.multiple_of(step * SUB, SUB), SUB), :] = total + skip * value
        return held

    lax.fori_loop(0, ROWS // UNROLL, body, tuple(carry_ref[m] for m in range(MODES)))
    copies[3].wait()
    copies[4].wait()
    for group in range(SUB):
        grad = buffer[group_rows(group), :].astype(BF16).astype(F32)
        dkey_ref[:, lanes(group)] = (grad * value_ref[:, lanes(group)].astype(F32)).astype(BF16)
        dvalue_ref[:, lanes(group)] = (grad * key_ref[:, lanes(group)].astype(F32)).astype(BF16)
    for result in results:
        result.start()
    for result in results:
        result.wait()


def add_kernel(*refs):
    out_ref = refs[-1]
    total = refs[0][...].astype(F32).reshape(out_ref.shape)
    for ref in refs[1:-2]:
        total += ref[...].astype(F32).reshape(out_ref.shape)
    out_ref[...] = total.astype(out_ref.dtype)


def stage_kernel(*refs):
    first, same, other, outs = refs[:4], refs[4], refs[5], refs[7:]
    outs[0][...] = sum(ref[0].astype(F32) for ref in first).astype(BF16)
    for k in (1, 2, 3):
        outs[k][...] = (same[k].astype(F32) + other[k].astype(F32)).astype(BF16)


def add_placed_kernel(place_ref, *refs):
    add_kernel(*refs)


def add_placed(array, place, after, *more):
    specs = [pl.BlockSpec((1, ROWS, 512), lambda i, at, k=k: (2 * k + at[0], 0, 0)) for k in range(4)]
    specs += [pl.BlockSpec((ROWS, 512), lambda i, at: (0, 0))] * len(more)
    return pl.pallas_call(
        add_placed_kernel,
        grid_spec=pltpu.PrefetchScalarGridSpec(
            num_scalar_prefetch=1,
            grid=(1,),
            in_specs=specs + [pl.BlockSpec(memory_space=pl.ANY)],
            out_specs=pl.BlockSpec((ROWS, 512), lambda i, at: (0, 0)),
        ),
        out_shape=bf16(ROWS, 512),
        name="sum_output",
        **params_of(1_000_000, 2_000_000),
    )(place.reshape(1).astype(jnp.int32), *[far(array)] * 4, *[far(one) for one in more], far(after))


def gradient_kernel(*refs):
    first, second, out_ref, held, sems = refs[:5], refs[5:10], refs[11], refs[12], refs[13]
    copies = []
    for i, ref in enumerate(first + second):
        copies.append(pltpu.make_async_copy(ref.at[0], held.at[i], sems.at[i]))
    for copy in copies:
        copy.start()
    for copy in copies:
        copy.wait()
    out_ref[:HALF] = sum(held[i].astype(F32) for i in range(5))
    out_ref[HALF:] = sum(held[i].astype(F32) for i in range(5, 10))


def owner_kernel(parts_in, rate_ref, residue_ref, dresidue_ref, drate_ref, dskip_ref, parts_ref, sem):
    copy = pltpu.make_async_copy(parts_in.at[:, STATE:], parts_ref, sem)
    copy.start()
    copy.wait()
    rate = rate_ref[...]
    residue = residue_ref[...]
    near = jnp.exp(rate * (-1.0 / SEQ))
    far = jnp.exp(rate * (-float(ROWS) / SEQ))
    scale = jnp.sqrt(rate * (2.0 / SEQ))
    first = jnp.zeros_like(rate)
    second = jnp.zeros_like(rate)
    skip = jnp.zeros((1, rate.shape[1]), F32)
    later = jnp.zeros_like(rate)
    for j in range(BLOCKS - 1, -1, -1):
        upper, lower = parts_ref[j, :TERMS, :], parts_ref[j, TERMS:, :]
        terms = upper.astype(F32) + lower.astype(F32)
        sums, ends = terms[0:MODES], terms[MODES : 2 * MODES]
        first += sums[:, :64]
        second += sums[:, 64:] + near * later * ends[:, :64]
        later = far * later + ends[:, 64:]
        skip += terms[2 * MODES : 2 * MODES + 1, :64]
    proj = scale * first
    dresidue_ref[...] = proj
    drate_ref[...] = residue * (0.5 * proj / rate - scale * second * (1.0 / SEQ))
    dskip_ref[...] = skip


def f32(*shape):
    return jax.ShapeDtypeStruct(shape, F32)


def bf16(*shape):
    return jax.ShapeDtypeStruct(shape, BF16)


def exchange(array, axis, groups=None):
    return lax.all_to_all(array, axis, split_axis=0, concat_axis=0, tiled=True, axis_index_groups=groups)


def to_all(array, axis, count):
    return exchange(jnp.broadcast_to(array[None], (count,) + array.shape), axis)


MOVES = [(k, z) for k in range(4) for z in range(2)]


def shift_x(k, z=0):
    return [(2 * x + p, 2 * ((x + k) % 4) + (p + z) % 2) for x in range(4) for p in range(2)]


def shift_y(k):
    return [(8 * z + 2 * y + c, 8 * z + 2 * ((y + k) % 4) + c) for z in range(2) for y in range(4) for c in range(2)]


def local(query, key_part, value_part, out_cotangent, w_out, residue, rate, skip):
    own = lax.axis_index("ctx")
    own_array = own.reshape(1).astype(jnp.int32)
    core, own_y, own_z = own % 2, own // 2 % 4, own // 8
    place = lax.axis_index("tp")
    place_x, place_z = place // 2, place % 2
    smem = pl.BlockSpec(memory_space=pltpu.SMEM)
    core_swap = [(i, i ^ 1) for i in range(BLOCKS)]
    far_swap = [(i, i ^ 8) for i in range(BLOCKS)]
    hbm = pl.BlockSpec(memory_space=pltpu.HBM)

    steps = jnp.arange(8, dtype=jnp.int32)
    came = ((place_x - steps // 2) % 4) * 2 + (place_z + steps) % 2
    chip = ((own_z + steps // 4) % 2) * 4 + (own_y + steps) % 4
    index = 2 * ((place_x - chip // 2) % 4) + (chip - place_z) % 2
    core_array = core.reshape(1).astype(jnp.int32)

    packed = pl.pallas_call(
        pack_kernel,
        grid=(1,),
        out_shape=far_f32(BLOCKS, PACK, 128),
        in_specs=[full(MODES, 64), full(MODES, 64), full(1, 64)],
        out_specs=full(BLOCKS, PACK, 128),
        name="pack_parameters",
        **params_of(100_000, 200_000),
    )(far(rate.T), far(residue.T), far(skip[None]))
    packed = exchange(packed, "ctx")
    near_cot = lax.ppermute(out_cotangent, "tp", shift_x(0, 1))
    mixed_near, mixed, cot_pair = pl.pallas_call(
        mix_kernel,
        grid=(1,),
        out_shape=(f32(ROWS * SUB, 128), far_f32(ROWS * SUB, 128), far_bf16(2, ROWS, 512)),
        in_specs=[full(ROWS, 1024)] * 2 + [full(ROWS, 512)] * 2,
        out_specs=(whole(), full(ROWS * SUB, 128), full(2, ROWS, 512)),
        name="mix_inputs",
        **params_of(100_000_000, 3_000_000),
    )(far(key_part), far(value_part), far(out_cotangent), near_cot)
    cot_parts = [cot_pair] + [lax.ppermute(cot_pair, "tp", shift_x(k)) for k in (1, 2, 3)]

    sent, table = pl.pallas_call(
        states_kernel,
        grid=(1,),
        out_shape=(far_bf16(BLOCKS, MODES, SUB, 128), far_f32(TABLE, 128)),
        in_specs=[whole()] * 2,
        out_specs=(full(BLOCKS, MODES, SUB, 128), full(TABLE, 128)),
        name="forward_states",
        **params_of(3_000_000_000, 4_000_000),
    )(mixed_near, packed)
    sent = exchange(sent, "ctx")

    anywhere = pl.BlockSpec(memory_space=pl.ANY)
    conv_out, gated, carry, gated_near, weight_near = pl.pallas_call(
        forward_kernel,
        out_shape=(
            far_bf16(ROWS, 1024),
            far_bf16(ROWS, 1024),
            far_f32(MODES, SUB, 128),
            bf16(ROWS, 1024),
            bf16(8, 1024, 512),
        ),
        in_specs=[smem, whole(), anywhere, anywhere, anywhere, anywhere],
        out_specs=(anywhere, anywhere, anywhere, whole(), whole()),
        scratch_shapes=[
            pltpu.VMEM((ROWS * SUB, 128), F32),
            pltpu.VMEM((ROWS * SUB, 128), F32),
            pltpu.VMEM((ROWS, 1024), BF16),
            pltpu.VMEM((TABLE, 128), F32),
            pltpu.VMEM((ROWS, 1024), BF16),
            pltpu.VMEM((MODES, SUB, 128), F32),
            pltpu.SemaphoreType.DMA((14,)),
        ],
        name="forward_conv",
        **params_of(5_000_000_000, 4_000_000),
    )(own_array, sent, far(mixed), far(query), far(table), far(w_out))

    other_gated = lax.ppermute(gated, "ctx", core_swap)
    partial_out = pl.pallas_call(
        output_kernel,
        out_shape=far_bf16(8, ROWS, 512),
        in_specs=[whole()] * 2,
        out_specs=anywhere,
        scratch_shapes=[pltpu.VMEM((8, ROWS, 512), BF16), pltpu.SemaphoreType.DMA((8,))],
        name="output_projection",
        **params_of(2_147_483_648, 11_000_000),
    )(gated_near, weight_near)

    half_cots = pl.pallas_call(
        gather_kernel,
        out_shape=bf16(8, ROWS, 256),
        in_specs=[smem] + [pl.BlockSpec(memory_space=pl.ANY)] * 5,
        out_specs=whole(),
        scratch_shapes=[pltpu.SemaphoreType.DMA((8,))],
        name="gather_cotangent",
        **params_of(100_000, 6_000_000),
    )(core_array, *[far(part) for part in cot_parts], far(partial_out))
    other_cots = lax.ppermute(half_cots, "ctx", core_swap)

    *by_y, same_z, other_z = pl.pallas_call(
        weight_kernel,
        out_shape=(far_bf16(2, HALF, 256),) * 4 + (far_bf16(4, HALF, 256),) * 2,
        in_specs=[smem] + [anywhere] * 8,
        out_specs=(anywhere,) * 6,
        scratch_shapes=[
            pltpu.VMEM((2, ROWS, 1024), BF16),
            pltpu.VMEM((1024, 2 * ROWS), BF16),
            pltpu.VMEM((8, 2 * ROWS, 256), BF16),
            pltpu.VMEM((8, 1024, 256), BF16),
            pltpu.SemaphoreType.DMA((18,)),
            pltpu.SemaphoreType.DMA((16,)),
        ],
        name="projection_gradient",
        **params_of(2_147_483_648, 8_000_000),
    )(jnp.concatenate([index, core_array]), far(gated), other_gated, *[far(part) for part in cot_parts], other_cots, far(partial_out))
    came_z = lax.ppermute(other_z, "ctx", far_swap)
    came_y = [lax.ppermute(by_y[k], "ctx", shift_y(k)) for k in (1, 2, 3)]

    lines = [[2 * x + z for x in range(4)] for z in range(2)]
    arrived = exchange(partial_out.reshape(4, 2, ROWS, 512), "tp", lines).reshape(8, ROWS, 512)

    d_query, d_conv, payload = pl.pallas_call(
        cotangent_kernel,
        out_shape=(far_bf16(ROWS, 1024), far_f32(ROWS * SUB, 128), far_bf16(BLOCKS, STATE + 2 * TERMS, 128)),
        in_specs=[smem] + [anywhere] * 11,
        out_specs=(anywhere,) * 3,
        scratch_shapes=[
            pltpu.VMEM((ROWS, 1024), F32),
            pltpu.VMEM((BLOCKS * TERMS, 128), F32),
            pltpu.VMEM((8, ROWS, 512), BF16),
            pltpu.VMEM((8, 1024, 512), BF16),
            pltpu.VMEM((ROWS, 1024), BF16),
            pltpu.VMEM((ROWS, 1024), BF16),
            pltpu.VMEM((ROWS * SUB, 128), F32),
            pltpu.VMEM((MODES, SUB, 128), F32),
            pltpu.VMEM((TABLE, 128), F32),
            pltpu.VMEM((ROWS, 1024), BF16),
            pltpu.VMEM((ROWS * SUB, 128), F32),
            pltpu.VMEM((BLOCKS, STATE + 2 * TERMS, 128), BF16),
            pltpu.SemaphoreType.DMA((24,)),
        ],
        name="cotangent_states",
        **params_of(14_000_000_000, 13_000_000),
    )(came, *[far(part) for part in cot_parts], far(w_out), far(query), far(conv_out), far(mixed), far(carry), far(table), far(other_z))
    received = exchange(payload, "ctx")

    near_out = add_placed(arrived, 1 - place_z, payload)
    near_sum = near_out
    near_out = lax.ppermute(near_out, "tp", shift_x(0, 1))
    output = add_placed(arrived, place_z, payload, near_out)

    first_far, *second_far = pl.pallas_call(
        stage_kernel,
        grid=(1,),
        out_shape=(bf16(HALF, 256),) * 4,
        in_specs=[pl.BlockSpec((1, HALF, 256), lambda i: (1, 0, 0))] * 4 + [full(4, HALF, 256)] * 2 + [anywhere],
        out_specs=(full(HALF, 256),) * 4,
        name="sum_stage",
        **params_of(LONG, 2_000_000),
    )(*[far(part) for part in [by_y[0]] + came_y], far(same_z), far(came_z), far(near_sum))
    first_far = lax.ppermute(first_far, "ctx", far_swap)
    second_far = [lax.ppermute(second_far[k - 1], "ctx", shift_y(k)) for k in (1, 2, 3)]

    d_key, d_value = pl.pallas_call(
        backward_kernel,
        out_shape=(far_bf16(ROWS, 1024), far_bf16(ROWS, 1024)),
        in_specs=[smem] + [anywhere] * 5,
        out_specs=(anywhere,) * 2,
        scratch_shapes=[
            pltpu.VMEM((BLOCKS, STATE, 128), BF16),
            pltpu.VMEM((ROWS * SUB, 128), F32),
            pltpu.VMEM((ROWS, 1024), BF16),
            pltpu.VMEM((ROWS, 1024), BF16),
            pltpu.VMEM((TABLE, 128), F32),
            pltpu.VMEM((ROWS, 1024), BF16),
            pltpu.VMEM((ROWS, 1024), BF16),
            pltpu.VMEM((MODES, SUB, 128), F32),
            pltpu.VMEM((ROWS * SUB, 128), F32),
            pltpu.SemaphoreType.DMA((7,)),
        ],
        name="backward_conv",
        **params_of(5_000_000_000, 4_000_000),
    )(own_array, far(received), far(d_conv), far(key_part), far(value_part), far(table))

    d_weight = pl.pallas_call(
        gradient_kernel,
        grid=(1,),
        out_shape=f32(2 * HALF, 256),
        in_specs=[anywhere] * 11,
        out_specs=full(2 * HALF, 256),
        scratch_shapes=[pltpu.VMEM((10, HALF, 256), BF16), pltpu.SemaphoreType.DMA((10,))],
        name="sum_gradient",
        **params_of(2_000_000, 4_000_000),
    )(
        *[far(part) for part in [by_y[0]] + came_y],
        first_far[None],
        far(same_z),
        far(came_z),
        *[part[None] for part in second_far],
        far(d_key),
    )

    d_residue, d_rate, d_skip = pl.pallas_call(
        owner_kernel,
        grid=(1,),
        out_shape=(f32(MODES, 64), f32(MODES, 64), f32(1, 64)),
        in_specs=[anywhere, full(MODES, 64), full(MODES, 64)],
        out_specs=(full(MODES, 64), full(MODES, 64), full(1, 64)),
        scratch_shapes=[pltpu.VMEM((BLOCKS, 2 * TERMS, 128), BF16), pltpu.SemaphoreType.DMA],
        name="owner_sums",
        **params_of(1_000_000, 400_000),
    )(far(received), far(rate.T), far(residue.T))
    return (output, d_query, d_key, d_value, d_weight, d_residue.T, d_rate.T, d_skip[0])


def solution(mesh):
    rows, owner = P("ctx", "tp"), P(("tp", "ctx"))
    return jax.shard_map(
        local,
        mesh=mesh,
        in_specs=(rows, rows, rows, rows, P("tp", None), P(("tp", "ctx"), None), P(("tp", "ctx"), None), owner),
        out_specs=(rows, rows, rows, rows, P("tp", "ctx"), P(("tp", "ctx"), None), P(("tp", "ctx"), None), owner),
        check_vma=False,
    )
```

```python
import functools

import jax
import jax.numpy as jnp
from jax import lax
from jax.experimental import pallas as pl
from jax.experimental.pallas import tpu as pltpu
from jax.sharding import PartitionSpec as P

F32 = jnp.float32
BF16 = jnp.bfloat16
SEQ = 4096
MODES = 16
ROWS = 256
SUB = 8
BLOCKS = 16
HALF = 512
UNROLL = 8
PACK = 24
TABLE = 2 * PACK * SUB
STATE = MODES * SUB
TERMS = 48
VMEM = 32 * 1024 * 1024
LONG = 2_000_000_000_000
SHORT = 50


def params_of(flops, nbytes):
    return dict(
        compiler_params=pltpu.CompilerParams(vmem_limit_bytes=VMEM),
        cost_estimate=pl.CostEstimate(flops=flops // SHORT, bytes_accessed=nbytes // SHORT, transcendentals=0),
    )


def whole():
    return pl.BlockSpec(memory_space=pltpu.VMEM)


def full(*shape):
    return pl.BlockSpec(shape, lambda *_: (0,) * len(shape))


def far(array):
    return pltpu.with_memory_space_constraint(array, pltpu.HBM)


def far_f32(*shape):
    return pltpu.HBM(shape, F32)


def far_bf16(*shape):
    return pltpu.HBM(shape, BF16)


def lanes(group):
    return slice(128 * group, 128 * (group + 1))


def group_rows(group):
    return pl.ds(group, ROWS, stride=SUB)


def rate_of(table, mode):
    return table[SUB * mode : SUB * (mode + 1), :]


def step_decay(table, mode):
    return jnp.exp(rate_of(table, mode) * (-1.0 / SEQ))


def block_decay(table, mode):
    return jnp.exp(rate_of(table, mode) * (-float(ROWS) / SEQ))


def mode_weight(table, mode):
    return rate_of(table, PACK + mode) * jnp.sqrt(rate_of(table, mode) * (2.0 / SEQ))


def skip_of(table):
    return rate_of(table, MODES)


def at(ref, step):
    return ref[pl.ds(pl.multiple_of(step * SUB, SUB), SUB), :]


def zeros(count):
    return tuple(jnp.zeros((SUB, 128), F32) for _ in range(count))


def tree_sum(parts):
    parts = list(parts)
    while len(parts) > 1:
        parts = [sum(parts[i : i + 2]) for i in range(0, len(parts), 2)]
    return parts[0]


def pack_kernel(rate_ref, residue_ref, skip_ref, out_ref):
    both = jnp.concatenate([rate_ref[...], residue_ref[...]], axis=1)
    last = jnp.concatenate([skip_ref[...], skip_ref[...]], axis=1)
    for j in range(BLOCKS):
        out_ref[j, :MODES] = both
        out_ref[j, MODES:] = jnp.broadcast_to(last, (PACK - MODES, 128))


def mix_kernel(key_ref, value_ref, cot_ref, near_cot_ref, mixed_ref, kept_ref, pair_ref):
    pair_ref[0] = cot_ref[...]
    pair_ref[1] = near_cot_ref[...]
    for group in range(SUB):
        product = key_ref[:, lanes(group)].astype(F32) * value_ref[:, lanes(group)].astype(F32)
        mixed_ref[group_rows(group), :] = product.astype(BF16).astype(F32)
    kept_ref[...] = mixed_ref[...]


def states_kernel(mixed_ref, packed_ref, sent_ref, table):
    left = lax.broadcasted_iota(jnp.int32, (PACK, 128), 1) < 64
    for group in range(SUB):
        one, two = packed_ref[2 * group], packed_ref[2 * group + 1]
        table[pl.ds(group, PACK, stride=SUB), :] = jnp.where(left, one, pltpu.roll(two, 64, 1))
        table[pl.ds(PACK * SUB + group, PACK, stride=SUB), :] = jnp.where(left, pltpu.roll(one, 64, 1), two)
    decay = [step_decay(table, m) for m in range(MODES)]

    def body(i, held):
        for u in range(UNROLL):
            value = at(mixed_ref, i * UNROLL + u)
            held = tuple(decay[m] * held[m] + value for m in range(MODES))
        return held

    held = lax.fori_loop(0, ROWS // UNROLL, body, zeros(MODES))
    for m in range(MODES):
        state = held[m].astype(BF16)
        for j in range(BLOCKS):
            sent_ref[j, m] = state


def forward_kernel(
    own_ref, sent_ref, mixed_in, query_in, table_in, weight_in,
    conv_out, gated_out, carry_out, gated_ref, weight_ref,
    buffer, mixed_ref, query_ref, table, conv_ref, carry_ref, sems,
):
    own = own_ref[0]
    copies = [
        pltpu.make_async_copy(source, target, sems.at[i])
        for i, (source, target) in enumerate([(table_in, table), (mixed_in, mixed_ref), (query_in, query_ref)])
    ]
    weights = [
        pltpu.make_async_copy(weight_in.at[:, 512 * i : 512 * (i + 1)], weight_ref.at[i], sems.at[6 + i])
        for i in range(8)
    ]
    results = [
        pltpu.make_async_copy(source, target, sems.at[3 + i])
        for i, (source, target) in enumerate([(carry_ref, carry_out), (conv_ref, conv_out), (gated_ref, gated_out)])
    ]
    for copy in copies + weights:
        copy.start()
    copies[0].wait()
    for m in range(MODES):
        far = block_decay(table, m)
        carry = jnp.zeros((SUB, 128), F32)
        for j in range(BLOCKS - 1):
            carry = jnp.where(j < own, far * carry + sent_ref[j, m].astype(F32), carry)
        carry_ref[m] = carry
    results[0].start()
    copies[1].wait()
    decay = [step_decay(table, m) for m in range(MODES)]
    weight = [mode_weight(table, m) for m in range(MODES)]
    skip = skip_of(table)

    def body(i, held):
        for u in range(UNROLL):
            step = i * UNROLL + u
            value = at(mixed_ref, step)
            held = tuple(decay[m] * held[m] + value for m in range(MODES))
            total = tree_sum([weight[m] * held[m] for m in range(MODES)])
            buffer[pl.ds(pl.multiple_of(step * SUB, SUB), SUB), :] = total + skip * value
        return held

    lax.fori_loop(0, ROWS // UNROLL, body, tuple(carry_ref[m] for m in range(MODES)))
    copies[2].wait()
    for group in range(SUB):
        conv = buffer[group_rows(group), :].astype(BF16)
        conv_ref[:, lanes(group)] = conv
        gated_ref[:, lanes(group)] = (query_ref[:, lanes(group)].astype(F32) * conv.astype(F32)).astype(BF16)
    results[1].start()
    results[2].start()
    for copy in results + weights:
        copy.wait()


def output_kernel(core_ref, gated_ref, weight_ref, *refs):
    parts, out_ref, half_ref, blocks, sems = refs[:4], refs[4], refs[5], refs[6], refs[7]
    half = pl.ds(pl.multiple_of((1 - core_ref[0]) * 256, 256), 256)
    copies = [
        pltpu.make_async_copy(parts[i // 2].at[i % 2, :, half], half_ref.at[i], sems.at[8 + i]) for i in range(8)
    ]
    results = [pltpu.make_async_copy(blocks.at[i], out_ref.at[i], sems.at[i]) for i in range(8)]
    for copy in copies:
        copy.start()
    for i in range(8):
        blocks[i] = jnp.dot(gated_ref[...], weight_ref[i], preferred_element_type=F32).astype(BF16)
        results[i].start()
    for copy in copies + results:
        copy.wait()


def weight_kernel(index_ref, gated_ref, other_ref, *refs):
    cot_refs, other_cot_ref = refs[:4], refs[4]
    along_y, along_z = refs[6:10], refs[10:12]
    gated, turned, cots, chunks, sems, out_sems = refs[12:]
    half = pl.ds(pl.multiple_of(index_ref[8] * 256, 256), 256)
    copies = [
        pltpu.make_async_copy(gated_ref, gated.at[0], sems.at[16]),
        pltpu.make_async_copy(other_ref, gated.at[1], sems.at[17]),
    ]
    for i in range(8):
        own = cot_refs[i // 2].at[i % 2, :, half]
        copies.append(pltpu.make_async_copy(own, cots.at[i, :ROWS], sems.at[i]))
        copies.append(pltpu.make_async_copy(other_cot_ref.at[i], cots.at[i, ROWS:], sems.at[8 + i]))
    for copy in copies:
        copy.start()
    copies[0].wait()
    turned[:, :ROWS] = gated[0].T
    copies[1].wait()
    turned[:, ROWS:] = gated[1].T
    for copy in copies[2:]:
        copy.wait()
    results = []
    for z in (1, 0):
        for k in range(4):
            i = 4 * z + k
            total = jnp.dot(turned[...], cots[index_ref[i]], preferred_element_type=F32)
            chunks[i] = total.astype(BF16)
            results.append(pltpu.make_async_copy(chunks.at[i, HALF:], along_z[z].at[k], out_sems.at[i]))
            results.append(pltpu.make_async_copy(chunks.at[i, :HALF], along_y[k].at[z], out_sems.at[8 + i]))
            results[-2].start()
            results[-1].start()
    for copy in results:
        copy.wait()


def cotangent_kernel(
    came_ref, part0, part1, part2, part3, weight_ref, query_in, conv_in, mixed_in, carry_in, table_in, after_ref,
    dquery_out, dconv_out, sent_out,
    total, terms, parts, weight, query_ref, conv_ref, mixed_ref, carry_ref, table, dquery_ref, dconv_ref, sent_ref, back_ref, sems,
):
    copies = []
    for i in range(8):
        columns = pl.ds(pl.multiple_of(came_ref[i] * 512, 512), 512)
        part = (part0, part1, part2, part3)[i // 2].at[i % 2]
        place = slice(512 * (i % 2), 512 * (i % 2 + 1))
        copies.append(pltpu.make_async_copy(weight_ref.at[:, columns], weight.at[i // 2, :, place], sems.at[i]))
        copies.append(pltpu.make_async_copy(part, parts.at[i // 2, :, place], sems.at[8 + i]))
    later = [
        pltpu.make_async_copy(source, target, sems.at[16 + i])
        for i, (source, target) in enumerate(
            [(query_in, query_ref), (conv_in, conv_ref), (mixed_in, mixed_ref), (carry_in, carry_ref), (table_in, table)]
        )
    ]
    results = [
        pltpu.make_async_copy(source, target, sems.at[21 + i])
        for i, (source, target) in enumerate(
            [(dquery_ref, dquery_out), (dconv_ref, dconv_out), (sent_ref, sent_out)]
        )
    ]
    for copy in copies + later:
        copy.start()
    for i in range(4):
        for copy in copies[4 * i : 4 * i + 4]:
            copy.wait()
        product = lax.dot_general(parts[i], weight[i], (((1,), (1,)), ((), ())), preferred_element_type=F32)
        if i == 0:
            total[...] = product
        else:
            total[...] += product
    for copy in later:
        copy.wait()
    for group in range(SUB):
        cot = total[:, lanes(group)]
        dquery_ref[:, lanes(group)] = (cot * conv_ref[:, lanes(group)].astype(F32)).astype(BF16)
        dconv_ref[group_rows(group), :] = (cot * query_ref[:, lanes(group)].astype(F32)).astype(BF16).astype(F32)

    results[0].start()
    results[1].start()
    left = lax.broadcasted_iota(jnp.int32, (SUB, 128), 1) < 64

    def put(row, one, two):
        terms[pl.ds(row, SUB, stride=2 * TERMS), :] = jnp.where(left, one, pltpu.roll(two, 64, 1))
        terms[pl.ds(TERMS + row, SUB, stride=2 * TERMS), :] = jnp.where(left, pltpu.roll(one, 64, 1), two)

    all_decay = [step_decay(table, m) for m in range(MODES)]

    def backward(i, back):
        for u in range(UNROLL):
            value = at(dconv_ref, ROWS - 1 - (i * UNROLL + u))
            back = tuple(all_decay[m] * back[m] + value for m in range(MODES))
        return back

    back = lax.fori_loop(0, ROWS // UNROLL, backward, zeros(MODES))
    for m in range(MODES):
        back_ref[m] = back[m]
    for m in range(0, MODES, 2):
        state = jnp.concatenate([back[m], back[m + 1]]).astype(BF16)
        for j in range(BLOCKS):
            sent_ref[j, SUB * m : SUB * (m + 2), :] = state
    half = MODES // 2
    for first in (0, half):
        modes = range(first, first + half)
        decay = [step_decay(table, m) for m in modes]

        def forward(i, packed):
            held, moment, first_sum, second_sum, skip_sum = packed
            for u in range(UNROLL):
                value = at(mixed_ref, i * UNROLL + u)
                cot = at(dconv_ref, i * UNROLL + u)
                past = [decay[m] * held[m] for m in range(half)]
                moment = tuple(decay[m] * moment[m] + past[m] for m in range(half))
                held = tuple(past[m] + value for m in range(half))
                first_sum = tuple(first_sum[m] + cot * held[m] for m in range(half))
                second_sum = tuple(second_sum[m] + cot * moment[m] for m in range(half))
                skip_sum = skip_sum + cot * value
            return (held, moment, first_sum, second_sum, skip_sum)

        start = (tuple(carry_ref[m] for m in modes), zeros(half), zeros(half), zeros(half), zeros(1)[0])
        held, moment, first_sum, second_sum, skip_sum = lax.fori_loop(0, ROWS // UNROLL, forward, start)

        for m in range(half):
            put(first + m, first_sum[m], second_sum[m])
            put(MODES + first + m, moment[m], back_ref[first + m])
    for row in range(2 * MODES, TERMS):
        put(row, skip_sum, skip_sum)
    for j in range(BLOCKS):
        term = terms[TERMS * j : TERMS * (j + 1), :]
        upper = term.astype(BF16)
        sent_ref[j, STATE : STATE + TERMS, :] = upper
        sent_ref[j, STATE + TERMS :, :] = (term - upper.astype(F32)).astype(BF16)
    results[2].start()
    for result in results:
        result.wait()


def owner_sums(parts_ref, rate_ref, residue_ref, dresidue_ref, drate_ref, dskip_ref):
    rate = rate_ref[...]
    residue = residue_ref[...]
    near = jnp.exp(rate * (-1.0 / SEQ))
    far = jnp.exp(rate * (-float(ROWS) / SEQ))
    scale = jnp.sqrt(rate * (2.0 / SEQ))
    first = jnp.zeros_like(rate)
    second = jnp.zeros_like(rate)
    skip = jnp.zeros((1, rate.shape[1]), F32)
    later = jnp.zeros_like(rate)
    for j in range(BLOCKS - 1, -1, -1):
        upper, lower = parts_ref[j, :TERMS, :], parts_ref[j, TERMS:, :]
        terms = upper.astype(F32) + lower.astype(F32)
        sums, ends = terms[0:MODES], terms[MODES : 2 * MODES]
        first += sums[:, :64]
        second += sums[:, 64:] + near * later * ends[:, :64]
        later = far * later + ends[:, 64:]
        skip += terms[2 * MODES : 2 * MODES + 1, :64]
    proj = scale * first
    dresidue_ref[...] = proj
    drate_ref[...] = residue * (0.5 * proj / rate - scale * second * (1.0 / SEQ))
    dskip_ref[...] = skip


def backward_kernel(
    own_ref, sent_in, dconv_in, key_in, value_in, table_in, rate_ref, residue_ref,
    dkey_out, dvalue_out, dresidue_ref, drate_ref, dskip_ref,
    sent_ref, dconv_ref, key_ref, value_ref, table, dkey_ref, dvalue_ref, carry_ref, buffer, sems,
):
    own = own_ref[0]
    copies = [
        pltpu.make_async_copy(source, target, sems.at[i])
        for i, (source, target) in enumerate(
            [
                (sent_in, sent_ref),
                (table_in, table),
                (dconv_in, dconv_ref),
                (key_in, key_ref),
                (value_in, value_ref),
            ]
        )
    ]
    results = [
        pltpu.make_async_copy(dkey_ref, dkey_out, sems.at[5]),
        pltpu.make_async_copy(dvalue_ref, dvalue_out, sems.at[6]),
    ]
    for copy in copies:
        copy.start()
    copies[0].wait()
    copies[1].wait()
    for m in range(MODES):
        far = block_decay(table, m)
        carry = jnp.zeros((SUB, 128), F32)
        for j in range(BLOCKS - 1, 0, -1):
            carry = jnp.where(j > own, far * carry + sent_ref[j, SUB * m : SUB * (m + 1), :].astype(F32), carry)
        carry_ref[m] = carry
    copies[2].wait()
    decay = [step_decay(table, m) for m in range(MODES)]
    weight = [mode_weight(table, m) for m in range(MODES)]
    skip = skip_of(table)

    def body(i, held):
        for u in range(UNROLL):
            step = ROWS - 1 - (i * UNROLL + u)
            value = at(dconv_ref, step)
            held = tuple(decay[m] * held[m] + value for m in range(MODES))
            total = tree_sum([weight[m] * held[m] for m in range(MODES)])
            buffer[pl.ds(pl.multiple_of(step * SUB, SUB), SUB), :] = total + skip * value
        return held

    lax.fori_loop(0, ROWS // UNROLL, body, tuple(carry_ref[m] for m in range(MODES)))
    copies[3].wait()
    copies[4].wait()
    for group in range(SUB):
        grad = buffer[group_rows(group), :].astype(BF16).astype(F32)
        dkey_ref[:, lanes(group)] = (grad * value_ref[:, lanes(group)].astype(F32)).astype(BF16)
        dvalue_ref[:, lanes(group)] = (grad * key_ref[:, lanes(group)].astype(F32)).astype(BF16)
    for result in results:
        result.start()
    owner_sums(sent_ref.at[:, STATE:], rate_ref, residue_ref, dresidue_ref, drate_ref, dskip_ref)
    for result in results:
        result.wait()


def add_kernel(*refs):
    out_ref = refs[-1]
    total = refs[0][...].astype(F32).reshape(out_ref.shape)
    for ref in refs[1:-2]:
        total += ref[...].astype(F32).reshape(out_ref.shape)
    out_ref[...] = total.astype(out_ref.dtype)


def stage_kernel(*refs):
    parts, outs, held, sems = refs[:6], refs[7:11], refs[11], refs[12]
    copies = [pltpu.make_async_copy(parts[i].at[1], held.at[i], sems.at[i]) for i in range(4)]
    for k in (1, 2, 3):
        for i in (0, 1):
            at = 2 * k + 2 + i
            copies.append(pltpu.make_async_copy(parts[4 + i].at[k], held.at[at], sems.at[at]))
    for copy in copies:
        copy.start()
    for copy in copies[:4]:
        copy.wait()
    outs[0][...] = sum(held[i].astype(F32) for i in range(4)).astype(BF16)
    for k in (1, 2, 3):
        copies[2 * k + 2].wait()
        copies[2 * k + 3].wait()
        outs[k][...] = (held[2 * k + 2].astype(F32) + held[2 * k + 3].astype(F32)).astype(BF16)


def add_placed_kernel(place_ref, *refs):
    add_kernel(*refs)


def add_placed(array, place, after):
    specs = [pl.BlockSpec((1, ROWS, 512), lambda i, at, k=k: (2 * k + at[0], 0, 0)) for k in range(4)]
    return pl.pallas_call(
        add_placed_kernel,
        grid_spec=pltpu.PrefetchScalarGridSpec(
            num_scalar_prefetch=1,
            grid=(1,),
            in_specs=specs + [pl.BlockSpec(memory_space=pl.ANY)],
            out_specs=pl.BlockSpec((ROWS, 512), lambda i, at: (0, 0)),
        ),
        out_shape=bf16(ROWS, 512),
        name="sum_output",
        **params_of(1_000_000, 2_000_000),
    )(place.reshape(1).astype(jnp.int32), *[far(array)] * 4, far(after))


def last_kernel(place_ref, *refs):
    parts, arrived_ref, last_ref = refs[:10], refs[10], refs[11]
    weight_out, output_out = refs[13:15]
    held, arrived, weight_ref, output_ref, sems = refs[15:]
    copies = [pltpu.make_async_copy(parts[i].at[0], held.at[i], sems.at[i]) for i in range(10)]
    for k in range(4):
        copies.append(pltpu.make_async_copy(arrived_ref.at[2 * k + place_ref[0]], arrived.at[k], sems.at[10 + k]))
    copies.append(pltpu.make_async_copy(last_ref, arrived.at[4], sems.at[14]))
    results = [
        pltpu.make_async_copy(weight_ref.at[:HALF], weight_out.at[:HALF], sems.at[15]),
        pltpu.make_async_copy(weight_ref.at[HALF:], weight_out.at[HALF:], sems.at[16]),
        pltpu.make_async_copy(output_ref, output_out, sems.at[17]),
    ]
    for copy in copies:
        copy.start()
    for half in (0, 1):
        for copy in copies[5 * half : 5 * half + 5]:
            copy.wait()
        weight_ref[HALF * half : HALF * (half + 1)] = sum(held[5 * half + i].astype(F32) for i in range(5))
        results[half].start()
    for copy in copies[10:]:
        copy.wait()
    output_ref[...] = sum(arrived[k].astype(F32) for k in range(5)).astype(BF16)
    results[2].start()
    for copy in results:
        copy.wait()


def f32(*shape):
    return jax.ShapeDtypeStruct(shape, F32)


def bf16(*shape):
    return jax.ShapeDtypeStruct(shape, BF16)


def exchange(array, axis, groups=None):
    return lax.all_to_all(array, axis, split_axis=0, concat_axis=0, tiled=True, axis_index_groups=groups)


def to_all(array, axis, count):
    return exchange(jnp.broadcast_to(array[None], (count,) + array.shape), axis)


MOVES = [(k, z) for k in range(4) for z in range(2)]


def shift_x(k, z=0):
    return [(2 * x + p, 2 * ((x + k) % 4) + (p + z) % 2) for x in range(4) for p in range(2)]


def shift_y(k):
    return [(8 * z + 2 * y + c, 8 * z + 2 * ((y + k) % 4) + c) for z in range(2) for y in range(4) for c in range(2)]


def local(query, key_part, value_part, out_cotangent, w_out, residue, rate, skip):
    own = lax.axis_index("ctx")
    own_array = own.reshape(1).astype(jnp.int32)
    core, own_y, own_z = own % 2, own // 2 % 4, own // 8
    place = lax.axis_index("tp")
    place_x, place_z = place // 2, place % 2
    smem = pl.BlockSpec(memory_space=pltpu.SMEM)
    core_swap = [(i, i ^ 1) for i in range(BLOCKS)]
    far_swap = [(i, i ^ 8) for i in range(BLOCKS)]
    hbm = pl.BlockSpec(memory_space=pltpu.HBM)

    steps = jnp.arange(8, dtype=jnp.int32)
    came = ((place_x - steps // 2) % 4) * 2 + (place_z + steps) % 2
    chip = ((own_z + steps // 4) % 2) * 4 + (own_y + steps) % 4
    index = 2 * ((place_x - chip // 2) % 4) + (chip - place_z) % 2
    core_array = core.reshape(1).astype(jnp.int32)

    packed = pl.pallas_call(
        pack_kernel,
        grid=(1,),
        out_shape=far_f32(BLOCKS, PACK, 128),
        in_specs=[full(MODES, 64), full(MODES, 64), full(1, 64)],
        out_specs=full(BLOCKS, PACK, 128),
        name="pack_parameters",
        **params_of(100_000, 200_000),
    )(far(rate.T), far(residue.T), far(skip[None]))
    packed = exchange(packed, "ctx")
    near_cot = lax.ppermute(out_cotangent, "tp", shift_x(0, 1))
    mixed_near, mixed, cot_pair = pl.pallas_call(
        mix_kernel,
        grid=(1,),
        out_shape=(f32(ROWS * SUB, 128), far_f32(ROWS * SUB, 128), far_bf16(2, ROWS, 512)),
        in_specs=[full(ROWS, 1024)] * 2 + [full(ROWS, 512)] * 2,
        out_specs=(whole(), full(ROWS * SUB, 128), full(2, ROWS, 512)),
        name="mix_inputs",
        **params_of(100_000_000, 3_000_000),
    )(far(key_part), far(value_part), far(out_cotangent), near_cot)
    cot_parts = [cot_pair] + [lax.ppermute(cot_pair, "tp", shift_x(k)) for k in (1, 2, 3)]

    sent, table = pl.pallas_call(
        states_kernel,
        grid=(1,),
        out_shape=(far_bf16(BLOCKS, MODES, SUB, 128), far_f32(TABLE, 128)),
        in_specs=[whole()] * 2,
        out_specs=(full(BLOCKS, MODES, SUB, 128), full(TABLE, 128)),
        name="forward_states",
        **params_of(3_000_000_000, 4_000_000),
    )(mixed_near, packed)
    sent = exchange(sent, "ctx")

    anywhere = pl.BlockSpec(memory_space=pl.ANY)
    conv_out, gated, carry, gated_near, weight_near = pl.pallas_call(
        forward_kernel,
        out_shape=(
            far_bf16(ROWS, 1024),
            far_bf16(ROWS, 1024),
            far_f32(MODES, SUB, 128),
            bf16(ROWS, 1024),
            bf16(8, 1024, 512),
        ),
        in_specs=[smem, whole(), anywhere, anywhere, anywhere, anywhere],
        out_specs=(anywhere, anywhere, anywhere, whole(), whole()),
        scratch_shapes=[
            pltpu.VMEM((ROWS * SUB, 128), F32),
            pltpu.VMEM((ROWS * SUB, 128), F32),
            pltpu.VMEM((ROWS, 1024), BF16),
            pltpu.VMEM((TABLE, 128), F32),
            pltpu.VMEM((ROWS, 1024), BF16),
            pltpu.VMEM((MODES, SUB, 128), F32),
            pltpu.SemaphoreType.DMA((14,)),
        ],
        name="forward_conv",
        **params_of(5_000_000_000, 4_000_000),
    )(own_array, sent, far(mixed), far(query), far(table), far(w_out))

    other_gated = lax.ppermute(gated, "ctx", core_swap)
    partial_out, half_cots = pl.pallas_call(
        output_kernel,
        out_shape=(far_bf16(8, ROWS, 512), bf16(8, ROWS, 256)),
        in_specs=[smem, whole(), whole()] + [anywhere] * 4,
        out_specs=(anywhere, whole()),
        scratch_shapes=[pltpu.VMEM((8, ROWS, 512), BF16), pltpu.SemaphoreType.DMA((16,))],
        name="output_projection",
        **params_of(2_147_483_648, 11_000_000),
    )(core_array, gated_near, weight_near, far(cot_parts[0]), *cot_parts[1:])
    other_cots = lax.ppermute(half_cots, "ctx", core_swap)

    *by_y, same_z, other_z = pl.pallas_call(
        weight_kernel,
        out_shape=(far_bf16(2, HALF, 256),) * 4 + (far_bf16(4, HALF, 256),) * 2,
        in_specs=[smem] + [anywhere] * 8,
        out_specs=(anywhere,) * 6,
        scratch_shapes=[
            pltpu.VMEM((2, ROWS, 1024), BF16),
            pltpu.VMEM((1024, 2 * ROWS), BF16),
            pltpu.VMEM((8, 2 * ROWS, 256), BF16),
            pltpu.VMEM((8, 1024, 256), BF16),
            pltpu.SemaphoreType.DMA((18,)),
            pltpu.SemaphoreType.DMA((16,)),
        ],
        name="projection_gradient",
        **params_of(2_147_483_648, 8_000_000),
    )(jnp.concatenate([index, core_array]), far(gated), other_gated, *[far(part) for part in cot_parts], other_cots, far(partial_out))
    came_z = lax.ppermute(other_z, "ctx", far_swap)
    came_y = [lax.ppermute(by_y[k], "ctx", shift_y(k)) for k in (1, 2, 3)]

    lines = [[2 * x + z for x in range(4)] for z in range(2)]
    arrived = exchange(partial_out.reshape(4, 2, ROWS, 512), "tp", lines).reshape(8, ROWS, 512)

    d_query, d_conv, payload = pl.pallas_call(
        cotangent_kernel,
        out_shape=(far_bf16(ROWS, 1024), far_f32(ROWS * SUB, 128), far_bf16(BLOCKS, STATE + 2 * TERMS, 128)),
        in_specs=[smem] + [anywhere] * 11,
        out_specs=(anywhere,) * 3,
        scratch_shapes=[
            pltpu.VMEM((ROWS, 1024), F32),
            pltpu.VMEM((BLOCKS * TERMS, 128), F32),
            pltpu.VMEM((4, ROWS, 1024), BF16),
            pltpu.VMEM((4, 1024, 1024), BF16),
            pltpu.VMEM((ROWS, 1024), BF16),
            pltpu.VMEM((ROWS, 1024), BF16),
            pltpu.VMEM((ROWS * SUB, 128), F32),
            pltpu.VMEM((MODES, SUB, 128), F32),
            pltpu.VMEM((TABLE, 128), F32),
            pltpu.VMEM((ROWS, 1024), BF16),
            pltpu.VMEM((ROWS * SUB, 128), F32),
            pltpu.VMEM((BLOCKS, STATE + 2 * TERMS, 128), BF16),
            pltpu.VMEM((MODES, SUB, 128), F32),
            pltpu.SemaphoreType.DMA((24,)),
        ],
        name="cotangent_states",
        **params_of(14_000_000_000, 13_000_000),
    )(came, *[far(part) for part in cot_parts], far(w_out), far(query), far(conv_out), far(mixed), far(carry), far(table), far(other_z))
    received = exchange(payload, "ctx")

    near_out = add_placed(arrived, 1 - place_z, payload)
    near_sum = near_out
    near_out = lax.ppermute(near_out, "tp", shift_x(0, 1))
    first_far, *second_far = pl.pallas_call(
        stage_kernel,
        out_shape=(bf16(HALF, 256),) * 4,
        in_specs=[anywhere] * 7,
        out_specs=(whole(),) * 4,
        scratch_shapes=[pltpu.VMEM((10, HALF, 256), BF16), pltpu.SemaphoreType.DMA((10,))],
        name="sum_stage",
        **params_of(LONG, 2_000_000),
    )(far(by_y[0]), *came_y, far(same_z), came_z, near_sum)
    first_far = lax.ppermute(first_far, "ctx", far_swap)
    second_far = [lax.ppermute(second_far[k - 1], "ctx", shift_y(k)) for k in (1, 2, 3)]

    d_key, d_value, d_residue, d_rate, d_skip = pl.pallas_call(
        backward_kernel,
        grid=(1,),
        out_shape=(
            far_bf16(ROWS, 1024),
            far_bf16(ROWS, 1024),
            f32(MODES, 64),
            f32(MODES, 64),
            f32(1, 64),
        ),
        in_specs=[smem] + [anywhere] * 5 + [full(MODES, 64)] * 2,
        out_specs=(anywhere, anywhere, full(MODES, 64), full(MODES, 64), full(1, 64)),
        scratch_shapes=[
            pltpu.VMEM((BLOCKS, STATE + 2 * TERMS, 128), BF16),
            pltpu.VMEM((ROWS * SUB, 128), F32),
            pltpu.VMEM((ROWS, 1024), BF16),
            pltpu.VMEM((ROWS, 1024), BF16),
            pltpu.VMEM((TABLE, 128), F32),
            pltpu.VMEM((ROWS, 1024), BF16),
            pltpu.VMEM((ROWS, 1024), BF16),
            pltpu.VMEM((MODES, SUB, 128), F32),
            pltpu.VMEM((ROWS * SUB, 128), F32),
            pltpu.SemaphoreType.DMA((7,)),
        ],
        name="backward_conv",
        **params_of(5_000_000_000, 4_000_000),
    )(
        own_array,
        received,
        far(d_conv),
        far(key_part),
        far(value_part),
        far(table),
        far(rate.T),
        far(residue.T),
    )

    d_weight, output = pl.pallas_call(
        last_kernel,
        out_shape=(far_f32(2 * HALF, 256), far_bf16(ROWS, 512)),
        in_specs=[smem] + [anywhere] * 13,
        out_specs=(anywhere,) * 2,
        scratch_shapes=[
            pltpu.VMEM((10, HALF, 256), BF16),
            pltpu.VMEM((5, ROWS, 512), BF16),
            pltpu.VMEM((2 * HALF, 256), F32),
            pltpu.VMEM((ROWS, 512), BF16),
            pltpu.SemaphoreType.DMA((18,)),
        ],
        name="last_sums",
        **params_of(2_000_000, 4_000_000),
    )(
        place_z.reshape(1).astype(jnp.int32),
        far(by_y[0]),
        *came_y,
        first_far[None],
        far(same_z),
        came_z,
        *[part[None] for part in second_far],
        far(arrived),
        near_out,
        far(d_key),
    )

    return (output, d_query, d_key, d_value, d_weight, d_residue.T, d_rate.T, d_skip[0])


def solution(mesh):
    rows, owner = P("ctx", "tp"), P(("tp", "ctx"))
    return jax.shard_map(
        local,
        mesh=mesh,
        in_specs=(rows, rows, rows, rows, P("tp", None), P(("tp", "ctx"), None), P(("tp", "ctx"), None), owner),
        out_specs=(rows, rows, rows, rows, P("tp", "ctx"), P(("tp", "ctx"), None), P(("tp", "ctx"), None), owner),
        check_vma=False,
    )
```

```python
import functools

import jax
import jax.numpy as jnp
from jax import lax
from jax.experimental import pallas as pl
from jax.experimental.pallas import tpu as pltpu
from jax.sharding import PartitionSpec as P

F32 = jnp.float32
BF16 = jnp.bfloat16
SEQ = 4096
MODES = 16
ROWS = 256
SUB = 8
BLOCKS = 16
HALF = 512
UNROLL = 8
PACK = 24
TABLE = 2 * PACK * SUB
STATE = MODES * SUB
TERMS = 48
VMEM = 32 * 1024 * 1024
LONG = 2_000_000_000_000
SHORT = 50


def params_of(flops, nbytes):
    return dict(
        compiler_params=pltpu.CompilerParams(vmem_limit_bytes=VMEM),
        cost_estimate=pl.CostEstimate(flops=flops // SHORT, bytes_accessed=nbytes // SHORT, transcendentals=0),
    )


def whole():
    return pl.BlockSpec(memory_space=pltpu.VMEM)


def full(*shape):
    return pl.BlockSpec(shape, lambda *_: (0,) * len(shape))


def far(array):
    return pltpu.with_memory_space_constraint(array, pltpu.HBM)


def far_f32(*shape):
    return pltpu.HBM(shape, F32)


def far_bf16(*shape):
    return pltpu.HBM(shape, BF16)


def lanes(group):
    return slice(128 * group, 128 * (group + 1))


def group_rows(group):
    return pl.ds(group, ROWS, stride=SUB)


def rate_of(table, mode):
    return table[SUB * mode : SUB * (mode + 1), :]


def step_decay(table, mode):
    return jnp.exp(rate_of(table, mode) * (-1.0 / SEQ))


def block_decay(table, mode):
    return jnp.exp(rate_of(table, mode) * (-float(ROWS) / SEQ))


def mode_weight(table, mode):
    return rate_of(table, PACK + mode) * jnp.sqrt(rate_of(table, mode) * (2.0 / SEQ))


def skip_of(table):
    return rate_of(table, MODES)


def at(ref, step):
    return ref[pl.ds(pl.multiple_of(step * SUB, SUB), SUB), :]


def zeros(count):
    return tuple(jnp.zeros((SUB, 128), F32) for _ in range(count))


def tree_sum(parts):
    parts = list(parts)
    while len(parts) > 1:
        parts = [sum(parts[i : i + 2]) for i in range(0, len(parts), 2)]
    return parts[0]


def pack_kernel(rate_ref, residue_ref, skip_ref, out_ref):
    both = jnp.concatenate([rate_ref[...], residue_ref[...]], axis=1)
    last = jnp.concatenate([skip_ref[...], skip_ref[...]], axis=1)
    for j in range(BLOCKS):
        out_ref[j, :MODES] = both
        out_ref[j, MODES:] = jnp.broadcast_to(last, (PACK - MODES, 128))


def mix_kernel(key_ref, value_ref, cot_ref, near_cot_ref, mixed_ref, kept_ref, pair_ref):
    pair_ref[0] = cot_ref[...]
    pair_ref[1] = near_cot_ref[...]
    for group in range(SUB):
        product = key_ref[:, lanes(group)].astype(F32) * value_ref[:, lanes(group)].astype(F32)
        mixed_ref[group_rows(group), :] = product.astype(BF16).astype(F32)
    kept_ref[...] = mixed_ref[...]


def states_kernel(mixed_ref, packed_ref, sent_ref, table):
    left = lax.broadcasted_iota(jnp.int32, (PACK, 128), 1) < 64
    for group in range(SUB):
        one, two = packed_ref[2 * group], packed_ref[2 * group + 1]
        table[pl.ds(group, PACK, stride=SUB), :] = jnp.where(left, one, pltpu.roll(two, 64, 1))
        table[pl.ds(PACK * SUB + group, PACK, stride=SUB), :] = jnp.where(left, pltpu.roll(one, 64, 1), two)
    decay = [step_decay(table, m) for m in range(MODES)]

    def body(i, held):
        for u in range(UNROLL):
            value = at(mixed_ref, i * UNROLL + u)
            held = tuple(decay[m] * held[m] + value for m in range(MODES))
        return held

    held = lax.fori_loop(0, ROWS // UNROLL, body, zeros(MODES))
    for m in range(MODES):
        state = held[m].astype(BF16)
        for j in range(BLOCKS):
            sent_ref[j, m] = state


def forward_kernel(
    own_ref, sent_ref, mixed_in, query_in, table_in, weight_in,
    conv_out, gated_out, carry_out, gated_ref, weight_ref,
    buffer, mixed_ref, query_ref, table, conv_ref, carry_ref, sems,
):
    own = own_ref[0]
    copies = [
        pltpu.make_async_copy(source, target, sems.at[i])
        for i, (source, target) in enumerate([(table_in, table), (mixed_in, mixed_ref), (query_in, query_ref)])
    ]
    weights = [
        pltpu.make_async_copy(weight_in.at[:, 512 * i : 512 * (i + 1)], weight_ref.at[i], sems.at[6 + i])
        for i in range(8)
    ]
    results = [
        pltpu.make_async_copy(source, target, sems.at[3 + i])
        for i, (source, target) in enumerate([(carry_ref, carry_out), (conv_ref, conv_out), (gated_ref, gated_out)])
    ]
    for copy in copies + weights:
        copy.start()
    copies[0].wait()
    for m in range(MODES):
        far = block_decay(table, m)
        carry = jnp.zeros((SUB, 128), F32)
        for j in range(BLOCKS - 1):
            carry = jnp.where(j < own, far * carry + sent_ref[j, m].astype(F32), carry)
        carry_ref[m] = carry
    results[0].start()
    copies[1].wait()
    decay = [step_decay(table, m) for m in range(MODES)]
    weight = [mode_weight(table, m) for m in range(MODES)]
    skip = skip_of(table)

    def body(i, held):
        for u in range(UNROLL):
            step = i * UNROLL + u
            value = at(mixed_ref, step)
            held = tuple(decay[m] * held[m] + value for m in range(MODES))
            total = tree_sum([weight[m] * held[m] for m in range(MODES)])
            buffer[pl.ds(pl.multiple_of(step * SUB, SUB), SUB), :] = total + skip * value
        return held

    lax.fori_loop(0, ROWS // UNROLL, body, tuple(carry_ref[m] for m in range(MODES)))
    copies[2].wait()
    for group in range(SUB):
        conv = buffer[group_rows(group), :].astype(BF16)
        conv_ref[:, lanes(group)] = conv
        gated_ref[:, lanes(group)] = (query_ref[:, lanes(group)].astype(F32) * conv.astype(F32)).astype(BF16)
    results[1].start()
    results[2].start()
    for copy in results + weights:
        copy.wait()


def output_kernel(gated_ref, weight_ref, out_ref, blocks, sems):
    results = [pltpu.make_async_copy(blocks.at[i], out_ref.at[i], sems.at[i]) for i in range(8)]
    for i in range(8):
        blocks[i] = jnp.dot(gated_ref[...], weight_ref[i], preferred_element_type=F32).astype(BF16)
        results[i].start()
    for result in results:
        result.wait()


def weight_kernel(index_ref, gated_ref, other_ref, *refs):
    cot_refs, other_refs = refs[:4], refs[4:8]
    along_y, along_z = refs[9:13], refs[13:15]
    gated, turned, cots, chunks, sems, out_sems = refs[15:]
    half = pl.ds(pl.multiple_of(index_ref[8] * 256, 256), 256)
    copies = [
        pltpu.make_async_copy(gated_ref, gated, sems.at[8]),
    ]
    for i in range(8):
        own = cot_refs[i // 2].at[i % 2, :, half]
        other = other_refs[i // 2].at[i % 2, :, half]
        copies.append(pltpu.make_async_copy(own, cots.at[i, :ROWS], sems.at[i]))
        copies.append(pltpu.make_async_copy(other, cots.at[i, ROWS:], sems.at[9 + i]))
    for copy in copies:
        copy.start()
    turned[:, ROWS:] = other_ref[...].T
    copies[0].wait()
    turned[:, :ROWS] = gated[...].T
    for copy in copies[1:]:
        copy.wait()
    results = []
    for z in (1, 0):
        for k in range(4):
            i = 4 * z + k
            total = jnp.dot(turned[...], cots[index_ref[i]], preferred_element_type=F32)
            chunks[i] = total.astype(BF16)
            results.append(pltpu.make_async_copy(chunks.at[i, HALF:], along_z[z].at[k], out_sems.at[i]))
            results.append(pltpu.make_async_copy(chunks.at[i, :HALF], along_y[k].at[z], out_sems.at[8 + i]))
            results[-2].start()
            results[-1].start()
    for copy in results:
        copy.wait()


def cotangent_kernel(
    came_ref, part0, part1, part2, part3, weight_ref, query_in, conv_in, mixed_in, carry_in, table_in, after_ref,
    dquery_out, dconv_out, sent_out,
    total, terms, parts, weight, query_ref, conv_ref, mixed_ref, carry_ref, table, dquery_ref, dconv_ref, sent_ref, back_ref, sems,
):
    copies = []
    for i in range(8):
        columns = pl.ds(pl.multiple_of(came_ref[i] * 512, 512), 512)
        part = (part0, part1, part2, part3)[i // 2].at[i % 2]
        place = slice(512 * (i % 2), 512 * (i % 2 + 1))
        copies.append(pltpu.make_async_copy(weight_ref.at[:, columns], weight.at[i // 2, :, place], sems.at[i]))
        copies.append(pltpu.make_async_copy(part, parts.at[i // 2, :, place], sems.at[8 + i]))
    later = [
        pltpu.make_async_copy(source, target, sems.at[16 + i])
        for i, (source, target) in enumerate(
            [(query_in, query_ref), (conv_in, conv_ref), (mixed_in, mixed_ref), (carry_in, carry_ref), (table_in, table)]
        )
    ]
    results = [
        pltpu.make_async_copy(source, target, sems.at[21 + i])
        for i, (source, target) in enumerate(
            [(dquery_ref, dquery_out), (dconv_ref, dconv_out), (sent_ref, sent_out)]
        )
    ]
    for copy in copies + later:
        copy.start()
    for i in range(4):
        for copy in copies[4 * i : 4 * i + 4]:
            copy.wait()
        product = lax.dot_general(parts[i], weight[i], (((1,), (1,)), ((), ())), preferred_element_type=F32)
        if i == 0:
            total[...] = product
        else:
            total[...] += product
    for copy in later:
        copy.wait()
    for group in range(SUB):
        cot = total[:, lanes(group)]
        dquery_ref[:, lanes(group)] = (cot * conv_ref[:, lanes(group)].astype(F32)).astype(BF16)
        dconv_ref[group_rows(group), :] = (cot * query_ref[:, lanes(group)].astype(F32)).astype(BF16).astype(F32)

    results[0].start()
    results[1].start()
    left = lax.broadcasted_iota(jnp.int32, (SUB, 128), 1) < 64

    def put(row, one, two):
        terms[pl.ds(row, SUB, stride=2 * TERMS), :] = jnp.where(left, one, pltpu.roll(two, 64, 1))
        terms[pl.ds(TERMS + row, SUB, stride=2 * TERMS), :] = jnp.where(left, pltpu.roll(one, 64, 1), two)

    all_decay = [step_decay(table, m) for m in range(MODES)]

    def backward(i, back):
        for u in range(UNROLL):
            value = at(dconv_ref, ROWS - 1 - (i * UNROLL + u))
            back = tuple(all_decay[m] * back[m] + value for m in range(MODES))
        return back

    back = lax.fori_loop(0, ROWS // UNROLL, backward, zeros(MODES))
    for m in range(MODES):
        back_ref[m] = back[m]
    for m in range(0, MODES, 2):
        state = jnp.concatenate([back[m], back[m + 1]]).astype(BF16)
        for j in range(BLOCKS):
            sent_ref[j, SUB * m : SUB * (m + 2), :] = state
    half = MODES // 2
    for first in (0, half):
        modes = range(first, first + half)
        decay = [step_decay(table, m) for m in modes]

        def forward(i, packed):
            held, moment, first_sum, second_sum, skip_sum = packed
            for u in range(UNROLL):
                value = at(mixed_ref, i * UNROLL + u)
                cot = at(dconv_ref, i * UNROLL + u)
                past = [decay[m] * held[m] for m in range(half)]
                moment = tuple(decay[m] * moment[m] + past[m] for m in range(half))
                held = tuple(past[m] + value for m in range(half))
                first_sum = tuple(first_sum[m] + cot * held[m] for m in range(half))
                second_sum = tuple(second_sum[m] + cot * moment[m] for m in range(half))
                skip_sum = skip_sum + cot * value
            return (held, moment, first_sum, second_sum, skip_sum)

        start = (tuple(carry_ref[m] for m in modes), zeros(half), zeros(half), zeros(half), zeros(1)[0])
        held, moment, first_sum, second_sum, skip_sum = lax.fori_loop(0, ROWS // UNROLL, forward, start)

        for m in range(half):
            put(first + m, first_sum[m], second_sum[m])
            put(MODES + first + m, moment[m], back_ref[first + m])
    for row in range(2 * MODES, TERMS):
        put(row, skip_sum, skip_sum)
    for j in range(BLOCKS):
        term = terms[TERMS * j : TERMS * (j + 1), :]
        sent_ref[j, STATE:, :] = term.astype(BF16)
    results[2].start()
    for result in results:
        result.wait()


def owner_sums(parts_ref, rate_ref, residue_ref, dresidue_ref, drate_ref, dskip_ref):
    rate = rate_ref[...]
    residue = residue_ref[...]
    near = jnp.exp(rate * (-1.0 / SEQ))
    far = jnp.exp(rate * (-float(ROWS) / SEQ))
    scale = jnp.sqrt(rate * (2.0 / SEQ))
    first = jnp.zeros_like(rate)
    second = jnp.zeros_like(rate)
    skip = jnp.zeros((1, rate.shape[1]), F32)
    later = jnp.zeros_like(rate)
    for j in range(BLOCKS - 1, -1, -1):
        terms = parts_ref[j].astype(F32)
        sums, ends = terms[0:MODES], terms[MODES : 2 * MODES]
        first += sums[:, :64]
        second += sums[:, 64:] + near * later * ends[:, :64]
        later = far * later + ends[:, 64:]
        skip += terms[2 * MODES : 2 * MODES + 1, :64]
    proj = scale * first
    dresidue_ref[...] = proj
    drate_ref[...] = residue * (0.5 * proj / rate - scale * second * (1.0 / SEQ))
    dskip_ref[...] = skip


def backward_kernel(
    own_ref, sent_ref, dconv_in, key_in, value_in, table_in, first_in, same_in, arrived_in,
    came1, came2, came3, came_z, rate_ref, residue_ref,
    dkey_out, dvalue_out, gradient_ref, output_ref, dresidue_ref, drate_ref, dskip_ref,
    dconv_ref, key_ref, value_ref, table, dkey_ref, dvalue_ref, carry_ref, buffer, blocks, arrived, sems,
):
    own = own_ref[0]
    copies = [
        pltpu.make_async_copy(source, target, sems.at[i])
        for i, (source, target) in enumerate(
            [
                (table_in, table),
                (dconv_in, dconv_ref),
                (key_in, key_ref),
                (value_in, value_ref),
                (first_in.at[0], blocks.at[0]),
                (same_in.at[0], blocks.at[1]),
            ]
            + [(arrived_in.at[2 * k + own_ref[1]], arrived.at[k]) for k in range(4)]
        )
    ]
    results = [
        pltpu.make_async_copy(dkey_ref, dkey_out, sems.at[10]),
        pltpu.make_async_copy(dvalue_ref, dvalue_out, sems.at[11]),
    ]
    for copy in copies:
        copy.start()
    copies[0].wait()
    for m in range(MODES):
        far = block_decay(table, m)
        carry = jnp.zeros((SUB, 128), F32)
        for j in range(BLOCKS - 1, 0, -1):
            carry = jnp.where(j > own, far * carry + sent_ref[j, SUB * m : SUB * (m + 1), :].astype(F32), carry)
        carry_ref[m] = carry
    copies[1].wait()
    decay = [step_decay(table, m) for m in range(MODES)]
    weight = [mode_weight(table, m) for m in range(MODES)]
    skip = skip_of(table)

    def body(i, held):
        for u in range(UNROLL):
            step = ROWS - 1 - (i * UNROLL + u)
            value = at(dconv_ref, step)
            held = tuple(decay[m] * held[m] + value for m in range(MODES))
            total = tree_sum([weight[m] * held[m] for m in range(MODES)])
            buffer[pl.ds(pl.multiple_of(step * SUB, SUB), SUB), :] = total + skip * value
        return held

    lax.fori_loop(0, ROWS // UNROLL, body, tuple(carry_ref[m] for m in range(MODES)))
    copies[2].wait()
    copies[3].wait()
    for group in range(SUB):
        grad = buffer[group_rows(group), :].astype(BF16).astype(F32)
        dkey_ref[:, lanes(group)] = (grad * value_ref[:, lanes(group)].astype(F32)).astype(BF16)
        dvalue_ref[:, lanes(group)] = (grad * key_ref[:, lanes(group)].astype(F32)).astype(BF16)
    for result in results:
        result.start()
    for copy in copies[4:]:
        copy.wait()
    gradient_ref[:HALF] = blocks[0].astype(F32) + sum(part[0].astype(F32) for part in (came1, came2, came3))
    gradient_ref[HALF:] = blocks[1].astype(F32) + came_z[0].astype(F32)
    output_ref[...] = sum(arrived[k].astype(F32) for k in range(4))
    owner_sums(sent_ref.at[:, STATE:], rate_ref, residue_ref, dresidue_ref, drate_ref, dskip_ref)
    for result in results:
        result.wait()


def add_kernel(*refs):
    out_ref = refs[-1]
    total = refs[0][...].astype(F32).reshape(out_ref.shape)
    for ref in refs[1:-2]:
        total += ref[...].astype(F32).reshape(out_ref.shape)
    out_ref[...] = total.astype(out_ref.dtype)


def stage_kernel(own_ref, *refs):
    came_y, came_z, outs = refs[:3], refs[3], refs[4:8]
    outs[0][...] = (own_ref[0].astype(F32) + sum(part[1].astype(F32) for part in came_y)).astype(BF16)
    for k in (1, 2, 3):
        outs[k][...] = (own_ref[k].astype(F32) + came_z[k].astype(F32)).astype(BF16)


def add_placed_kernel(place_ref, arrived_ref, first_ref, same_ref, after_ref, out_ref, own_ref, held, sems):
    copies = [pltpu.make_async_copy(arrived_ref.at[2 * k + place_ref[0]], held.at[k], sems.at[k]) for k in range(4)]
    copies.append(pltpu.make_async_copy(first_ref.at[1], own_ref.at[0], sems.at[4]))
    copies += [pltpu.make_async_copy(same_ref.at[k], own_ref.at[k], sems.at[4 + k]) for k in (1, 2, 3)]
    for copy in copies:
        copy.start()
    for copy in copies[:4]:
        copy.wait()
    out_ref[...] = sum(held[k].astype(F32) for k in range(4)).astype(BF16)
    for copy in copies[4:]:
        copy.wait()


def last_kernel(gradient_ref, out_sum_ref, *refs):
    parts, last_in, weight_out, output_out = refs[:4], refs[4], refs[5], refs[6]
    held, last, weight_ref, output_ref, sems = refs[7:]
    copies = [pltpu.make_async_copy(parts[i], held.at[i], sems.at[i]) for i in range(4)]
    copies.append(pltpu.make_async_copy(last_in, last, sems.at[4]))
    results = [
        pltpu.make_async_copy(weight_ref.at[:HALF], weight_out.at[:HALF], sems.at[5]),
        pltpu.make_async_copy(weight_ref.at[HALF:], weight_out.at[HALF:], sems.at[6]),
        pltpu.make_async_copy(output_ref, output_out, sems.at[7]),
    ]
    for copy in copies:
        copy.start()
    copies[0].wait()
    weight_ref[:HALF] = gradient_ref[:HALF] + held[0].astype(F32)
    results[0].start()
    for copy in copies[1:4]:
        copy.wait()
    weight_ref[HALF:] = gradient_ref[HALF:] + sum(held[i].astype(F32) for i in (1, 2, 3))
    results[1].start()
    copies[4].wait()
    output_ref[...] = (out_sum_ref[...] + last[...].astype(F32)).astype(BF16)
    results[2].start()
    for copy in results:
        copy.wait()


def f32(*shape):
    return jax.ShapeDtypeStruct(shape, F32)


def bf16(*shape):
    return jax.ShapeDtypeStruct(shape, BF16)


def exchange(array, axis, groups=None):
    return lax.all_to_all(array, axis, split_axis=0, concat_axis=0, tiled=True, axis_index_groups=groups)


def to_all(array, axis, count):
    return exchange(jnp.broadcast_to(array[None], (count,) + array.shape), axis)


MOVES = [(k, z) for k in range(4) for z in range(2)]


def shift_x(k, z=0):
    return [(2 * x + p, 2 * ((x + k) % 4) + (p + z) % 2) for x in range(4) for p in range(2)]


def shift_y(k):
    return [(8 * z + 2 * y + c, 8 * z + 2 * ((y + k) % 4) + c) for z in range(2) for y in range(4) for c in range(2)]


def local(query, key_part, value_part, out_cotangent, w_out, residue, rate, skip):
    own = lax.axis_index("ctx")
    own_array = own.reshape(1).astype(jnp.int32)
    core, own_y, own_z = own % 2, own // 2 % 4, own // 8
    place = lax.axis_index("tp")
    place_x, place_z = place // 2, place % 2
    smem = pl.BlockSpec(memory_space=pltpu.SMEM)
    core_swap = [(i, i ^ 1) for i in range(BLOCKS)]
    far_swap = [(i, i ^ 8) for i in range(BLOCKS)]
    hbm = pl.BlockSpec(memory_space=pltpu.HBM)

    steps = jnp.arange(8, dtype=jnp.int32)
    came = ((place_x - steps // 2) % 4) * 2 + (place_z + steps) % 2
    chip = ((own_z + steps // 4) % 2) * 4 + (own_y + steps) % 4
    index = 2 * ((place_x - chip // 2) % 4) + (chip - place_z) % 2
    core_array = core.reshape(1).astype(jnp.int32)

    packed = pl.pallas_call(
        pack_kernel,
        grid=(1,),
        out_shape=far_f32(BLOCKS, PACK, 128),
        in_specs=[full(MODES, 64), full(MODES, 64), full(1, 64)],
        out_specs=full(BLOCKS, PACK, 128),
        name="pack_parameters",
        **params_of(100_000, 200_000),
    )(far(rate.T), far(residue.T), far(skip[None]))
    packed = exchange(packed, "ctx")
    near_cot = lax.ppermute(out_cotangent, "tp", shift_x(0, 1))
    mixed_near, mixed, cot_pair = pl.pallas_call(
        mix_kernel,
        grid=(1,),
        out_shape=(f32(ROWS * SUB, 128), far_f32(ROWS * SUB, 128), far_bf16(2, ROWS, 512)),
        in_specs=[full(ROWS, 1024)] * 2 + [full(ROWS, 512)] * 2,
        out_specs=(whole(), full(ROWS * SUB, 128), full(2, ROWS, 512)),
        name="mix_inputs",
        **params_of(100_000_000, 3_000_000),
    )(far(key_part), far(value_part), far(out_cotangent), near_cot)
    cot_parts = [cot_pair] + [lax.ppermute(cot_pair, "tp", shift_x(k)) for k in (1, 2, 3)]

    sent, table = pl.pallas_call(
        states_kernel,
        grid=(1,),
        out_shape=(far_bf16(BLOCKS, MODES, SUB, 128), far_f32(TABLE, 128)),
        in_specs=[whole()] * 2,
        out_specs=(full(BLOCKS, MODES, SUB, 128), full(TABLE, 128)),
        name="forward_states",
        **params_of(3_000_000_000, 4_000_000),
    )(mixed_near, packed)
    sent = exchange(sent, "ctx")

    anywhere = pl.BlockSpec(memory_space=pl.ANY)
    conv_out, gated, carry, gated_near, weight_near = pl.pallas_call(
        forward_kernel,
        out_shape=(
            far_bf16(ROWS, 1024),
            far_bf16(ROWS, 1024),
            far_f32(MODES, SUB, 128),
            bf16(ROWS, 1024),
            bf16(8, 1024, 512),
        ),
        in_specs=[smem, whole(), anywhere, anywhere, anywhere, anywhere],
        out_specs=(anywhere, anywhere, anywhere, whole(), whole()),
        scratch_shapes=[
            pltpu.VMEM((ROWS * SUB, 128), F32),
            pltpu.VMEM((ROWS * SUB, 128), F32),
            pltpu.VMEM((ROWS, 1024), BF16),
            pltpu.VMEM((TABLE, 128), F32),
            pltpu.VMEM((ROWS, 1024), BF16),
            pltpu.VMEM((MODES, SUB, 128), F32),
            pltpu.SemaphoreType.DMA((14,)),
        ],
        name="forward_conv",
        **params_of(5_000_000_000, 4_000_000),
    )(own_array, sent, far(mixed), far(query), far(table), far(w_out))

    other_gated = lax.ppermute(gated, "ctx", core_swap)
    partial_out = pl.pallas_call(
        output_kernel,
        out_shape=far_bf16(8, ROWS, 512),
        in_specs=[whole(), whole()],
        out_specs=anywhere,
        scratch_shapes=[pltpu.VMEM((8, ROWS, 512), BF16), pltpu.SemaphoreType.DMA((8,))],
        name="output_projection",
        **params_of(2_147_483_648, 11_000_000),
    )(gated_near, weight_near)
    other_parts = [lax.ppermute(part, "ctx", core_swap) for part in cot_parts]

    *by_y, same_z, other_z = pl.pallas_call(
        weight_kernel,
        out_shape=(far_bf16(2, HALF, 256),) * 4 + (far_bf16(4, HALF, 256),) * 2,
        in_specs=[smem, anywhere, whole()] + [anywhere] * 9,
        out_specs=(anywhere,) * 6,
        scratch_shapes=[
            pltpu.VMEM((ROWS, 1024), BF16),
            pltpu.VMEM((1024, 2 * ROWS), BF16),
            pltpu.VMEM((8, 2 * ROWS, 256), BF16),
            pltpu.VMEM((8, 1024, 256), BF16),
            pltpu.SemaphoreType.DMA((17,)),
            pltpu.SemaphoreType.DMA((16,)),
        ],
        name="projection_gradient",
        **params_of(2_147_483_648, 8_000_000),
    )(jnp.concatenate([index, core_array]), far(gated), other_gated, *[far(part) for part in cot_parts], *other_parts, far(partial_out))
    came_z = lax.ppermute(other_z, "ctx", far_swap)
    came_y = [lax.ppermute(by_y[k], "ctx", shift_y(k)) for k in (1, 2, 3)]

    lines = [[2 * x + z for x in range(4)] for z in range(2)]
    arrived = exchange(partial_out.reshape(4, 2, ROWS, 512), "tp", lines).reshape(8, ROWS, 512)

    d_query, d_conv, payload = pl.pallas_call(
        cotangent_kernel,
        out_shape=(far_bf16(ROWS, 1024), far_f32(ROWS * SUB, 128), far_bf16(BLOCKS, STATE + TERMS, 128)),
        in_specs=[smem] + [anywhere] * 11,
        out_specs=(anywhere,) * 3,
        scratch_shapes=[
            pltpu.VMEM((ROWS, 1024), F32),
            pltpu.VMEM((BLOCKS * TERMS, 128), F32),
            pltpu.VMEM((4, ROWS, 1024), BF16),
            pltpu.VMEM((4, 1024, 1024), BF16),
            pltpu.VMEM((ROWS, 1024), BF16),
            pltpu.VMEM((ROWS, 1024), BF16),
            pltpu.VMEM((ROWS * SUB, 128), F32),
            pltpu.VMEM((MODES, SUB, 128), F32),
            pltpu.VMEM((TABLE, 128), F32),
            pltpu.VMEM((ROWS, 1024), BF16),
            pltpu.VMEM((ROWS * SUB, 128), F32),
            pltpu.VMEM((BLOCKS, STATE + TERMS, 128), BF16),
            pltpu.VMEM((MODES, SUB, 128), F32),
            pltpu.SemaphoreType.DMA((24,)),
        ],
        name="cotangent_states",
        **params_of(14_000_000_000, 13_000_000),
    )(came, *[far(part) for part in cot_parts], far(w_out), far(query), far(conv_out), far(mixed), far(carry), far(table), far(other_z))
    received = exchange(payload, "ctx")

    near_sum, own_blocks = pl.pallas_call(
        add_placed_kernel,
        out_shape=(bf16(ROWS, 512), bf16(4, HALF, 256)),
        in_specs=[smem] + [anywhere] * 4,
        out_specs=(whole(), whole()),
        scratch_shapes=[pltpu.VMEM((4, ROWS, 512), BF16), pltpu.SemaphoreType.DMA((8,))],
        name="sum_output",
        **params_of(1_000_000, 2_000_000),
    )(
        (1 - place_z).reshape(1).astype(jnp.int32),
        far(arrived),
        far(by_y[0]),
        far(same_z),
        far(payload),
    )
    near_out = lax.ppermute(near_sum, "tp", shift_x(0, 1))

    first_far, *second_far = pl.pallas_call(
        stage_kernel,
        out_shape=(bf16(HALF, 256),) * 4,
        in_specs=[whole()] * 5,
        out_specs=(whole(),) * 4,
        name="sum_stage",
        **params_of(LONG, 2_000_000),
    )(own_blocks, *came_y, came_z)
    first_far = lax.ppermute(first_far, "ctx", far_swap)
    second_far = [lax.ppermute(second_far[k - 1], "ctx", shift_y(k)) for k in (1, 2, 3)]

    d_key, d_value, gradient, out_sum, d_residue, d_rate, d_skip = pl.pallas_call(
        backward_kernel,
        grid=(1,),
        out_shape=(
            far_bf16(ROWS, 1024),
            far_bf16(ROWS, 1024),
            f32(2 * HALF, 256),
            f32(ROWS, 512),
            f32(MODES, 64),
            f32(MODES, 64),
            f32(1, 64),
        ),
        in_specs=[smem, whole()] + [anywhere] * 7 + [whole()] * 4 + [full(MODES, 64)] * 2,
        out_specs=(anywhere, anywhere, whole(), whole(), full(MODES, 64), full(MODES, 64), full(1, 64)),
        scratch_shapes=[
            pltpu.VMEM((ROWS * SUB, 128), F32),
            pltpu.VMEM((ROWS, 1024), BF16),
            pltpu.VMEM((ROWS, 1024), BF16),
            pltpu.VMEM((TABLE, 128), F32),
            pltpu.VMEM((ROWS, 1024), BF16),
            pltpu.VMEM((ROWS, 1024), BF16),
            pltpu.VMEM((MODES, SUB, 128), F32),
            pltpu.VMEM((ROWS * SUB, 128), F32),
            pltpu.VMEM((2, HALF, 256), BF16),
            pltpu.VMEM((4, ROWS, 512), BF16),
            pltpu.SemaphoreType.DMA((12,)),
        ],
        name="backward_conv",
        **params_of(5_000_000_000, 4_000_000),
    )(
        jnp.stack([own, place_z]).astype(jnp.int32),
        received,
        far(d_conv),
        far(key_part),
        far(value_part),
        far(table),
        far(by_y[0]),
        far(same_z),
        far(arrived),
        *came_y,
        came_z,
        far(rate.T),
        far(residue.T),
    )

    d_weight, output = pl.pallas_call(
        last_kernel,
        out_shape=(far_f32(2 * HALF, 256), far_bf16(ROWS, 512)),
        in_specs=[whole(), whole()] + [anywhere] * 5,
        out_specs=(anywhere,) * 2,
        scratch_shapes=[
            pltpu.VMEM((4, HALF, 256), BF16),
            pltpu.VMEM((ROWS, 512), BF16),
            pltpu.VMEM((2 * HALF, 256), F32),
            pltpu.VMEM((ROWS, 512), BF16),
            pltpu.SemaphoreType.DMA((8,)),
        ],
        name="last_sums",
        **params_of(2_000_000, 4_000_000),
    )(gradient, out_sum, first_far, *second_far, near_out)

    return (output, d_query, d_key, d_value, d_weight, d_residue.T, d_rate.T, d_skip[0])


def solution(mesh):
    rows, owner = P("ctx", "tp"), P(("tp", "ctx"))
    return jax.shard_map(
        local,
        mesh=mesh,
        in_specs=(rows, rows, rows, rows, P("tp", None), P(("tp", "ctx"), None), P(("tp", "ctx"), None), owner),
        out_specs=(rows, rows, rows, rows, P("tp", "ctx"), P(("tp", "ctx"), None), P(("tp", "ctx"), None), owner),
        check_vma=False,
    )
```

```python
import functools

import jax
import jax.numpy as jnp
from jax import lax
from jax.experimental import pallas as pl
from jax.experimental.pallas import tpu as pltpu
from jax.sharding import PartitionSpec as P

F32 = jnp.float32
BF16 = jnp.bfloat16
SEQ = 4096
MODES = 16
ROWS = 256
SUB = 8
BLOCKS = 16
HALF = 512
UNROLL = 8
PACK = 24
TABLE = 2 * PACK * SUB
STATE = MODES * SUB
TERMS = 32
VMEM = 32 * 1024 * 1024
LONG = 2_000_000_000_000
SHORT = 50


def params_of(flops, nbytes):
    return dict(
        compiler_params=pltpu.CompilerParams(vmem_limit_bytes=VMEM),
        cost_estimate=pl.CostEstimate(flops=flops // SHORT, bytes_accessed=nbytes // SHORT, transcendentals=0),
    )


def whole():
    return pl.BlockSpec(memory_space=pltpu.VMEM)


def full(*shape):
    return pl.BlockSpec(shape, lambda *_: (0,) * len(shape))


def far(array):
    return pltpu.with_memory_space_constraint(array, pltpu.HBM)


def far_f32(*shape):
    return pltpu.HBM(shape, F32)


def far_bf16(*shape):
    return pltpu.HBM(shape, BF16)


def lanes(group):
    return slice(128 * group, 128 * (group + 1))


def group_rows(group):
    return pl.ds(group, ROWS, stride=SUB)


def rate_of(table, mode):
    return table[SUB * mode : SUB * (mode + 1), :]


def step_decay(table, mode):
    return jnp.exp(rate_of(table, mode) * (-1.0 / SEQ))


def block_decay(table, mode):
    return jnp.exp(rate_of(table, mode) * (-float(ROWS) / SEQ))


def mode_weight(table, mode):
    return rate_of(table, PACK + mode) * jnp.sqrt(rate_of(table, mode) * (2.0 / SEQ))


def skip_of(table):
    return rate_of(table, MODES)


def at(ref, step):
    return ref[pl.ds(pl.multiple_of(step * SUB, SUB), SUB), :]


def zeros(count):
    return tuple(jnp.zeros((SUB, 128), F32) for _ in range(count))


def tree_sum(parts):
    parts = list(parts)
    while len(parts) > 1:
        parts = [sum(parts[i : i + 2]) for i in range(0, len(parts), 2)]
    return parts[0]


def pack_kernel(rate_ref, residue_ref, skip_ref, out_ref):
    both = jnp.concatenate([rate_ref[...], residue_ref[...]], axis=1)
    last = jnp.concatenate([skip_ref[...], skip_ref[...]], axis=1)
    for j in range(BLOCKS):
        out_ref[j, :MODES] = both
        out_ref[j, MODES:] = jnp.broadcast_to(last, (PACK - MODES, 128))


def mix_kernel(
    key_in, value_in, cot_in, near_cot_in, mixed_ref, mixed_out, pair_out, key_ref, value_ref, cot_ref, sems
):
    copies = [
        pltpu.make_async_copy(key_in, key_ref, sems.at[0]),
        pltpu.make_async_copy(value_in, value_ref, sems.at[1]),
        pltpu.make_async_copy(near_cot_in, pair_out.at[1], sems.at[2]),
        pltpu.make_async_copy(cot_in, cot_ref, sems.at[3]),
    ]
    results = [
        pltpu.make_async_copy(mixed_ref, mixed_out, sems.at[4]),
        pltpu.make_async_copy(cot_ref, pair_out.at[0], sems.at[5]),
    ]
    for copy in copies:
        copy.start()
    copies[0].wait()
    copies[1].wait()
    for group in range(SUB):
        product = key_ref[:, lanes(group)].astype(F32) * value_ref[:, lanes(group)].astype(F32)
        mixed_ref[group_rows(group), :] = product.astype(BF16).astype(F32)
    results[0].start()
    copies[3].wait()
    results[1].start()
    for copy in copies[2:3] + results:
        copy.wait()


def states_kernel(mixed_ref, packed_ref, sent_ref, table):
    left = lax.broadcasted_iota(jnp.int32, (PACK, 128), 1) < 64
    for group in range(SUB):
        one, two = packed_ref[2 * group], packed_ref[2 * group + 1]
        table[pl.ds(group, PACK, stride=SUB), :] = jnp.where(left, one, pltpu.roll(two, 64, 1))
        table[pl.ds(PACK * SUB + group, PACK, stride=SUB), :] = jnp.where(left, pltpu.roll(one, 64, 1), two)
    decay = [step_decay(table, m) for m in range(MODES)]

    def body(i, held):
        for u in range(UNROLL):
            value = at(mixed_ref, i * UNROLL + u)
            held = tuple(decay[m] * held[m] + value for m in range(MODES))
        return held

    held = lax.fori_loop(0, ROWS // UNROLL, body, zeros(MODES))
    for m in range(MODES):
        state = held[m].astype(BF16)
        for j in range(BLOCKS):
            sent_ref[j, m] = state


def forward_kernel(
    own_ref, sent_ref, mixed_in, query_in, table_in, weight_in,
    conv_out, gated_out, carry_out, gated_ref, weight_ref,
    buffer, mixed_ref, query_ref, table, conv_ref, carry_ref, sems,
):
    own = own_ref[0]
    copies = [
        pltpu.make_async_copy(source, target, sems.at[i])
        for i, (source, target) in enumerate([(table_in, table), (mixed_in, mixed_ref), (query_in, query_ref)])
    ]
    weights = [
        pltpu.make_async_copy(weight_in.at[:, 512 * i : 512 * (i + 1)], weight_ref.at[i], sems.at[6 + i])
        for i in range(8)
    ]
    results = [
        pltpu.make_async_copy(source, target, sems.at[3 + i])
        for i, (source, target) in enumerate([(carry_ref, carry_out), (conv_ref, conv_out), (gated_ref, gated_out)])
    ]
    for copy in copies + weights:
        copy.start()
    copies[0].wait()
    for m in range(MODES):
        far = block_decay(table, m)
        carry = jnp.zeros((SUB, 128), F32)
        for j in range(BLOCKS - 1):
            carry = jnp.where(j < own, far * carry + sent_ref[j, m].astype(F32), carry)
        carry_ref[m] = carry
    results[0].start()
    copies[1].wait()
    decay = [step_decay(table, m) for m in range(MODES)]
    weight = [mode_weight(table, m) for m in range(MODES)]
    skip = skip_of(table)

    def body(i, held):
        for u in range(UNROLL):
            step = i * UNROLL + u
            value = at(mixed_ref, step)
            held = tuple(decay[m] * held[m] + value for m in range(MODES))
            total = tree_sum([weight[m] * held[m] for m in range(MODES)])
            buffer[pl.ds(pl.multiple_of(step * SUB, SUB), SUB), :] = total + skip * value
        return held

    lax.fori_loop(0, ROWS // UNROLL, body, tuple(carry_ref[m] for m in range(MODES)))
    copies[2].wait()
    for group in range(SUB):
        conv = buffer[group_rows(group), :].astype(BF16)
        conv_ref[:, lanes(group)] = conv
        gated_ref[:, lanes(group)] = (query_ref[:, lanes(group)].astype(F32) * conv.astype(F32)).astype(BF16)
    results[1].start()
    results[2].start()
    for copy in results + weights:
        copy.wait()


def output_kernel(gated_ref, weight_ref, out_ref, blocks, sems):
    results = [pltpu.make_async_copy(blocks.at[i], out_ref.at[i], sems.at[i]) for i in range(8)]
    for i in range(8):
        blocks[i] = jnp.dot(gated_ref[...], weight_ref[i], preferred_element_type=F32).astype(BF16)
        results[i].start()
    for result in results:
        result.wait()


def weight_kernel(index_ref, gated_ref, other_ref, *refs):
    cot_refs, other_refs = refs[:4], refs[4:8]
    along_y, along_z = refs[9:13], refs[13:15]
    gated, turned, cots, chunks, sems, out_sems = refs[15:]
    half = pl.ds(pl.multiple_of(index_ref[8] * 256, 256), 256)
    copies = [
        pltpu.make_async_copy(gated_ref, gated, sems.at[8]),
    ]
    for i in range(8):
        own = cot_refs[i // 2].at[i % 2, :, half]
        other = other_refs[i // 2].at[i % 2, :, half]
        copies.append(pltpu.make_async_copy(own, cots.at[i, :ROWS], sems.at[i]))
        copies.append(pltpu.make_async_copy(other, cots.at[i, ROWS:], sems.at[9 + i]))
    for copy in copies:
        copy.start()
    turned[:, ROWS:] = other_ref[...].T
    copies[0].wait()
    turned[:, :ROWS] = gated[...].T
    for copy in copies[1:]:
        copy.wait()
    results = []
    for z in (1, 0):
        for k in range(4):
            i = 4 * z + k
            total = jnp.dot(turned[...], cots[index_ref[i]], preferred_element_type=F32)
            chunks[i] = total.astype(BF16)
            results.append(pltpu.make_async_copy(chunks.at[i, HALF:], along_z[z].at[k], out_sems.at[i]))
            results.append(pltpu.make_async_copy(chunks.at[i, :HALF], along_y[k].at[z], out_sems.at[8 + i]))
            results[-2].start()
            results[-1].start()
    for copy in results:
        copy.wait()


def cotangent_kernel(
    came_ref, part0, part1, part2, part3, weight_ref, query_in, conv_in, mixed_in, carry_in, table_in, after_ref,
    dquery_out, dconv_out, sent_out,
    total, terms, parts, weight, query_ref, conv_ref, mixed_ref, carry_ref, table, dquery_ref, dconv_ref, sent_ref, moments, sems,
):
    copies = []
    for i in range(8):
        columns = pl.ds(pl.multiple_of(came_ref[i] * 512, 512), 512)
        part = (part0, part1, part2, part3)[i // 2].at[i % 2]
        place = slice(512 * (i % 2), 512 * (i % 2 + 1))
        copies.append(pltpu.make_async_copy(weight_ref.at[:, columns], weight.at[i // 2, :, place], sems.at[i]))
        copies.append(pltpu.make_async_copy(part, parts.at[i // 2, :, place], sems.at[8 + i]))
    later = [
        pltpu.make_async_copy(source, target, sems.at[16 + i])
        for i, (source, target) in enumerate(
            [(query_in, query_ref), (conv_in, conv_ref), (mixed_in, mixed_ref), (carry_in, carry_ref), (table_in, table)]
        )
    ]
    results = [
        pltpu.make_async_copy(source, target, sems.at[21 + i])
        for i, (source, target) in enumerate(
            [(dquery_ref, dquery_out), (dconv_ref, dconv_out), (sent_ref, sent_out)]
        )
    ]
    for copy in copies + later:
        copy.start()
    for i in range(4):
        for copy in copies[4 * i : 4 * i + 4]:
            copy.wait()
        product = lax.dot_general(parts[i], weight[i], (((1,), (1,)), ((), ())), preferred_element_type=F32)
        if i == 0:
            total[...] = product
        else:
            total[...] += product
    for copy in later:
        copy.wait()
    for group in range(SUB):
        cot = total[:, lanes(group)]
        dquery_ref[:, lanes(group)] = (cot * conv_ref[:, lanes(group)].astype(F32)).astype(BF16)
        dconv_ref[group_rows(group), :] = (cot * query_ref[:, lanes(group)].astype(F32)).astype(BF16).astype(F32)

    results[0].start()
    results[1].start()
    left = lax.broadcasted_iota(jnp.int32, (SUB, 128), 1) < 64

    def put(row, one, two):
        terms[pl.ds(row, SUB, stride=2 * TERMS), :] = jnp.where(left, one, pltpu.roll(two, 64, 1))
        terms[pl.ds(TERMS + row, SUB, stride=2 * TERMS), :] = jnp.where(left, pltpu.roll(one, 64, 1), two)

    all_decay = [step_decay(table, m) for m in range(MODES)]

    def backward(i, back):
        for u in range(UNROLL):
            value = at(dconv_ref, ROWS - 1 - (i * UNROLL + u))
            back = tuple(all_decay[m] * back[m] + value for m in range(MODES))
        return back

    back = lax.fori_loop(0, ROWS // UNROLL, backward, zeros(MODES))
    for m in range(0, MODES, 2):
        state = jnp.concatenate([back[m], back[m + 1]]).astype(BF16)
        for j in range(BLOCKS):
            sent_ref[j, SUB * m : SUB * (m + 2), :] = state
    half = MODES // 2
    for first in (0, half):
        modes = range(first, first + half)
        decay = [step_decay(table, m) for m in modes]

        def forward(i, packed):
            held, moment, first_sum, second_sum, skip_sum = packed
            for u in range(UNROLL):
                value = at(mixed_ref, i * UNROLL + u)
                cot = at(dconv_ref, i * UNROLL + u)
                past = [decay[m] * held[m] for m in range(half)]
                moment = tuple(decay[m] * moment[m] + past[m] for m in range(half))
                held = tuple(past[m] + value for m in range(half))
                first_sum = tuple(first_sum[m] + cot * held[m] for m in range(half))
                second_sum = tuple(second_sum[m] + cot * moment[m] for m in range(half))
                skip_sum = skip_sum + cot * value
            return (held, moment, first_sum, second_sum, skip_sum)

        start = (tuple(carry_ref[m] for m in modes), zeros(half), zeros(half), zeros(half), zeros(1)[0])
        held, moment, first_sum, second_sum, skip_sum = lax.fori_loop(0, ROWS // UNROLL, forward, start)

        for m in range(half):
            put(first + m, first_sum[m], second_sum[m])
            moments[first + m] = moment[m]
    for m in range(half):
        put(MODES + m, moments[m], moments[half + m])
    for row in range(MODES + half, TERMS):
        put(row, skip_sum, skip_sum)
    for j in range(BLOCKS):
        term = terms[TERMS * j : TERMS * (j + 1), :]
        sent_ref[j, STATE:, :] = term.astype(BF16)
    results[2].start()
    for result in results:
        result.wait()


def owner_sums(parts_ref, place_ref, rate_ref, residue_ref, dresidue_ref, drate_ref, dskip_ref, states):
    rate = rate_ref[...]
    residue = residue_ref[...]
    near = jnp.exp(rate * (-1.0 / SEQ))
    far = jnp.exp(rate * (-float(ROWS) / SEQ))
    scale = jnp.sqrt(rate * (2.0 / SEQ))
    half = MODES // 2
    first = jnp.zeros_like(rate)
    second = jnp.zeros_like(rate)
    skip = jnp.zeros((1, rate.shape[1]), F32)
    later = jnp.zeros_like(rate)
    for j in range(BLOCKS):
        states[STATE * j : STATE * (j + 1), :] = parts_ref[j, :STATE, :].astype(F32)
    for j in range(BLOCKS - 1, -1, -1):
        terms = parts_ref[j, STATE:, :].astype(F32)
        sums, ends = terms[0:MODES], terms[MODES : MODES + half]
        ends = jnp.concatenate([ends[:, :64], ends[:, 64:]])
        back = states[pl.ds(STATE * j + place_ref[2], MODES, stride=SUB), :]
        back = jnp.where(place_ref[3] == 0, back, pltpu.roll(back, 64, 1))[:, :64]
        first += sums[:, :64]
        second += sums[:, 64:] + near * later * ends
        later = far * later + back
        skip += terms[MODES + half : MODES + half + 1, :64]
    proj = scale * first
    dresidue_ref[...] = proj
    drate_ref[...] = residue * (0.5 * proj / rate - scale * second * (1.0 / SEQ))
    dskip_ref[...] = skip


def backward_kernel(
    own_ref, sent_ref, dconv_in, key_in, value_in, table_in, first_in, same_in, arrived_in,
    came1, came2, came3, came_z, rate_ref, residue_ref,
    dkey_out, dvalue_out, gradient_ref, output_ref, dresidue_ref, drate_ref, dskip_ref,
    dconv_ref, key_ref, value_ref, table, dkey_ref, dvalue_ref, carry_ref, buffer, blocks, arrived, states, sems,
):
    own = own_ref[0]
    copies = [
        pltpu.make_async_copy(source, target, sems.at[i])
        for i, (source, target) in enumerate(
            [
                (table_in, table),
                (dconv_in, dconv_ref),
                (key_in, key_ref),
                (value_in, value_ref),
                (first_in.at[0], blocks.at[0]),
                (same_in.at[0], blocks.at[1]),
            ]
            + [(arrived_in.at[2 * k + own_ref[1]], arrived.at[k]) for k in range(4)]
        )
    ]
    results = [
        pltpu.make_async_copy(dkey_ref, dkey_out, sems.at[10]),
        pltpu.make_async_copy(dvalue_ref, dvalue_out, sems.at[11]),
    ]
    for copy in copies:
        copy.start()
    copies[0].wait()
    for m in range(MODES):
        far = block_decay(table, m)
        carry = jnp.zeros((SUB, 128), F32)
        for j in range(BLOCKS - 1, 0, -1):
            carry = jnp.where(j > own, far * carry + sent_ref[j, SUB * m : SUB * (m + 1), :].astype(F32), carry)
        carry_ref[m] = carry
    copies[1].wait()
    decay = [step_decay(table, m) for m in range(MODES)]
    weight = [mode_weight(table, m) for m in range(MODES)]
    skip = skip_of(table)

    def body(i, held):
        for u in range(UNROLL):
            step = ROWS - 1 - (i * UNROLL + u)
            value = at(dconv_ref, step)
            held = tuple(decay[m] * held[m] + value for m in range(MODES))
            total = tree_sum([weight[m] * held[m] for m in range(MODES)])
            buffer[pl.ds(pl.multiple_of(step * SUB, SUB), SUB), :] = total + skip * value
        return held

    lax.fori_loop(0, ROWS // UNROLL, body, tuple(carry_ref[m] for m in range(MODES)))
    copies[2].wait()
    copies[3].wait()
    for group in range(SUB):
        grad = buffer[group_rows(group), :].astype(BF16).astype(F32)
        dkey_ref[:, lanes(group)] = (grad * value_ref[:, lanes(group)].astype(F32)).astype(BF16)
        dvalue_ref[:, lanes(group)] = (grad * key_ref[:, lanes(group)].astype(F32)).astype(BF16)
    for result in results:
        result.start()
    for copy in copies[4:]:
        copy.wait()
    gradient_ref[:HALF] = blocks[0].astype(F32) + sum(part[0].astype(F32) for part in (came1, came2, came3))
    gradient_ref[HALF:] = blocks[1].astype(F32) + came_z[0].astype(F32)
    output_ref[...] = sum(arrived[k].astype(F32) for k in range(4))
    owner_sums(sent_ref, own_ref, rate_ref, residue_ref, dresidue_ref, drate_ref, dskip_ref, states)
    for result in results:
        result.wait()


def add_kernel(*refs):
    out_ref = refs[-1]
    total = refs[0][...].astype(F32).reshape(out_ref.shape)
    for ref in refs[1:-2]:
        total += ref[...].astype(F32).reshape(out_ref.shape)
    out_ref[...] = total.astype(out_ref.dtype)


def stage_kernel(own_ref, *refs):
    came_y, came_z, outs = refs[:3], refs[3], refs[4:8]
    outs[0][...] = (own_ref[0].astype(F32) + sum(part[1].astype(F32) for part in came_y)).astype(BF16)
    for k in (1, 2, 3):
        outs[k][...] = (own_ref[k].astype(F32) + came_z[k].astype(F32)).astype(BF16)


def add_placed_kernel(place_ref, arrived_ref, first_ref, same_ref, after_ref, out_ref, own_ref, held, sems):
    copies = [pltpu.make_async_copy(arrived_ref.at[2 * k + place_ref[0]], held.at[k], sems.at[k]) for k in range(4)]
    copies.append(pltpu.make_async_copy(first_ref.at[1], own_ref.at[0], sems.at[4]))
    copies += [pltpu.make_async_copy(same_ref.at[k], own_ref.at[k], sems.at[4 + k]) for k in (1, 2, 3)]
    for copy in copies:
        copy.start()
    for copy in copies[:4]:
        copy.wait()
    out_ref[...] = sum(held[k].astype(F32) for k in range(4)).astype(BF16)
    for copy in copies[4:]:
        copy.wait()


def last_kernel(gradient_ref, out_sum_ref, *refs):
    parts, last_in, weight_out, output_out = refs[:4], refs[4], refs[5], refs[6]
    held, last, weight_ref, output_ref, sems = refs[7:]
    copies = [pltpu.make_async_copy(parts[i], held.at[i], sems.at[i]) for i in range(4)]
    copies.append(pltpu.make_async_copy(last_in, last, sems.at[4]))
    results = [
        pltpu.make_async_copy(weight_ref.at[:HALF], weight_out.at[:HALF], sems.at[5]),
        pltpu.make_async_copy(weight_ref.at[HALF:], weight_out.at[HALF:], sems.at[6]),
        pltpu.make_async_copy(output_ref, output_out, sems.at[7]),
    ]
    for copy in copies:
        copy.start()
    copies[0].wait()
    weight_ref[:HALF] = gradient_ref[:HALF] + held[0].astype(F32)
    results[0].start()
    for copy in copies[1:4]:
        copy.wait()
    weight_ref[HALF:] = gradient_ref[HALF:] + sum(held[i].astype(F32) for i in (1, 2, 3))
    results[1].start()
    copies[4].wait()
    output_ref[...] = (out_sum_ref[...] + last[...].astype(F32)).astype(BF16)
    results[2].start()
    for copy in results:
        copy.wait()


def f32(*shape):
    return jax.ShapeDtypeStruct(shape, F32)


def bf16(*shape):
    return jax.ShapeDtypeStruct(shape, BF16)


def exchange(array, axis, groups=None):
    return lax.all_to_all(array, axis, split_axis=0, concat_axis=0, tiled=True, axis_index_groups=groups)


def to_all(array, axis, count):
    return exchange(jnp.broadcast_to(array[None], (count,) + array.shape), axis)


MOVES = [(k, z) for k in range(4) for z in range(2)]


def shift_x(k, z=0):
    return [(2 * x + p, 2 * ((x + k) % 4) + (p + z) % 2) for x in range(4) for p in range(2)]


def shift_y(k):
    return [(8 * z + 2 * y + c, 8 * z + 2 * ((y + k) % 4) + c) for z in range(2) for y in range(4) for c in range(2)]


def local(query, key_part, value_part, out_cotangent, w_out, residue, rate, skip):
    own = lax.axis_index("ctx")
    own_array = own.reshape(1).astype(jnp.int32)
    core, own_y, own_z = own % 2, own // 2 % 4, own // 8
    place = lax.axis_index("tp")
    place_x, place_z = place // 2, place % 2
    smem = pl.BlockSpec(memory_space=pltpu.SMEM)
    core_swap = [(i, i ^ 1) for i in range(BLOCKS)]
    far_swap = [(i, i ^ 8) for i in range(BLOCKS)]
    hbm = pl.BlockSpec(memory_space=pltpu.HBM)

    steps = jnp.arange(8, dtype=jnp.int32)
    came = ((place_x - steps // 2) % 4) * 2 + (place_z + steps) % 2
    chip = ((own_z + steps // 4) % 2) * 4 + (own_y + steps) % 4
    index = 2 * ((place_x - chip // 2) % 4) + (chip - place_z) % 2
    core_array = core.reshape(1).astype(jnp.int32)

    packed = pl.pallas_call(
        pack_kernel,
        grid=(1,),
        out_shape=far_f32(BLOCKS, PACK, 128),
        in_specs=[full(MODES, 64), full(MODES, 64), full(1, 64)],
        out_specs=full(BLOCKS, PACK, 128),
        name="pack_parameters",
        **params_of(100_000, 200_000),
    )(far(rate.T), far(residue.T), far(skip[None]))
    packed = exchange(packed, "ctx")
    near_cot = lax.ppermute(out_cotangent, "tp", shift_x(0, 1))
    mixed_near, mixed, cot_pair = pl.pallas_call(
        mix_kernel,
        out_shape=(f32(ROWS * SUB, 128), far_f32(ROWS * SUB, 128), far_bf16(2, ROWS, 512)),
        in_specs=[pl.BlockSpec(memory_space=pl.ANY)] * 4,
        out_specs=(whole(), pl.BlockSpec(memory_space=pl.ANY), pl.BlockSpec(memory_space=pl.ANY)),
        scratch_shapes=[
            pltpu.VMEM((ROWS, 1024), BF16),
            pltpu.VMEM((ROWS, 1024), BF16),
            pltpu.VMEM((ROWS, 512), BF16),
            pltpu.SemaphoreType.DMA((6,)),
        ],
        name="mix_inputs",
        **params_of(100_000_000, 3_000_000),
    )(far(key_part), far(value_part), far(out_cotangent), near_cot)
    cot_parts = [cot_pair] + [lax.ppermute(cot_pair, "tp", shift_x(k)) for k in (1, 2, 3)]

    sent, table = pl.pallas_call(
        states_kernel,
        grid=(1,),
        out_shape=(far_bf16(BLOCKS, MODES, SUB, 128), far_f32(TABLE, 128)),
        in_specs=[whole()] * 2,
        out_specs=(full(BLOCKS, MODES, SUB, 128), full(TABLE, 128)),
        name="forward_states",
        **params_of(3_000_000_000, 4_000_000),
    )(mixed_near, packed)
    sent = exchange(sent, "ctx")

    anywhere = pl.BlockSpec(memory_space=pl.ANY)
    conv_out, gated, carry, gated_near, weight_near = pl.pallas_call(
        forward_kernel,
        out_shape=(
            far_bf16(ROWS, 1024),
            far_bf16(ROWS, 1024),
            far_f32(MODES, SUB, 128),
            bf16(ROWS, 1024),
            bf16(8, 1024, 512),
        ),
        in_specs=[smem, whole(), anywhere, anywhere, anywhere, anywhere],
        out_specs=(anywhere, anywhere, anywhere, whole(), whole()),
        scratch_shapes=[
            pltpu.VMEM((ROWS * SUB, 128), F32),
            pltpu.VMEM((ROWS * SUB, 128), F32),
            pltpu.VMEM((ROWS, 1024), BF16),
            pltpu.VMEM((TABLE, 128), F32),
            pltpu.VMEM((ROWS, 1024), BF16),
            pltpu.VMEM((MODES, SUB, 128), F32),
            pltpu.SemaphoreType.DMA((14,)),
        ],
        name="forward_conv",
        **params_of(5_000_000_000, 4_000_000),
    )(own_array, sent, far(mixed), far(query), far(table), far(w_out))

    other_gated = lax.ppermute(gated, "ctx", core_swap)
    partial_out = pl.pallas_call(
        output_kernel,
        out_shape=far_bf16(8, ROWS, 512),
        in_specs=[whole(), whole()],
        out_specs=anywhere,
        scratch_shapes=[pltpu.VMEM((8, ROWS, 512), BF16), pltpu.SemaphoreType.DMA((8,))],
        name="output_projection",
        **params_of(2_147_483_648, 11_000_000),
    )(gated_near, weight_near)
    other_parts = [lax.ppermute(part, "ctx", core_swap) for part in cot_parts]

    *by_y, same_z, other_z = pl.pallas_call(
        weight_kernel,
        out_shape=(far_bf16(2, HALF, 256),) * 4 + (far_bf16(4, HALF, 256),) * 2,
        in_specs=[smem, anywhere, whole()] + [anywhere] * 9,
        out_specs=(anywhere,) * 6,
        scratch_shapes=[
            pltpu.VMEM((ROWS, 1024), BF16),
            pltpu.VMEM((1024, 2 * ROWS), BF16),
            pltpu.VMEM((8, 2 * ROWS, 256), BF16),
            pltpu.VMEM((8, 1024, 256), BF16),
            pltpu.SemaphoreType.DMA((17,)),
            pltpu.SemaphoreType.DMA((16,)),
        ],
        name="projection_gradient",
        **params_of(2_147_483_648, 8_000_000),
    )(jnp.concatenate([index, core_array]), far(gated), other_gated, *[far(part) for part in cot_parts], *other_parts, far(partial_out))
    came_z = lax.ppermute(other_z, "ctx", far_swap)
    came_y = [lax.ppermute(by_y[k], "ctx", shift_y(k)) for k in (1, 2, 3)]

    lines = [[2 * x + z for x in range(4)] for z in range(2)]
    arrived = exchange(partial_out.reshape(4, 2, ROWS, 512), "tp", lines).reshape(8, ROWS, 512)

    d_query, d_conv, payload = pl.pallas_call(
        cotangent_kernel,
        out_shape=(far_bf16(ROWS, 1024), far_f32(ROWS * SUB, 128), far_bf16(BLOCKS, STATE + TERMS, 128)),
        in_specs=[smem] + [anywhere] * 11,
        out_specs=(anywhere,) * 3,
        scratch_shapes=[
            pltpu.VMEM((ROWS, 1024), F32),
            pltpu.VMEM((BLOCKS * TERMS, 128), F32),
            pltpu.VMEM((4, ROWS, 1024), BF16),
            pltpu.VMEM((4, 1024, 1024), BF16),
            pltpu.VMEM((ROWS, 1024), BF16),
            pltpu.VMEM((ROWS, 1024), BF16),
            pltpu.VMEM((ROWS * SUB, 128), F32),
            pltpu.VMEM((MODES, SUB, 128), F32),
            pltpu.VMEM((TABLE, 128), F32),
            pltpu.VMEM((ROWS, 1024), BF16),
            pltpu.VMEM((ROWS * SUB, 128), F32),
            pltpu.VMEM((BLOCKS, STATE + TERMS, 128), BF16),
            pltpu.VMEM((MODES, SUB, 128), F32),
            pltpu.SemaphoreType.DMA((24,)),
        ],
        name="cotangent_states",
        **params_of(14_000_000_000, 13_000_000),
    )(came, *[far(part) for part in cot_parts], far(w_out), far(query), far(conv_out), far(mixed), far(carry), far(table), far(other_z))
    received = exchange(payload, "ctx")

    near_sum, own_blocks = pl.pallas_call(
        add_placed_kernel,
        out_shape=(bf16(ROWS, 512), bf16(4, HALF, 256)),
        in_specs=[smem] + [anywhere] * 4,
        out_specs=(whole(), whole()),
        scratch_shapes=[pltpu.VMEM((4, ROWS, 512), BF16), pltpu.SemaphoreType.DMA((8,))],
        name="sum_output",
        **params_of(1_000_000, 2_000_000),
    )(
        (1 - place_z).reshape(1).astype(jnp.int32),
        far(arrived),
        far(by_y[0]),
        far(same_z),
        far(payload),
    )
    near_out = lax.ppermute(near_sum, "tp", shift_x(0, 1))

    first_far, *second_far = pl.pallas_call(
        stage_kernel,
        out_shape=(bf16(HALF, 256),) * 4,
        in_specs=[whole()] * 5,
        out_specs=(whole(),) * 4,
        name="sum_stage",
        **params_of(LONG, 2_000_000),
    )(own_blocks, *came_y, came_z)
    first_far = lax.ppermute(first_far, "ctx", far_swap)
    second_far = [lax.ppermute(second_far[k - 1], "ctx", shift_y(k)) for k in (1, 2, 3)]

    d_key, d_value, gradient, out_sum, d_residue, d_rate, d_skip = pl.pallas_call(
        backward_kernel,
        grid=(1,),
        out_shape=(
            far_bf16(ROWS, 1024),
            far_bf16(ROWS, 1024),
            f32(2 * HALF, 256),
            f32(ROWS, 512),
            f32(MODES, 64),
            f32(MODES, 64),
            f32(1, 64),
        ),
        in_specs=[smem, whole()] + [anywhere] * 7 + [whole()] * 4 + [full(MODES, 64)] * 2,
        out_specs=(anywhere, anywhere, whole(), whole(), full(MODES, 64), full(MODES, 64), full(1, 64)),
        scratch_shapes=[
            pltpu.VMEM((ROWS * SUB, 128), F32),
            pltpu.VMEM((ROWS, 1024), BF16),
            pltpu.VMEM((ROWS, 1024), BF16),
            pltpu.VMEM((TABLE, 128), F32),
            pltpu.VMEM((ROWS, 1024), BF16),
            pltpu.VMEM((ROWS, 1024), BF16),
            pltpu.VMEM((MODES, SUB, 128), F32),
            pltpu.VMEM((ROWS * SUB, 128), F32),
            pltpu.VMEM((2, HALF, 256), BF16),
            pltpu.VMEM((4, ROWS, 512), BF16),
            pltpu.VMEM((BLOCKS * STATE, 128), F32),
            pltpu.SemaphoreType.DMA((12,)),
        ],
        name="backward_conv",
        **params_of(5_000_000_000, 4_000_000),
    )(
        jnp.stack([own, place_z, own // 2, core]).astype(jnp.int32),
        received,
        far(d_conv),
        far(key_part),
        far(value_part),
        far(table),
        far(by_y[0]),
        far(same_z),
        far(arrived),
        *came_y,
        came_z,
        far(rate.T),
        far(residue.T),
    )

    d_weight, output = pl.pallas_call(
        last_kernel,
        out_shape=(far_f32(2 * HALF, 256), far_bf16(ROWS, 512)),
        in_specs=[whole(), whole()] + [anywhere] * 5,
        out_specs=(anywhere,) * 2,
        scratch_shapes=[
            pltpu.VMEM((4, HALF, 256), BF16),
            pltpu.VMEM((ROWS, 512), BF16),
            pltpu.VMEM((2 * HALF, 256), F32),
            pltpu.VMEM((ROWS, 512), BF16),
            pltpu.SemaphoreType.DMA((8,)),
        ],
        name="last_sums",
        **params_of(2_000_000, 4_000_000),
    )(gradient, out_sum, first_far, *second_far, near_out)

    return (output, d_query, d_key, d_value, d_weight, d_residue.T, d_rate.T, d_skip[0])


def solution(mesh):
    rows, owner = P("ctx", "tp"), P(("tp", "ctx"))
    return jax.shard_map(
        local,
        mesh=mesh,
        in_specs=(rows, rows, rows, rows, P("tp", None), P(("tp", "ctx"), None), P(("tp", "ctx"), None), owner),
        out_specs=(rows, rows, rows, rows, P("tp", "ctx"), P(("tp", "ctx"), None), P(("tp", "ctx"), None), owner),
        check_vma=False,
    )
```

```python
import functools

import jax
import jax.numpy as jnp
from jax import lax
from jax.experimental import pallas as pl
from jax.experimental.pallas import tpu as pltpu
from jax.sharding import PartitionSpec as P

F32 = jnp.float32
BF16 = jnp.bfloat16
SEQ = 4096
MODES = 16
ROWS = 256
SUB = 8
BLOCKS = 16
HALF = 512
UNROLL = 16
PACK = 24
TABLE = 2 * PACK * SUB
STATE = MODES * SUB
TERMS = 32
VMEM = 32 * 1024 * 1024
LONG = 2_000_000_000_000
SHORT = 50


def params_of(flops, nbytes):
    return dict(
        compiler_params=pltpu.CompilerParams(vmem_limit_bytes=VMEM),
        cost_estimate=pl.CostEstimate(flops=flops // SHORT, bytes_accessed=nbytes // SHORT, transcendentals=0),
    )


def whole():
    return pl.BlockSpec(memory_space=pltpu.VMEM)


def full(*shape):
    return pl.BlockSpec(shape, lambda *_: (0,) * len(shape))


def far(array):
    return pltpu.with_memory_space_constraint(array, pltpu.HBM)


def far_f32(*shape):
    return pltpu.HBM(shape, F32)


def far_bf16(*shape):
    return pltpu.HBM(shape, BF16)


def lanes(group):
    return slice(128 * group, 128 * (group + 1))


def group_rows(group):
    return pl.ds(group, ROWS, stride=SUB)


def rate_of(table, mode):
    return table[SUB * mode : SUB * (mode + 1), :]


def step_decay(table, mode):
    return jnp.exp(rate_of(table, mode) * (-1.0 / SEQ))


def block_decay(table, mode):
    return jnp.exp(rate_of(table, mode) * (-float(ROWS) / SEQ))


def mode_weight(table, mode):
    return rate_of(table, PACK + mode) * jnp.sqrt(rate_of(table, mode) * (2.0 / SEQ))


def skip_of(table):
    return rate_of(table, MODES)


def at(ref, step):
    return ref[pl.ds(pl.multiple_of(step * SUB, SUB), SUB), :]


def zeros(count):
    return tuple(jnp.zeros((SUB, 128), F32) for _ in range(count))


def tree_sum(parts):
    parts = list(parts)
    while len(parts) > 1:
        parts = [sum(parts[i : i + 2]) for i in range(0, len(parts), 2)]
    return parts[0]


def pack_kernel(rate_ref, residue_ref, skip_ref, out_ref):
    both = jnp.concatenate([rate_ref[...], residue_ref[...]], axis=1)
    last = jnp.concatenate([skip_ref[...], skip_ref[...]], axis=1)
    for j in range(BLOCKS):
        out_ref[j, :MODES] = both
        out_ref[j, MODES:] = jnp.broadcast_to(last, (PACK - MODES, 128))


def mix_kernel(
    key_in, value_in, cot_in, near_cot_in, mixed_ref, mixed_out, pair_out, key_ref, value_ref, cot_ref, sems
):
    copies = [
        pltpu.make_async_copy(key_in, key_ref, sems.at[0]),
        pltpu.make_async_copy(value_in, value_ref, sems.at[1]),
        pltpu.make_async_copy(near_cot_in, pair_out.at[1], sems.at[2]),
        pltpu.make_async_copy(cot_in, cot_ref, sems.at[3]),
    ]
    results = [
        pltpu.make_async_copy(mixed_ref, mixed_out, sems.at[4]),
        pltpu.make_async_copy(cot_ref, pair_out.at[0], sems.at[5]),
    ]
    for copy in copies:
        copy.start()
    copies[0].wait()
    copies[1].wait()
    for group in range(SUB):
        product = key_ref[:, lanes(group)].astype(F32) * value_ref[:, lanes(group)].astype(F32)
        mixed_ref[group_rows(group), :] = product.astype(BF16).astype(F32)
    results[0].start()
    copies[3].wait()
    results[1].start()
    for copy in copies[2:3] + results:
        copy.wait()


def states_kernel(mixed_ref, packed_ref, sent_ref, table):
    left = lax.broadcasted_iota(jnp.int32, (PACK, 128), 1) < 64
    for group in range(SUB):
        one, two = packed_ref[2 * group], packed_ref[2 * group + 1]
        table[pl.ds(group, PACK, stride=SUB), :] = jnp.where(left, one, pltpu.roll(two, 64, 1))
        table[pl.ds(PACK * SUB + group, PACK, stride=SUB), :] = jnp.where(left, pltpu.roll(one, 64, 1), two)
    decay = [step_decay(table, m) for m in range(MODES)]

    def body(i, held):
        for u in range(UNROLL):
            value = at(mixed_ref, i * UNROLL + u)
            held = tuple(decay[m] * held[m] + value for m in range(MODES))
        return held

    held = lax.fori_loop(0, ROWS // UNROLL, body, zeros(MODES))
    for m in range(0, MODES, 2):
        state = jnp.concatenate([held[m], held[m + 1]]).astype(BF16)
        for j in range(BLOCKS):
            sent_ref[j, SUB * m : SUB * (m + 2), :] = state


def forward_kernel(
    own_ref, sent_ref, mixed_in, query_in, table_in, weight_in,
    conv_out, gated_out, carry_out, gated_ref, weight_ref,
    buffer, mixed_ref, query_ref, table, conv_ref, carry_ref, sems,
):
    own = own_ref[0]
    copies = [
        pltpu.make_async_copy(source, target, sems.at[i])
        for i, (source, target) in enumerate([(table_in, table), (mixed_in, mixed_ref), (query_in, query_ref)])
    ]
    weights = [
        pltpu.make_async_copy(weight_in.at[:, 512 * i : 512 * (i + 1)], weight_ref.at[i], sems.at[6 + i])
        for i in range(8)
    ]
    results = [
        pltpu.make_async_copy(source, target, sems.at[3 + i])
        for i, (source, target) in enumerate([(carry_ref, carry_out), (conv_ref, conv_out), (gated_ref, gated_out)])
    ]
    for copy in copies + weights:
        copy.start()
    copies[0].wait()
    for m in range(0, MODES, 2):
        decays = jnp.concatenate([block_decay(table, m), block_decay(table, m + 1)])
        carry = jnp.zeros((2 * SUB, 128), F32)
        for j in range(BLOCKS - 1):
            state = sent_ref[j, SUB * m : SUB * (m + 2), :].astype(F32)
            carry = jnp.where(j < own, decays * carry + state, carry)
        carry_ref[m] = carry[:SUB]
        carry_ref[m + 1] = carry[SUB:]
    results[0].start()
    copies[1].wait()
    decay = [step_decay(table, m) for m in range(MODES)]
    weight = [mode_weight(table, m) for m in range(MODES)]
    skip = skip_of(table)

    def body(i, held):
        for u in range(UNROLL):
            step = i * UNROLL + u
            value = at(mixed_ref, step)
            held = tuple(decay[m] * held[m] + value for m in range(MODES))
            total = tree_sum([weight[m] * held[m] for m in range(MODES)])
            buffer[pl.ds(pl.multiple_of(step * SUB, SUB), SUB), :] = total + skip * value
        return held

    lax.fori_loop(0, ROWS // UNROLL, body, tuple(carry_ref[m] for m in range(MODES)))
    copies[2].wait()
    for group in range(SUB):
        conv = buffer[group_rows(group), :].astype(BF16)
        conv_ref[:, lanes(group)] = conv
        gated_ref[:, lanes(group)] = (query_ref[:, lanes(group)].astype(F32) * conv.astype(F32)).astype(BF16)
    results[1].start()
    results[2].start()
    for copy in results + weights:
        copy.wait()


def output_kernel(gated_ref, weight_ref, out_ref, blocks, sems):
    results = [pltpu.make_async_copy(blocks.at[i], out_ref.at[i], sems.at[i]) for i in range(8)]
    for i in range(8):
        blocks[i] = jnp.dot(gated_ref[...], weight_ref[i], preferred_element_type=F32).astype(BF16)
        results[i].start()
    for result in results:
        result.wait()


def weight_kernel(index_ref, gated_ref, other_ref, *refs):
    cot_refs, other_refs = refs[:4], refs[4:8]
    along_y, along_z = refs[9:13], refs[13:15]
    gated, turned, cots, chunks, sems, out_sems = refs[15:]
    half = pl.ds(pl.multiple_of(index_ref[8] * 256, 256), 256)
    copies = [
        pltpu.make_async_copy(gated_ref, gated, sems.at[8]),
    ]
    for i in range(8):
        own = cot_refs[i // 2].at[i % 2, :, half]
        other = other_refs[i // 2].at[i % 2, :, half]
        copies.append(pltpu.make_async_copy(own, cots.at[i, :ROWS], sems.at[i]))
        copies.append(pltpu.make_async_copy(other, cots.at[i, ROWS:], sems.at[9 + i]))
    for copy in copies:
        copy.start()
    turned[:, ROWS:] = other_ref[...].T
    copies[0].wait()
    turned[:, :ROWS] = gated[...].T
    for copy in copies[1:]:
        copy.wait()
    results = []
    for z in (1, 0):
        for k in range(4):
            i = 4 * z + k
            total = jnp.dot(turned[...], cots[index_ref[i]], preferred_element_type=F32)
            chunks[i] = total.astype(BF16)
            results.append(pltpu.make_async_copy(chunks.at[i, HALF:], along_z[z].at[k], out_sems.at[i]))
            results.append(pltpu.make_async_copy(chunks.at[i, :HALF], along_y[k].at[z], out_sems.at[8 + i]))
            results[-2].start()
            results[-1].start()
    for copy in results:
        copy.wait()


def cotangent_kernel(
    came_ref, part0, part1, part2, part3, weight_ref, query_in, conv_in, mixed_in, carry_in, table_in, after_ref,
    dquery_out, dconv_out, sent_out,
    total, terms, parts, weight, query_ref, conv_ref, mixed_ref, carry_ref, table, dquery_ref, dconv_ref, sent_ref, moments, sems,
):
    copies = []
    for i in range(8):
        columns = pl.ds(pl.multiple_of(came_ref[i] * 512, 512), 512)
        part = (part0, part1, part2, part3)[i // 2].at[i % 2]
        place = slice(512 * (i % 2), 512 * (i % 2 + 1))
        copies.append(pltpu.make_async_copy(weight_ref.at[:, columns], weight.at[i // 2, :, place], sems.at[i]))
        copies.append(pltpu.make_async_copy(part, parts.at[i // 2, :, place], sems.at[8 + i]))
    later = [
        pltpu.make_async_copy(source, target, sems.at[16 + i])
        for i, (source, target) in enumerate(
            [(query_in, query_ref), (conv_in, conv_ref), (mixed_in, mixed_ref), (carry_in, carry_ref), (table_in, table)]
        )
    ]
    results = [
        pltpu.make_async_copy(source, target, sems.at[21 + i])
        for i, (source, target) in enumerate(
            [(dquery_ref, dquery_out), (dconv_ref, dconv_out), (sent_ref, sent_out)]
        )
    ]
    for copy in copies + later:
        copy.start()
    for i in range(4):
        for copy in copies[4 * i : 4 * i + 4]:
            copy.wait()
        product = lax.dot_general(parts[i], weight[i], (((1,), (1,)), ((), ())), preferred_element_type=F32)
        if i == 0:
            total[...] = product
        else:
            total[...] += product
    for copy in later:
        copy.wait()
    for group in range(SUB):
        cot = total[:, lanes(group)]
        dquery_ref[:, lanes(group)] = (cot * conv_ref[:, lanes(group)].astype(F32)).astype(BF16)
        dconv_ref[group_rows(group), :] = (cot * query_ref[:, lanes(group)].astype(F32)).astype(BF16).astype(F32)

    results[0].start()
    results[1].start()
    left = lax.broadcasted_iota(jnp.int32, (SUB, 128), 1) < 64

    def put(row, one, two):
        terms[pl.ds(row, SUB, stride=2 * TERMS), :] = jnp.where(left, one, pltpu.roll(two, 64, 1))
        terms[pl.ds(TERMS + row, SUB, stride=2 * TERMS), :] = jnp.where(left, pltpu.roll(one, 64, 1), two)

    all_decay = [step_decay(table, m) for m in range(MODES)]

    def backward(i, back):
        for u in range(UNROLL):
            value = at(dconv_ref, ROWS - 1 - (i * UNROLL + u))
            back = tuple(all_decay[m] * back[m] + value for m in range(MODES))
        return back

    back = lax.fori_loop(0, ROWS // UNROLL, backward, zeros(MODES))
    for m in range(0, MODES, 2):
        state = jnp.concatenate([back[m], back[m + 1]]).astype(BF16)
        for j in range(BLOCKS):
            sent_ref[j, SUB * m : SUB * (m + 2), :] = state
    half = MODES // 2
    for first in (0, half):
        modes = range(first, first + half)
        decay = [step_decay(table, m) for m in modes]

        def forward(i, packed):
            held, moment, first_sum, second_sum, skip_sum = packed
            for u in range(UNROLL):
                value = at(mixed_ref, i * UNROLL + u)
                cot = at(dconv_ref, i * UNROLL + u)
                past = [decay[m] * held[m] for m in range(half)]
                moment = tuple(decay[m] * moment[m] + past[m] for m in range(half))
                held = tuple(past[m] + value for m in range(half))
                first_sum = tuple(first_sum[m] + cot * held[m] for m in range(half))
                second_sum = tuple(second_sum[m] + cot * moment[m] for m in range(half))
                skip_sum = skip_sum + cot * value
            return (held, moment, first_sum, second_sum, skip_sum)

        start = (tuple(carry_ref[m] for m in modes), zeros(half), zeros(half), zeros(half), zeros(1)[0])
        held, moment, first_sum, second_sum, skip_sum = lax.fori_loop(0, ROWS // UNROLL, forward, start)

        for m in range(half):
            put(first + m, first_sum[m], second_sum[m])
            moments[first + m] = moment[m]
    for m in range(half):
        put(MODES + m, moments[m], moments[half + m])
    for row in range(MODES + half, TERMS):
        put(row, skip_sum, skip_sum)
    for j in range(BLOCKS):
        term = terms[TERMS * j : TERMS * (j + 1), :]
        sent_ref[j, STATE:, :] = term.astype(BF16)
    results[2].start()
    for result in results:
        result.wait()


def owner_sums(parts_ref, place_ref, rate_ref, residue_ref, dresidue_ref, drate_ref, dskip_ref, states):
    rate = rate_ref[...]
    residue = residue_ref[...]
    near = jnp.exp(rate * (-1.0 / SEQ))
    far = jnp.exp(rate * (-float(ROWS) / SEQ))
    scale = jnp.sqrt(rate * (2.0 / SEQ))
    half = MODES // 2
    first = jnp.zeros_like(rate)
    second = jnp.zeros_like(rate)
    skip = jnp.zeros((1, rate.shape[1]), F32)
    later = jnp.zeros_like(rate)
    for j in range(BLOCKS):
        states[STATE * j : STATE * (j + 1), :] = parts_ref[j, :STATE, :].astype(F32)
    for j in range(BLOCKS - 1, -1, -1):
        terms = parts_ref[j, STATE:, :].astype(F32)
        sums, ends = terms[0:MODES], terms[MODES : MODES + half]
        ends = jnp.concatenate([ends[:, :64], ends[:, 64:]])
        back = states[pl.ds(STATE * j + place_ref[2], MODES, stride=SUB), :]
        back = jnp.where(place_ref[3] == 0, back, pltpu.roll(back, 64, 1))[:, :64]
        first += sums[:, :64]
        second += sums[:, 64:] + near * later * ends
        later = far * later + back
        skip += terms[MODES + half : MODES + half + 1, :64]
    proj = scale * first
    dresidue_ref[...] = proj
    drate_ref[...] = residue * (0.5 * proj / rate - scale * second * (1.0 / SEQ))
    dskip_ref[...] = skip


def backward_kernel(
    own_ref, sent_ref, dconv_in, key_in, value_in, table_in, first_in, same_in, arrived_in,
    came1, came2, came3, came_z, rate_ref, residue_ref,
    dkey_out, dvalue_out, gradient_ref, output_ref, dresidue_ref, drate_ref, dskip_ref,
    dconv_ref, key_ref, value_ref, table, dkey_ref, dvalue_ref, carry_ref, buffer, blocks, arrived, states, sems,
):
    own = own_ref[0]
    copies = [
        pltpu.make_async_copy(source, target, sems.at[i])
        for i, (source, target) in enumerate(
            [
                (table_in, table),
                (dconv_in, dconv_ref),
                (key_in, key_ref),
                (value_in, value_ref),
                (first_in.at[0], blocks.at[0]),
                (same_in.at[0], blocks.at[1]),
            ]
            + [(arrived_in.at[2 * k + own_ref[1]], arrived.at[k]) for k in range(4)]
        )
    ]
    results = [
        pltpu.make_async_copy(dkey_ref, dkey_out, sems.at[10]),
        pltpu.make_async_copy(dvalue_ref, dvalue_out, sems.at[11]),
    ]
    for copy in copies:
        copy.start()
    copies[0].wait()
    for m in range(0, MODES, 2):
        decays = jnp.concatenate([block_decay(table, m), block_decay(table, m + 1)])
        carry = jnp.zeros((2 * SUB, 128), F32)
        for j in range(BLOCKS - 1, 0, -1):
            state = sent_ref[j, SUB * m : SUB * (m + 2), :].astype(F32)
            carry = jnp.where(j > own, decays * carry + state, carry)
        carry_ref[m] = carry[:SUB]
        carry_ref[m + 1] = carry[SUB:]
    copies[1].wait()
    decay = [step_decay(table, m) for m in range(MODES)]
    weight = [mode_weight(table, m) for m in range(MODES)]
    skip = skip_of(table)

    def body(i, held):
        for u in range(UNROLL):
            step = ROWS - 1 - (i * UNROLL + u)
            value = at(dconv_ref, step)
            held = tuple(decay[m] * held[m] + value for m in range(MODES))
            total = tree_sum([weight[m] * held[m] for m in range(MODES)])
            buffer[pl.ds(pl.multiple_of(step * SUB, SUB), SUB), :] = total + skip * value
        return held

    lax.fori_loop(0, ROWS // UNROLL, body, tuple(carry_ref[m] for m in range(MODES)))
    copies[2].wait()
    copies[3].wait()
    for group in range(SUB):
        grad = buffer[group_rows(group), :].astype(BF16).astype(F32)
        dkey_ref[:, lanes(group)] = (grad * value_ref[:, lanes(group)].astype(F32)).astype(BF16)
        dvalue_ref[:, lanes(group)] = (grad * key_ref[:, lanes(group)].astype(F32)).astype(BF16)
    for result in results:
        result.start()
    for copy in copies[4:]:
        copy.wait()
    gradient_ref[:HALF] = blocks[0].astype(F32) + sum(part[0].astype(F32) for part in (came1, came2, came3))
    gradient_ref[HALF:] = blocks[1].astype(F32) + came_z[0].astype(F32)
    output_ref[...] = sum(arrived[k].astype(F32) for k in range(4))
    owner_sums(sent_ref, own_ref, rate_ref, residue_ref, dresidue_ref, drate_ref, dskip_ref, states)
    for result in results:
        result.wait()


def add_kernel(*refs):
    out_ref = refs[-1]
    total = refs[0][...].astype(F32).reshape(out_ref.shape)
    for ref in refs[1:-2]:
        total += ref[...].astype(F32).reshape(out_ref.shape)
    out_ref[...] = total.astype(out_ref.dtype)


def stage_kernel(own_ref, *refs):
    came_y, came_z, outs = refs[:3], refs[3], refs[4:8]
    outs[0][...] = (own_ref[0].astype(F32) + sum(part[1].astype(F32) for part in came_y)).astype(BF16)
    for k in (1, 2, 3):
        outs[k][...] = (own_ref[k].astype(F32) + came_z[k].astype(F32)).astype(BF16)


def add_placed_kernel(place_ref, arrived_ref, first_ref, same_ref, after_ref, out_ref, own_ref, held, sems):
    copies = [pltpu.make_async_copy(arrived_ref.at[2 * k + place_ref[0]], held.at[k], sems.at[k]) for k in range(4)]
    copies.append(pltpu.make_async_copy(first_ref.at[1], own_ref.at[0], sems.at[4]))
    copies += [pltpu.make_async_copy(same_ref.at[k], own_ref.at[k], sems.at[4 + k]) for k in (1, 2, 3)]
    for copy in copies:
        copy.start()
    for copy in copies[:4]:
        copy.wait()
    out_ref[...] = sum(held[k].astype(F32) for k in range(4)).astype(BF16)
    for copy in copies[4:]:
        copy.wait()


def last_kernel(gradient_ref, out_sum_ref, *refs):
    parts, last_in, weight_out, output_out = refs[:4], refs[4], refs[5], refs[6]
    held, last, weight_ref, output_ref, sems = refs[7:]
    copies = [pltpu.make_async_copy(parts[i], held.at[i], sems.at[i]) for i in range(4)]
    copies.append(pltpu.make_async_copy(last_in, last, sems.at[4]))
    results = [
        pltpu.make_async_copy(weight_ref.at[:HALF], weight_out.at[:HALF], sems.at[5]),
        pltpu.make_async_copy(weight_ref.at[HALF:], weight_out.at[HALF:], sems.at[6]),
        pltpu.make_async_copy(output_ref, output_out, sems.at[7]),
    ]
    for copy in copies:
        copy.start()
    copies[0].wait()
    weight_ref[:HALF] = gradient_ref[:HALF] + held[0].astype(F32)
    results[0].start()
    for copy in copies[1:4]:
        copy.wait()
    weight_ref[HALF:] = gradient_ref[HALF:] + sum(held[i].astype(F32) for i in (1, 2, 3))
    results[1].start()
    copies[4].wait()
    output_ref[...] = (out_sum_ref[...] + last[...].astype(F32)).astype(BF16)
    results[2].start()
    for copy in results:
        copy.wait()


def f32(*shape):
    return jax.ShapeDtypeStruct(shape, F32)


def bf16(*shape):
    return jax.ShapeDtypeStruct(shape, BF16)


def exchange(array, axis, groups=None):
    return lax.all_to_all(array, axis, split_axis=0, concat_axis=0, tiled=True, axis_index_groups=groups)


def to_all(array, axis, count):
    return exchange(jnp.broadcast_to(array[None], (count,) + array.shape), axis)


MOVES = [(k, z) for k in range(4) for z in range(2)]


def shift_x(k, z=0):
    return [(2 * x + p, 2 * ((x + k) % 4) + (p + z) % 2) for x in range(4) for p in range(2)]


def shift_y(k):
    return [(8 * z + 2 * y + c, 8 * z + 2 * ((y + k) % 4) + c) for z in range(2) for y in range(4) for c in range(2)]


def local(query, key_part, value_part, out_cotangent, w_out, residue, rate, skip):
    own = lax.axis_index("ctx")
    own_array = own.reshape(1).astype(jnp.int32)
    core, own_y, own_z = own % 2, own // 2 % 4, own // 8
    place = lax.axis_index("tp")
    place_x, place_z = place // 2, place % 2
    smem = pl.BlockSpec(memory_space=pltpu.SMEM)
    core_swap = [(i, i ^ 1) for i in range(BLOCKS)]
    far_swap = [(i, i ^ 8) for i in range(BLOCKS)]
    hbm = pl.BlockSpec(memory_space=pltpu.HBM)

    steps = jnp.arange(8, dtype=jnp.int32)
    came = ((place_x - steps // 2) % 4) * 2 + (place_z + steps) % 2
    chip = ((own_z + steps // 4) % 2) * 4 + (own_y + steps) % 4
    index = 2 * ((place_x - chip // 2) % 4) + (chip - place_z) % 2
    core_array = core.reshape(1).astype(jnp.int32)

    packed = pl.pallas_call(
        pack_kernel,
        grid=(1,),
        out_shape=far_f32(BLOCKS, PACK, 128),
        in_specs=[full(MODES, 64), full(MODES, 64), full(1, 64)],
        out_specs=full(BLOCKS, PACK, 128),
        name="pack_parameters",
        **params_of(100_000, 200_000),
    )(far(rate.T), far(residue.T), far(skip[None]))
    packed = exchange(packed, "ctx")
    near_cot = lax.ppermute(out_cotangent, "tp", shift_x(0, 1))
    mixed_near, mixed, cot_pair = pl.pallas_call(
        mix_kernel,
        out_shape=(f32(ROWS * SUB, 128), far_f32(ROWS * SUB, 128), far_bf16(2, ROWS, 512)),
        in_specs=[pl.BlockSpec(memory_space=pl.ANY)] * 4,
        out_specs=(whole(), pl.BlockSpec(memory_space=pl.ANY), pl.BlockSpec(memory_space=pl.ANY)),
        scratch_shapes=[
            pltpu.VMEM((ROWS, 1024), BF16),
            pltpu.VMEM((ROWS, 1024), BF16),
            pltpu.VMEM((ROWS, 512), BF16),
            pltpu.SemaphoreType.DMA((6,)),
        ],
        name="mix_inputs",
        **params_of(100_000_000, 3_000_000),
    )(far(key_part), far(value_part), far(out_cotangent), near_cot)
    cot_parts = [cot_pair] + [lax.ppermute(cot_pair, "tp", shift_x(k)) for k in (1, 2, 3)]

    sent, table = pl.pallas_call(
        states_kernel,
        grid=(1,),
        out_shape=(far_bf16(BLOCKS, STATE, 128), far_f32(TABLE, 128)),
        in_specs=[whole()] * 2,
        out_specs=(full(BLOCKS, STATE, 128), full(TABLE, 128)),
        name="forward_states",
        **params_of(3_000_000_000, 4_000_000),
    )(mixed_near, packed)
    sent = exchange(sent, "ctx")

    anywhere = pl.BlockSpec(memory_space=pl.ANY)
    conv_out, gated, carry, gated_near, weight_near = pl.pallas_call(
        forward_kernel,
        out_shape=(
            far_bf16(ROWS, 1024),
            far_bf16(ROWS, 1024),
            far_f32(MODES, SUB, 128),
            bf16(ROWS, 1024),
            bf16(8, 1024, 512),
        ),
        in_specs=[smem, whole(), anywhere, anywhere, anywhere, anywhere],
        out_specs=(anywhere, anywhere, anywhere, whole(), whole()),
        scratch_shapes=[
            pltpu.VMEM((ROWS * SUB, 128), F32),
            pltpu.VMEM((ROWS * SUB, 128), F32),
            pltpu.VMEM((ROWS, 1024), BF16),
            pltpu.VMEM((TABLE, 128), F32),
            pltpu.VMEM((ROWS, 1024), BF16),
            pltpu.VMEM((MODES, SUB, 128), F32),
            pltpu.SemaphoreType.DMA((14,)),
        ],
        name="forward_conv",
        **params_of(5_000_000_000, 4_000_000),
    )(own_array, sent, far(mixed), far(query), far(table), far(w_out))

    other_gated = lax.ppermute(gated, "ctx", core_swap)
    partial_out = pl.pallas_call(
        output_kernel,
        out_shape=far_bf16(8, ROWS, 512),
        in_specs=[whole(), whole()],
        out_specs=anywhere,
        scratch_shapes=[pltpu.VMEM((8, ROWS, 512), BF16), pltpu.SemaphoreType.DMA((8,))],
        name="output_projection",
        **params_of(2_147_483_648, 11_000_000),
    )(gated_near, weight_near)
    other_parts = [lax.ppermute(part, "ctx", core_swap) for part in cot_parts]

    *by_y, same_z, other_z = pl.pallas_call(
        weight_kernel,
        out_shape=(far_bf16(2, HALF, 256),) * 4 + (far_bf16(4, HALF, 256),) * 2,
        in_specs=[smem, anywhere, whole()] + [anywhere] * 9,
        out_specs=(anywhere,) * 6,
        scratch_shapes=[
            pltpu.VMEM((ROWS, 1024), BF16),
            pltpu.VMEM((1024, 2 * ROWS), BF16),
            pltpu.VMEM((8, 2 * ROWS, 256), BF16),
            pltpu.VMEM((8, 1024, 256), BF16),
            pltpu.SemaphoreType.DMA((17,)),
            pltpu.SemaphoreType.DMA((16,)),
        ],
        name="projection_gradient",
        **params_of(2_147_483_648, 8_000_000),
    )(jnp.concatenate([index, core_array]), far(gated), other_gated, *[far(part) for part in cot_parts], *other_parts, far(partial_out))
    came_z = lax.ppermute(other_z, "ctx", far_swap)
    came_y = [lax.ppermute(by_y[k], "ctx", shift_y(k)) for k in (1, 2, 3)]

    lines = [[2 * x + z for x in range(4)] for z in range(2)]
    arrived = exchange(partial_out.reshape(4, 2, ROWS, 512), "tp", lines).reshape(8, ROWS, 512)

    d_query, d_conv, payload = pl.pallas_call(
        cotangent_kernel,
        out_shape=(far_bf16(ROWS, 1024), far_f32(ROWS * SUB, 128), far_bf16(BLOCKS, STATE + TERMS, 128)),
        in_specs=[smem] + [anywhere] * 11,
        out_specs=(anywhere,) * 3,
        scratch_shapes=[
            pltpu.VMEM((ROWS, 1024), F32),
            pltpu.VMEM((BLOCKS * TERMS, 128), F32),
            pltpu.VMEM((4, ROWS, 1024), BF16),
            pltpu.VMEM((4, 1024, 1024), BF16),
            pltpu.VMEM((ROWS, 1024), BF16),
            pltpu.VMEM((ROWS, 1024), BF16),
            pltpu.VMEM((ROWS * SUB, 128), F32),
            pltpu.VMEM((MODES, SUB, 128), F32),
            pltpu.VMEM((TABLE, 128), F32),
            pltpu.VMEM((ROWS, 1024), BF16),
            pltpu.VMEM((ROWS * SUB, 128), F32),
            pltpu.VMEM((BLOCKS, STATE + TERMS, 128), BF16),
            pltpu.VMEM((MODES, SUB, 128), F32),
            pltpu.SemaphoreType.DMA((24,)),
        ],
        name="cotangent_states",
        **params_of(14_000_000_000, 13_000_000),
    )(came, *[far(part) for part in cot_parts], far(w_out), far(query), far(conv_out), far(mixed), far(carry), far(table), far(other_z))
    received = exchange(payload, "ctx")

    near_sum, own_blocks = pl.pallas_call(
        add_placed_kernel,
        out_shape=(bf16(ROWS, 512), bf16(4, HALF, 256)),
        in_specs=[smem] + [anywhere] * 4,
        out_specs=(whole(), whole()),
        scratch_shapes=[pltpu.VMEM((4, ROWS, 512), BF16), pltpu.SemaphoreType.DMA((8,))],
        name="sum_output",
        **params_of(1_000_000, 2_000_000),
    )(
        (1 - place_z).reshape(1).astype(jnp.int32),
        far(arrived),
        far(by_y[0]),
        far(same_z),
        far(payload),
    )
    near_out = lax.ppermute(near_sum, "tp", shift_x(0, 1))

    first_far, *second_far = pl.pallas_call(
        stage_kernel,
        out_shape=(bf16(HALF, 256),) * 4,
        in_specs=[whole()] * 5,
        out_specs=(whole(),) * 4,
        name="sum_stage",
        **params_of(LONG, 2_000_000),
    )(own_blocks, *came_y, came_z)
    first_far = lax.ppermute(first_far, "ctx", far_swap)
    second_far = [lax.ppermute(second_far[k - 1], "ctx", shift_y(k)) for k in (1, 2, 3)]

    d_key, d_value, gradient, out_sum, d_residue, d_rate, d_skip = pl.pallas_call(
        backward_kernel,
        grid=(1,),
        out_shape=(
            far_bf16(ROWS, 1024),
            far_bf16(ROWS, 1024),
            f32(2 * HALF, 256),
            f32(ROWS, 512),
            f32(MODES, 64),
            f32(MODES, 64),
            f32(1, 64),
        ),
        in_specs=[smem, whole()] + [anywhere] * 7 + [whole()] * 4 + [full(MODES, 64)] * 2,
        out_specs=(anywhere, anywhere, whole(), whole(), full(MODES, 64), full(MODES, 64), full(1, 64)),
        scratch_shapes=[
            pltpu.VMEM((ROWS * SUB, 128), F32),
            pltpu.VMEM((ROWS, 1024), BF16),
            pltpu.VMEM((ROWS, 1024), BF16),
            pltpu.VMEM((TABLE, 128), F32),
            pltpu.VMEM((ROWS, 1024), BF16),
            pltpu.VMEM((ROWS, 1024), BF16),
            pltpu.VMEM((MODES, SUB, 128), F32),
            pltpu.VMEM((ROWS * SUB, 128), F32),
            pltpu.VMEM((2, HALF, 256), BF16),
            pltpu.VMEM((4, ROWS, 512), BF16),
            pltpu.VMEM((BLOCKS * STATE, 128), F32),
            pltpu.SemaphoreType.DMA((12,)),
        ],
        name="backward_conv",
        **params_of(5_000_000_000, 4_000_000),
    )(
        jnp.stack([own, place_z, own // 2, core]).astype(jnp.int32),
        received,
        far(d_conv),
        far(key_part),
        far(value_part),
        far(table),
        far(by_y[0]),
        far(same_z),
        far(arrived),
        *came_y,
        came_z,
        far(rate.T),
        far(residue.T),
    )

    d_weight, output = pl.pallas_call(
        last_kernel,
        out_shape=(far_f32(2 * HALF, 256), far_bf16(ROWS, 512)),
        in_specs=[whole(), whole()] + [anywhere] * 5,
        out_specs=(anywhere,) * 2,
        scratch_shapes=[
            pltpu.VMEM((4, HALF, 256), BF16),
            pltpu.VMEM((ROWS, 512), BF16),
            pltpu.VMEM((2 * HALF, 256), F32),
            pltpu.VMEM((ROWS, 512), BF16),
            pltpu.SemaphoreType.DMA((8,)),
        ],
        name="last_sums",
        **params_of(2_000_000, 4_000_000),
    )(gradient, out_sum, first_far, *second_far, near_out)

    return (output, d_query, d_key, d_value, d_weight, d_residue.T, d_rate.T, d_skip[0])


def solution(mesh):
    rows, owner = P("ctx", "tp"), P(("tp", "ctx"))
    return jax.shard_map(
        local,
        mesh=mesh,
        in_specs=(rows, rows, rows, rows, P("tp", None), P(("tp", "ctx"), None), P(("tp", "ctx"), None), owner),
        out_specs=(rows, rows, rows, rows, P("tp", "ctx"), P(("tp", "ctx"), None), P(("tp", "ctx"), None), owner),
        check_vma=False,
    )
```

```python
import functools

import jax
import jax.numpy as jnp
from jax import lax
from jax.experimental import pallas as pl
from jax.experimental.pallas import tpu as pltpu
from jax.sharding import PartitionSpec as P

F32 = jnp.float32
BF16 = jnp.bfloat16
SEQ = 4096
MODES = 16
ROWS = 256
SUB = 8
BLOCKS = 16
HALF = 512
UNROLL = 16
PACK = 24
TABLE = 2 * PACK * SUB
STATE = MODES * SUB
TERMS = 32
VMEM = 32 * 1024 * 1024
LONG = 2_000_000_000_000
SHORT = 50


def params_of(flops, nbytes):
    return dict(
        compiler_params=pltpu.CompilerParams(vmem_limit_bytes=VMEM),
        cost_estimate=pl.CostEstimate(flops=flops // SHORT, bytes_accessed=nbytes // SHORT, transcendentals=0),
    )


def whole():
    return pl.BlockSpec(memory_space=pltpu.VMEM)


def full(*shape):
    return pl.BlockSpec(shape, lambda *_: (0,) * len(shape))


def far(array):
    return pltpu.with_memory_space_constraint(array, pltpu.HBM)


def far_f32(*shape):
    return pltpu.HBM(shape, F32)


def far_bf16(*shape):
    return pltpu.HBM(shape, BF16)


def lanes(group):
    return slice(128 * group, 128 * (group + 1))


def group_rows(group):
    return pl.ds(group, ROWS, stride=SUB)


def rate_of(table, mode):
    return table[SUB * mode : SUB * (mode + 1), :]


def step_decay(table, mode):
    return jnp.exp(rate_of(table, mode) * (-1.0 / SEQ))


def block_decay(table, mode):
    return jnp.exp(rate_of(table, mode) * (-float(ROWS) / SEQ))


def mode_weight(table, mode):
    return rate_of(table, PACK + mode) * jnp.sqrt(rate_of(table, mode) * (2.0 / SEQ))


def skip_of(table):
    return rate_of(table, MODES)


def at(ref, step):
    return ref[pl.ds(pl.multiple_of(step * SUB, SUB), SUB), :]


def zeros(count):
    return tuple(jnp.zeros((SUB, 128), F32) for _ in range(count))


def tree_sum(parts):
    parts = list(parts)
    while len(parts) > 1:
        parts = [sum(parts[i : i + 2]) for i in range(0, len(parts), 2)]
    return parts[0]


def pack_kernel(rate_ref, residue_ref, skip_ref, out_ref):
    both = jnp.concatenate([rate_ref[...], residue_ref[...]], axis=1)
    last = jnp.concatenate([skip_ref[...], skip_ref[...]], axis=1)
    for j in range(BLOCKS):
        out_ref[j, :MODES] = both
        out_ref[j, MODES:] = jnp.broadcast_to(last, (PACK - MODES, 128))


def mix_kernel(
    key_in, value_in, cot_in, near_cot_in, mixed_ref, mixed_out, pair_out, key_ref, value_ref, cot_ref, sems
):
    copies = [
        pltpu.make_async_copy(key_in, key_ref, sems.at[0]),
        pltpu.make_async_copy(value_in, value_ref, sems.at[1]),
        pltpu.make_async_copy(near_cot_in, pair_out.at[1], sems.at[2]),
        pltpu.make_async_copy(cot_in, cot_ref, sems.at[3]),
    ]
    results = [
        pltpu.make_async_copy(mixed_ref, mixed_out, sems.at[4]),
        pltpu.make_async_copy(cot_ref, pair_out.at[0], sems.at[5]),
    ]
    for copy in copies:
        copy.start()
    copies[0].wait()
    copies[1].wait()
    for group in range(SUB):
        product = key_ref[:, lanes(group)].astype(F32) * value_ref[:, lanes(group)].astype(F32)
        mixed_ref[group_rows(group), :] = product.astype(BF16).astype(F32)
    results[0].start()
    copies[3].wait()
    results[1].start()
    for copy in copies[2:3] + results:
        copy.wait()


def states_kernel(mixed_ref, packed_ref, sent_ref, table):
    left = lax.broadcasted_iota(jnp.int32, (PACK, 128), 1) < 64
    for group in range(SUB):
        one, two = packed_ref[2 * group], packed_ref[2 * group + 1]
        table[pl.ds(group, PACK, stride=SUB), :] = jnp.where(left, one, pltpu.roll(two, 64, 1))
        table[pl.ds(PACK * SUB + group, PACK, stride=SUB), :] = jnp.where(left, pltpu.roll(one, 64, 1), two)
    decay = [step_decay(table, m) for m in range(MODES)]

    def body(i, held):
        for u in range(UNROLL):
            value = at(mixed_ref, i * UNROLL + u)
            held = tuple(decay[m] * held[m] + value for m in range(MODES))
        return held

    held = lax.fori_loop(0, ROWS // UNROLL, body, zeros(MODES))
    for m in range(0, MODES, 2):
        state = jnp.concatenate([held[m], held[m + 1]]).astype(BF16)
        for j in range(BLOCKS):
            sent_ref[j, SUB * m : SUB * (m + 2), :] = state


def forward_kernel(
    own_ref, sent_ref, mixed_in, query_in, table_in, weight_in,
    conv_out, gated_out, carry_out, gated_ref, weight_ref,
    buffer, mixed_ref, query_ref, table, conv_ref, carry_ref, sems,
):
    own = own_ref[0]
    copies = [
        pltpu.make_async_copy(source, target, sems.at[i])
        for i, (source, target) in enumerate([(table_in, table), (mixed_in, mixed_ref), (query_in, query_ref)])
    ]
    weights = [
        pltpu.make_async_copy(weight_in.at[:, 512 * i : 512 * (i + 1)], weight_ref.at[i], sems.at[6 + i])
        for i in range(8)
    ]
    results = [
        pltpu.make_async_copy(source, target, sems.at[3 + i])
        for i, (source, target) in enumerate([(carry_ref, carry_out), (conv_ref, conv_out), (gated_ref, gated_out)])
    ]
    for copy in copies + weights:
        copy.start()
    copies[0].wait()
    for m in range(0, MODES, 2):
        decays = jnp.concatenate([block_decay(table, m), block_decay(table, m + 1)])
        carry = jnp.zeros((2 * SUB, 128), F32)
        for j in range(BLOCKS - 1):
            state = sent_ref[j, SUB * m : SUB * (m + 2), :].astype(F32)
            carry = jnp.where(j < own, decays * carry + state, carry)
        carry_ref[m] = carry[:SUB]
        carry_ref[m + 1] = carry[SUB:]
    results[0].start()
    copies[1].wait()
    decay = [step_decay(table, m) for m in range(MODES)]
    weight = [mode_weight(table, m) for m in range(MODES)]
    skip = skip_of(table)

    def body(i, held):
        for u in range(UNROLL):
            step = i * UNROLL + u
            value = at(mixed_ref, step)
            held = tuple(decay[m] * held[m] + value for m in range(MODES))
            total = tree_sum([weight[m] * held[m] for m in range(MODES)])
            buffer[pl.ds(pl.multiple_of(step * SUB, SUB), SUB), :] = total + skip * value
        return held

    lax.fori_loop(0, ROWS // UNROLL, body, tuple(carry_ref[m] for m in range(MODES)))
    copies[2].wait()
    for group in range(SUB):
        conv = buffer[group_rows(group), :].astype(BF16)
        conv_ref[:, lanes(group)] = conv
        gated_ref[:, lanes(group)] = (query_ref[:, lanes(group)].astype(F32) * conv.astype(F32)).astype(BF16)
    results[1].start()
    results[2].start()
    for copy in results + weights:
        copy.wait()


def output_kernel(gated_ref, weight_ref, out_ref, blocks, sems):
    results = [pltpu.make_async_copy(blocks.at[i], out_ref.at[i], sems.at[i]) for i in range(8)]
    for i in range(8):
        blocks[i] = jnp.dot(gated_ref[...], weight_ref[i], preferred_element_type=F32).astype(BF16)
        results[i].start()
    for result in results:
        result.wait()


def weight_kernel(index_ref, gated_ref, other_ref, *refs):
    cot_refs, other_refs = refs[:4], refs[4:8]
    along_y, along_z = refs[9:13], refs[13:15]
    gated, turned, cots, chunks, sems, out_sems = refs[15:]
    half = pl.ds(pl.multiple_of(index_ref[8] * 256, 256), 256)
    copies = [
        pltpu.make_async_copy(gated_ref, gated, sems.at[8]),
    ]
    for i in range(8):
        own = cot_refs[i // 2].at[i % 2, :, half]
        copies.append(pltpu.make_async_copy(own, cots.at[i, :ROWS], sems.at[i]))
    for copy in copies:
        copy.start()
    for i in range(8):
        cots[i, ROWS:] = other_refs[i // 2][i % 2, :, half]
    turned[:, ROWS:] = other_ref[...].T
    copies[0].wait()
    turned[:, :ROWS] = gated[...].T
    for copy in copies[1:]:
        copy.wait()
    results = []
    for z in (1, 0):
        for k in range(4):
            i = 4 * z + k
            total = jnp.dot(turned[...], cots[index_ref[i]], preferred_element_type=F32)
            chunks[i] = total.astype(BF16)
            results.append(pltpu.make_async_copy(chunks.at[i, HALF:], along_z[z].at[k], out_sems.at[i]))
            results.append(pltpu.make_async_copy(chunks.at[i, :HALF], along_y[k].at[z], out_sems.at[8 + i]))
            results[-2].start()
            results[-1].start()
    for copy in results:
        copy.wait()


def cotangent_kernel(
    came_ref, part0, part1, part2, part3, weight_ref, query_in, conv_in, mixed_in, carry_in, table_in, after_ref,
    dquery_out, dconv_out, sent_out,
    total, terms, parts, weight, query_ref, conv_ref, mixed_ref, carry_ref, table, dquery_ref, dconv_ref, sent_ref, moments, sems,
):
    copies = []
    for i in range(8):
        columns = pl.ds(pl.multiple_of(came_ref[i] * 512, 512), 512)
        part = (part0, part1, part2, part3)[i // 2].at[i % 2]
        place = slice(512 * (i % 2), 512 * (i % 2 + 1))
        copies.append(pltpu.make_async_copy(weight_ref.at[:, columns], weight.at[i // 2, :, place], sems.at[i]))
        copies.append(pltpu.make_async_copy(part, parts.at[i // 2, :, place], sems.at[8 + i]))
    later = [
        pltpu.make_async_copy(source, target, sems.at[16 + i])
        for i, (source, target) in enumerate(
            [(query_in, query_ref), (conv_in, conv_ref), (mixed_in, mixed_ref), (carry_in, carry_ref), (table_in, table)]
        )
    ]
    results = [
        pltpu.make_async_copy(source, target, sems.at[21 + i])
        for i, (source, target) in enumerate(
            [(dquery_ref, dquery_out), (dconv_ref, dconv_out), (sent_ref, sent_out)]
        )
    ]
    for copy in copies + later:
        copy.start()
    for i in range(4):
        for copy in copies[4 * i : 4 * i + 4]:
            copy.wait()
        product = lax.dot_general(parts[i], weight[i], (((1,), (1,)), ((), ())), preferred_element_type=F32)
        if i == 0:
            total[...] = product
        else:
            total[...] += product
    for copy in later:
        copy.wait()
    for group in range(SUB):
        cot = total[:, lanes(group)]
        dquery_ref[:, lanes(group)] = (cot * conv_ref[:, lanes(group)].astype(F32)).astype(BF16)
        dconv_ref[group_rows(group), :] = (cot * query_ref[:, lanes(group)].astype(F32)).astype(BF16).astype(F32)

    results[0].start()
    results[1].start()
    left = lax.broadcasted_iota(jnp.int32, (SUB, 128), 1) < 64

    def put(row, one, two):
        terms[pl.ds(row, SUB, stride=2 * TERMS), :] = jnp.where(left, one, pltpu.roll(two, 64, 1))
        terms[pl.ds(TERMS + row, SUB, stride=2 * TERMS), :] = jnp.where(left, pltpu.roll(one, 64, 1), two)

    all_decay = [step_decay(table, m) for m in range(MODES)]

    def backward(i, back):
        for u in range(UNROLL):
            value = at(dconv_ref, ROWS - 1 - (i * UNROLL + u))
            back = tuple(all_decay[m] * back[m] + value for m in range(MODES))
        return back

    back = lax.fori_loop(0, ROWS // UNROLL, backward, zeros(MODES))
    for m in range(0, MODES, 2):
        state = jnp.concatenate([back[m], back[m + 1]]).astype(BF16)
        for j in range(BLOCKS):
            sent_ref[j, SUB * m : SUB * (m + 2), :] = state
    half = MODES // 2
    for first in (0, half):
        modes = range(first, first + half)
        decay = [step_decay(table, m) for m in modes]

        def forward(i, packed):
            held, moment, first_sum, second_sum, skip_sum = packed
            for u in range(UNROLL):
                value = at(mixed_ref, i * UNROLL + u)
                cot = at(dconv_ref, i * UNROLL + u)
                past = [decay[m] * held[m] for m in range(half)]
                moment = tuple(decay[m] * moment[m] + past[m] for m in range(half))
                held = tuple(past[m] + value for m in range(half))
                first_sum = tuple(first_sum[m] + cot * held[m] for m in range(half))
                second_sum = tuple(second_sum[m] + cot * moment[m] for m in range(half))
                skip_sum = skip_sum + cot * value
            return (held, moment, first_sum, second_sum, skip_sum)

        start = (tuple(carry_ref[m] for m in modes), zeros(half), zeros(half), zeros(half), zeros(1)[0])
        held, moment, first_sum, second_sum, skip_sum = lax.fori_loop(0, ROWS // UNROLL, forward, start)

        for m in range(half):
            put(first + m, first_sum[m], second_sum[m])
            moments[first + m] = moment[m]
    for m in range(half):
        put(MODES + m, moments[m], moments[half + m])
    for row in range(MODES + half, TERMS):
        put(row, skip_sum, skip_sum)
    for j in range(BLOCKS):
        term = terms[TERMS * j : TERMS * (j + 1), :]
        sent_ref[j, STATE:, :] = term.astype(BF16)
    results[2].start()
    for result in results:
        result.wait()


def owner_sums(parts_ref, place_ref, rate_ref, residue_ref, dresidue_ref, drate_ref, dskip_ref, states):
    rate = rate_ref[...]
    residue = residue_ref[...]
    near = jnp.exp(rate * (-1.0 / SEQ))
    far = jnp.exp(rate * (-float(ROWS) / SEQ))
    scale = jnp.sqrt(rate * (2.0 / SEQ))
    half = MODES // 2
    first = jnp.zeros_like(rate)
    second = jnp.zeros_like(rate)
    skip = jnp.zeros((1, rate.shape[1]), F32)
    later = jnp.zeros_like(rate)
    for j in range(BLOCKS):
        states[STATE * j : STATE * (j + 1), :] = parts_ref[j, :STATE, :].astype(F32)
    for j in range(BLOCKS - 1, -1, -1):
        terms = parts_ref[j, STATE:, :].astype(F32)
        sums, ends = terms[0:MODES], terms[MODES : MODES + half]
        ends = jnp.concatenate([ends[:, :64], ends[:, 64:]])
        back = states[pl.ds(STATE * j + place_ref[2], MODES, stride=SUB), :]
        back = jnp.where(place_ref[3] == 0, back, pltpu.roll(back, 64, 1))[:, :64]
        first += sums[:, :64]
        second += sums[:, 64:] + near * later * ends
        later = far * later + back
        skip += terms[MODES + half : MODES + half + 1, :64]
    proj = scale * first
    dresidue_ref[...] = proj
    drate_ref[...] = residue * (0.5 * proj / rate - scale * second * (1.0 / SEQ))
    dskip_ref[...] = skip


def backward_kernel(
    own_ref, sent_ref, dconv_in, key_in, value_in, table_in, first_in, same_in, arrived_in,
    came1, came2, came3, came_z, rate_ref, residue_ref,
    dkey_out, dvalue_out, gradient_ref, output_ref, dresidue_ref, drate_ref, dskip_ref,
    dconv_ref, key_ref, value_ref, table, dkey_ref, dvalue_ref, carry_ref, buffer, blocks, arrived, states, sems,
):
    own = own_ref[0]
    copies = [
        pltpu.make_async_copy(source, target, sems.at[i])
        for i, (source, target) in enumerate(
            [
                (table_in, table),
                (dconv_in, dconv_ref),
                (key_in, key_ref),
                (value_in, value_ref),
                (first_in.at[0], blocks.at[0]),
                (same_in.at[0], blocks.at[1]),
            ]
            + [(arrived_in.at[2 * k + own_ref[1]], arrived.at[k]) for k in range(4)]
        )
    ]
    results = [
        pltpu.make_async_copy(dkey_ref, dkey_out, sems.at[10]),
        pltpu.make_async_copy(dvalue_ref, dvalue_out, sems.at[11]),
    ]
    for copy in copies:
        copy.start()
    copies[0].wait()
    for m in range(0, MODES, 2):
        decays = jnp.concatenate([block_decay(table, m), block_decay(table, m + 1)])
        carry = jnp.zeros((2 * SUB, 128), F32)
        for j in range(BLOCKS - 1, 0, -1):
            state = sent_ref[j, SUB * m : SUB * (m + 2), :].astype(F32)
            carry = jnp.where(j > own, decays * carry + state, carry)
        carry_ref[m] = carry[:SUB]
        carry_ref[m + 1] = carry[SUB:]
    copies[1].wait()
    decay = [step_decay(table, m) for m in range(MODES)]
    weight = [mode_weight(table, m) for m in range(MODES)]
    skip = skip_of(table)

    def body(i, held):
        for u in range(UNROLL):
            step = ROWS - 1 - (i * UNROLL + u)
            value = at(dconv_ref, step)
            held = tuple(decay[m] * held[m] + value for m in range(MODES))
            total = tree_sum([weight[m] * held[m] for m in range(MODES)])
            buffer[pl.ds(pl.multiple_of(step * SUB, SUB), SUB), :] = total + skip * value
        return held

    lax.fori_loop(0, ROWS // UNROLL, body, tuple(carry_ref[m] for m in range(MODES)))
    copies[2].wait()
    copies[3].wait()
    for group in range(SUB):
        grad = buffer[group_rows(group), :].astype(BF16).astype(F32)
        dkey_ref[:, lanes(group)] = (grad * value_ref[:, lanes(group)].astype(F32)).astype(BF16)
        dvalue_ref[:, lanes(group)] = (grad * key_ref[:, lanes(group)].astype(F32)).astype(BF16)
    for result in results:
        result.start()
    for copy in copies[4:]:
        copy.wait()
    gradient_ref[:HALF] = blocks[0].astype(F32) + sum(part[0].astype(F32) for part in (came1, came2, came3))
    gradient_ref[HALF:] = blocks[1].astype(F32) + came_z[0].astype(F32)
    output_ref[...] = sum(arrived[k].astype(F32) for k in range(4))
    owner_sums(sent_ref, own_ref, rate_ref, residue_ref, dresidue_ref, drate_ref, dskip_ref, states)
    for result in results:
        result.wait()


def add_kernel(*refs):
    out_ref = refs[-1]
    total = refs[0][...].astype(F32).reshape(out_ref.shape)
    for ref in refs[1:-2]:
        total += ref[...].astype(F32).reshape(out_ref.shape)
    out_ref[...] = total.astype(out_ref.dtype)


def stage_kernel(own_ref, *refs):
    came_y, came_z, outs = refs[:3], refs[3], refs[4:8]
    outs[0][...] = (own_ref[0].astype(F32) + sum(part[1].astype(F32) for part in came_y)).astype(BF16)
    for k in (1, 2, 3):
        outs[k][...] = (own_ref[k].astype(F32) + came_z[k].astype(F32)).astype(BF16)


def add_placed_kernel(place_ref, arrived_ref, first_ref, same_ref, after_ref, out_ref, own_ref, held, sems):
    copies = [pltpu.make_async_copy(arrived_ref.at[2 * k + place_ref[0]], held.at[k], sems.at[k]) for k in range(4)]
    copies.append(pltpu.make_async_copy(first_ref.at[1], own_ref.at[0], sems.at[4]))
    copies += [pltpu.make_async_copy(same_ref.at[k], own_ref.at[k], sems.at[4 + k]) for k in (1, 2, 3)]
    for copy in copies:
        copy.start()
    for copy in copies[:4]:
        copy.wait()
    out_ref[...] = sum(held[k].astype(F32) for k in range(4)).astype(BF16)
    for copy in copies[4:]:
        copy.wait()


def last_kernel(gradient_ref, out_sum_ref, *refs):
    parts, last_in, weight_out, output_out = refs[:4], refs[4], refs[5], refs[6]
    held, last, weight_ref, output_ref, sems = refs[7:]
    copies = [pltpu.make_async_copy(parts[i], held.at[i], sems.at[i]) for i in range(4)]
    copies.append(pltpu.make_async_copy(last_in, last, sems.at[4]))
    results = [
        pltpu.make_async_copy(weight_ref.at[:HALF], weight_out.at[:HALF], sems.at[5]),
        pltpu.make_async_copy(weight_ref.at[HALF:], weight_out.at[HALF:], sems.at[6]),
        pltpu.make_async_copy(output_ref, output_out, sems.at[7]),
    ]
    for copy in copies:
        copy.start()
    copies[0].wait()
    weight_ref[:HALF] = gradient_ref[:HALF] + held[0].astype(F32)
    results[0].start()
    for copy in copies[1:4]:
        copy.wait()
    weight_ref[HALF:] = gradient_ref[HALF:] + sum(held[i].astype(F32) for i in (1, 2, 3))
    results[1].start()
    copies[4].wait()
    output_ref[...] = (out_sum_ref[...] + last[...].astype(F32)).astype(BF16)
    results[2].start()
    for copy in results:
        copy.wait()


def f32(*shape):
    return jax.ShapeDtypeStruct(shape, F32)


def bf16(*shape):
    return jax.ShapeDtypeStruct(shape, BF16)


def exchange(array, axis, groups=None):
    return lax.all_to_all(array, axis, split_axis=0, concat_axis=0, tiled=True, axis_index_groups=groups)


def to_all(array, axis, count):
    return exchange(jnp.broadcast_to(array[None], (count,) + array.shape), axis)


MOVES = [(k, z) for k in range(4) for z in range(2)]


def shift_x(k, z=0):
    return [(2 * x + p, 2 * ((x + k) % 4) + (p + z) % 2) for x in range(4) for p in range(2)]


def shift_y(k):
    return [(8 * z + 2 * y + c, 8 * z + 2 * ((y + k) % 4) + c) for z in range(2) for y in range(4) for c in range(2)]


def local(query, key_part, value_part, out_cotangent, w_out, residue, rate, skip):
    own = lax.axis_index("ctx")
    own_array = own.reshape(1).astype(jnp.int32)
    core, own_y, own_z = own % 2, own // 2 % 4, own // 8
    place = lax.axis_index("tp")
    place_x, place_z = place // 2, place % 2
    smem = pl.BlockSpec(memory_space=pltpu.SMEM)
    core_swap = [(i, i ^ 1) for i in range(BLOCKS)]
    far_swap = [(i, i ^ 8) for i in range(BLOCKS)]
    hbm = pl.BlockSpec(memory_space=pltpu.HBM)

    steps = jnp.arange(8, dtype=jnp.int32)
    came = ((place_x - steps // 2) % 4) * 2 + (place_z + steps) % 2
    chip = ((own_z + steps // 4) % 2) * 4 + (own_y + steps) % 4
    index = 2 * ((place_x - chip // 2) % 4) + (chip - place_z) % 2
    core_array = core.reshape(1).astype(jnp.int32)

    packed = pl.pallas_call(
        pack_kernel,
        grid=(1,),
        out_shape=far_f32(BLOCKS, PACK, 128),
        in_specs=[full(MODES, 64), full(MODES, 64), full(1, 64)],
        out_specs=full(BLOCKS, PACK, 128),
        name="pack_parameters",
        **params_of(100_000, 200_000),
    )(far(rate.T), far(residue.T), far(skip[None]))
    packed = exchange(packed, "ctx")
    near_cot = lax.ppermute(out_cotangent, "tp", shift_x(0, 1))
    mixed_near, mixed, cot_pair = pl.pallas_call(
        mix_kernel,
        out_shape=(f32(ROWS * SUB, 128), far_f32(ROWS * SUB, 128), far_bf16(2, ROWS, 512)),
        in_specs=[pl.BlockSpec(memory_space=pl.ANY)] * 4,
        out_specs=(whole(), pl.BlockSpec(memory_space=pl.ANY), pl.BlockSpec(memory_space=pl.ANY)),
        scratch_shapes=[
            pltpu.VMEM((ROWS, 1024), BF16),
            pltpu.VMEM((ROWS, 1024), BF16),
            pltpu.VMEM((ROWS, 512), BF16),
            pltpu.SemaphoreType.DMA((6,)),
        ],
        name="mix_inputs",
        **params_of(100_000_000, 3_000_000),
    )(far(key_part), far(value_part), far(out_cotangent), near_cot)
    cot_parts = [cot_pair] + [lax.ppermute(cot_pair, "tp", shift_x(k)) for k in (1, 2, 3)]

    sent, table = pl.pallas_call(
        states_kernel,
        grid=(1,),
        out_shape=(far_bf16(BLOCKS, STATE, 128), far_f32(TABLE, 128)),
        in_specs=[whole()] * 2,
        out_specs=(full(BLOCKS, STATE, 128), full(TABLE, 128)),
        name="forward_states",
        **params_of(3_000_000_000, 4_000_000),
    )(mixed_near, packed)
    sent = exchange(sent, "ctx")

    anywhere = pl.BlockSpec(memory_space=pl.ANY)
    conv_out, gated, carry, gated_near, weight_near = pl.pallas_call(
        forward_kernel,
        out_shape=(
            far_bf16(ROWS, 1024),
            far_bf16(ROWS, 1024),
            far_f32(MODES, SUB, 128),
            bf16(ROWS, 1024),
            bf16(8, 1024, 512),
        ),
        in_specs=[smem, whole(), anywhere, anywhere, anywhere, anywhere],
        out_specs=(anywhere, anywhere, anywhere, whole(), whole()),
        scratch_shapes=[
            pltpu.VMEM((ROWS * SUB, 128), F32),
            pltpu.VMEM((ROWS * SUB, 128), F32),
            pltpu.VMEM((ROWS, 1024), BF16),
            pltpu.VMEM((TABLE, 128), F32),
            pltpu.VMEM((ROWS, 1024), BF16),
            pltpu.VMEM((MODES, SUB, 128), F32),
            pltpu.SemaphoreType.DMA((14,)),
        ],
        name="forward_conv",
        **params_of(5_000_000_000, 4_000_000),
    )(own_array, sent, far(mixed), far(query), far(table), far(w_out))

    other_gated = lax.ppermute(gated, "ctx", core_swap)
    partial_out = pl.pallas_call(
        output_kernel,
        out_shape=far_bf16(8, ROWS, 512),
        in_specs=[whole(), whole()],
        out_specs=anywhere,
        scratch_shapes=[pltpu.VMEM((8, ROWS, 512), BF16), pltpu.SemaphoreType.DMA((8,))],
        name="output_projection",
        **params_of(2_147_483_648, 11_000_000),
    )(gated_near, weight_near)
    other_parts = [lax.ppermute(part, "ctx", core_swap) for part in cot_parts]

    *by_y, same_z, other_z = pl.pallas_call(
        weight_kernel,
        out_shape=(far_bf16(2, HALF, 256),) * 4 + (far_bf16(4, HALF, 256),) * 2,
        in_specs=[smem, anywhere, whole()] + [anywhere] * 4 + [whole()] * 4 + [anywhere],
        out_specs=(anywhere,) * 6,
        scratch_shapes=[
            pltpu.VMEM((ROWS, 1024), BF16),
            pltpu.VMEM((1024, 2 * ROWS), BF16),
            pltpu.VMEM((8, 2 * ROWS, 256), BF16),
            pltpu.VMEM((8, 1024, 256), BF16),
            pltpu.SemaphoreType.DMA((9,)),
            pltpu.SemaphoreType.DMA((16,)),
        ],
        name="projection_gradient",
        **params_of(2_147_483_648, 8_000_000),
    )(jnp.concatenate([index, core_array]), far(gated), other_gated, *[far(part) for part in cot_parts], *other_parts, far(partial_out))
    came_z = lax.ppermute(other_z, "ctx", far_swap)
    came_y = [lax.ppermute(by_y[k], "ctx", shift_y(k)) for k in (1, 2, 3)]

    lines = [[2 * x + z for x in range(4)] for z in range(2)]
    arrived = exchange(partial_out.reshape(4, 2, ROWS, 512), "tp", lines).reshape(8, ROWS, 512)

    d_query, d_conv, payload = pl.pallas_call(
        cotangent_kernel,
        out_shape=(far_bf16(ROWS, 1024), far_f32(ROWS * SUB, 128), far_bf16(BLOCKS, STATE + TERMS, 128)),
        in_specs=[smem] + [anywhere] * 11,
        out_specs=(anywhere,) * 3,
        scratch_shapes=[
            pltpu.VMEM((ROWS, 1024), F32),
            pltpu.VMEM((BLOCKS * TERMS, 128), F32),
            pltpu.VMEM((4, ROWS, 1024), BF16),
            pltpu.VMEM((4, 1024, 1024), BF16),
            pltpu.VMEM((ROWS, 1024), BF16),
            pltpu.VMEM((ROWS, 1024), BF16),
            pltpu.VMEM((ROWS * SUB, 128), F32),
            pltpu.VMEM((MODES, SUB, 128), F32),
            pltpu.VMEM((TABLE, 128), F32),
            pltpu.VMEM((ROWS, 1024), BF16),
            pltpu.VMEM((ROWS * SUB, 128), F32),
            pltpu.VMEM((BLOCKS, STATE + TERMS, 128), BF16),
            pltpu.VMEM((MODES, SUB, 128), F32),
            pltpu.SemaphoreType.DMA((24,)),
        ],
        name="cotangent_states",
        **params_of(14_000_000_000, 13_000_000),
    )(came, *[far(part) for part in cot_parts], far(w_out), far(query), far(conv_out), far(mixed), far(carry), far(table), far(other_z))
    received = exchange(payload, "ctx")

    near_sum, own_blocks = pl.pallas_call(
        add_placed_kernel,
        out_shape=(bf16(ROWS, 512), bf16(4, HALF, 256)),
        in_specs=[smem] + [anywhere] * 4,
        out_specs=(whole(), whole()),
        scratch_shapes=[pltpu.VMEM((4, ROWS, 512), BF16), pltpu.SemaphoreType.DMA((8,))],
        name="sum_output",
        **params_of(1_000_000, 2_000_000),
    )(
        (1 - place_z).reshape(1).astype(jnp.int32),
        far(arrived),
        far(by_y[0]),
        far(same_z),
        far(payload),
    )
    near_out = lax.ppermute(near_sum, "tp", shift_x(0, 1))

    first_far, *second_far = pl.pallas_call(
        stage_kernel,
        out_shape=(bf16(HALF, 256),) * 4,
        in_specs=[whole()] * 5,
        out_specs=(whole(),) * 4,
        name="sum_stage",
        **params_of(LONG, 2_000_000),
    )(own_blocks, *came_y, came_z)
    first_far = lax.ppermute(first_far, "ctx", far_swap)
    second_far = [lax.ppermute(second_far[k - 1], "ctx", shift_y(k)) for k in (1, 2, 3)]

    d_key, d_value, gradient, out_sum, d_residue, d_rate, d_skip = pl.pallas_call(
        backward_kernel,
        grid=(1,),
        out_shape=(
            far_bf16(ROWS, 1024),
            far_bf16(ROWS, 1024),
            f32(2 * HALF, 256),
            f32(ROWS, 512),
            f32(MODES, 64),
            f32(MODES, 64),
            f32(1, 64),
        ),
        in_specs=[smem, whole()] + [anywhere] * 7 + [whole()] * 4 + [full(MODES, 64)] * 2,
        out_specs=(anywhere, anywhere, whole(), whole(), full(MODES, 64), full(MODES, 64), full(1, 64)),
        scratch_shapes=[
            pltpu.VMEM((ROWS * SUB, 128), F32),
            pltpu.VMEM((ROWS, 1024), BF16),
            pltpu.VMEM((ROWS, 1024), BF16),
            pltpu.VMEM((TABLE, 128), F32),
            pltpu.VMEM((ROWS, 1024), BF16),
            pltpu.VMEM((ROWS, 1024), BF16),
            pltpu.VMEM((MODES, SUB, 128), F32),
            pltpu.VMEM((ROWS * SUB, 128), F32),
            pltpu.VMEM((2, HALF, 256), BF16),
            pltpu.VMEM((4, ROWS, 512), BF16),
            pltpu.VMEM((BLOCKS * STATE, 128), F32),
            pltpu.SemaphoreType.DMA((12,)),
        ],
        name="backward_conv",
        **params_of(5_000_000_000, 4_000_000),
    )(
        jnp.stack([own, place_z, own // 2, core]).astype(jnp.int32),
        received,
        far(d_conv),
        far(key_part),
        far(value_part),
        far(table),
        far(by_y[0]),
        far(same_z),
        far(arrived),
        *came_y,
        came_z,
        far(rate.T),
        far(residue.T),
    )

    d_weight, output = pl.pallas_call(
        last_kernel,
        out_shape=(far_f32(2 * HALF, 256), far_bf16(ROWS, 512)),
        in_specs=[whole(), whole()] + [anywhere] * 5,
        out_specs=(anywhere,) * 2,
        scratch_shapes=[
            pltpu.VMEM((4, HALF, 256), BF16),
            pltpu.VMEM((ROWS, 512), BF16),
            pltpu.VMEM((2 * HALF, 256), F32),
            pltpu.VMEM((ROWS, 512), BF16),
            pltpu.SemaphoreType.DMA((8,)),
        ],
        name="last_sums",
        **params_of(2_000_000, 4_000_000),
    )(gradient, out_sum, first_far, *second_far, near_out)

    return (output, d_query, d_key, d_value, d_weight, d_residue.T, d_rate.T, d_skip[0])


def solution(mesh):
    rows, owner = P("ctx", "tp"), P(("tp", "ctx"))
    return jax.shard_map(
        local,
        mesh=mesh,
        in_specs=(rows, rows, rows, rows, P("tp", None), P(("tp", "ctx"), None), P(("tp", "ctx"), None), owner),
        out_specs=(rows, rows, rows, rows, P("tp", "ctx"), P(("tp", "ctx"), None), P(("tp", "ctx"), None), owner),
        check_vma=False,
    )
```
